32 devices in a mesh: dp: 4 (over x, core), fsdp: 8 (over z, y).
Axes of the slice: x: 2, y: 2, z: 4, core: 2. Of those that a mesh axis runs over, the one named last changes fastest.
Arguments:
- tokens: bfloat16 [32, 1024, 768], P(('dp', 'fsdp')), may hold values from -6 to 6
- lengths: int32 [32, 8], P(('dp', 'fsdp')), may hold values from 1 to 256, 896 in all within a row
- lead_index: int32 [32, 8], P(('dp', 'fsdp')), may hold values from 0 to 19
- cotangent: bfloat16 [32, 1024, 768], P(('dp', 'fsdp')), may hold values from -6 to 6
- qkv_weight: bfloat16 [768, 2304], P('dp', 'fsdp'), may hold values from -0.21875 to 0.21875
- out_weight: bfloat16 [768, 768], P('dp', 'fsdp'), may hold values from -2 to 2
- up_weight: bfloat16 [768, 3072], P('dp', 'fsdp'), may hold values from -0.21875 to 0.21875
- down_weight: bfloat16 [3072, 768], P('dp', 'fsdp'), may hold values from -0.109375 to 0.109375
- vectors: bfloat16 [8, 768], P('dp', 'fsdp'), may hold values from -1.75 to 1.75
- lead_table: bfloat16 [20, 768], P('dp', 'fsdp'), may hold values from -3 to 3
- up_bias: bfloat16 [4, 768], P('dp', 'fsdp'), may hold values from -1.75 to 1.75
Outputs:
- block_output: bfloat16 [32, 1024, 768], P(('dp', 'fsdp'))
- input_grad: float32 [32, 1024, 768], P(('dp', 'fsdp'))
- qkv_grad: float32 [768, 2304], P('dp', 'fsdp')
- out_grad: float32 [768, 768], P('dp', 'fsdp')
- up_grad: float32 [768, 3072], P('dp', 'fsdp')
- down_grad: float32 [3072, 768], P('dp', 'fsdp')
- vectors_grad: float32 [8, 768], P('dp', 'fsdp')
- table_grad: float32 [20, 768], P('dp', 'fsdp')
- up_bias_grad: float32 [4, 768], P('dp', 'fsdp')
The draws below stay inside these ranges and needn't reach their ends.
Inputs may be any that keep to these rules, and one draw needn't show every extreme that they name: `lengths`: the 8 windows of a row hold 896 patches together, the longest exactly 256; the last 128 positions of every row are padding.
All inputs are finite; a program needn't handle non-finite values.
Results may differ from the reference program's by a relative error of at most 0.012.
Values may be sent and summed in bfloat16 or wider, within the bound.
No kernel may reach another device: no remote copies, remote signals or barrier semaphores. Data moves between devices by JAX's collectives and lax.ppermute only.
A program may use at most 256 MiB of HBM per device.

```python
import math
import jax
import jax.numpy as jnp
import numpy as np
from jax import lax

D = 768
HEADS = 12
HD = 64
FF = 3072
LEADS = 20
WIN = 8
L = 1024
SEQS = 32


def touch_ends(drawn, stream_key, low, top_value):
    place = [jax.random.randint(jax.random.fold_in(stream_key, axis), (), 0, length) for axis, length in enumerate(drawn.shape)]
    widest = drawn.shape.index(max(drawn.shape))
    next_to = place[:widest] + [(place[widest] + 1) % drawn.shape[widest]] + place[widest + 1:]
    return drawn.at[tuple(place)].set(low).at[tuple(next_to)].set(top_value)


def levels(rng, dims, split, smallest, high):
    gain = 1.0
    for dim, shards_of in split:
        heights = jax.random.uniform(jax.random.fold_in(jax.random.fold_in(rng, 6), dim), (shards_of,), jnp.float32, smallest / len(split), high / len(split))
        gain = gain * jnp.repeat(jnp.exp(heights), dims[dim] // shards_of).reshape((-1,) + (1,) * (len(dims) - 1 - dim))
    return gain


def split_up(number_of, total, reach, slope):
    weights = [(1 << 20) // math.isqrt(grade ** slope) + 1 for grade in range(2, number_of + 1)]
    spare, counts = total - reach - (number_of - 1), [1] * (number_of - 1)
    while spare > 0:
        candidates = [i for i in range(number_of - 1) if counts[i] < reach]
        whole, budget = sum([weights[i] for i in candidates]), spare
        for i in candidates:
            more = min(reach - counts[i], max(1, budget * weights[i] // whole), spare)
            counts[i] = counts[i] + more
            spare = spare - more
    return np.array([reach] + counts)


def ragged(rng, amount, total, most, skew):
    if amount == 2:
        one = jax.random.randint(rng, (), max(1, total - most), min(most, total - 1) + 1)
        return jnp.stack([one, total - one])
    tallies = jnp.asarray(split_up(amount, total, most, skew), jnp.int32)
    pairs = (amount - 1) // 2
    source_of, sink = tallies[1:1 + 2 * pairs:2], tallies[2:2 + 2 * pairs:2]
    margin = jnp.minimum(source_of - 1, most - sink)
    moved = jax.random.randint(jax.random.fold_in(rng, 1), (pairs,), 0, 1 << 20) % (margin + 1)
    tallies = tallies.at[1:1 + 2 * pairs:2].set(source_of - moved).at[2:2 + 2 * pairs:2].set(sink + moved)
    return tallies[jax.random.permutation(jax.random.fold_in(rng, 2), amount)]


def noise(key, shape, width, reach, cuts=(), kind=jnp.bfloat16):
    drawn = width * jax.random.normal(key, shape, jnp.float32)
    if cuts:
        drawn = drawn * levels(key, shape, cuts, -0.22, 0.18)
    return jnp.clip(drawn, -reach, reach).astype(kind)


def setup_inputs(seed: int = 0) -> dict:
    seeds = jax.random.split(jax.random.key(seed), 12)
    tokens = noise(seeds[0], (SEQS, L, D), 1.0, 6.0, ((0, 32),))
    lengths = jax.vmap(lambda own: ragged(own, WIN, L - L // 8, L // 4, 2))(jax.random.split(seeds[1], SEQS)).reshape((SEQS, WIN)).astype(jnp.int32)
    lead_index = touch_ends(jax.random.randint(seeds[2], (SEQS, WIN), 0, LEADS), jax.random.fold_in(seeds[2], 1), 0, LEADS - 1).astype(jnp.int32)
    cotangent = noise(seeds[3], (SEQS, L, D), 1.0, 6.0, ((0, 32),))
    qkv_weight = noise(seeds[4], (D, 3 * D), D ** -0.5, 0.21875, ((0, 4), (1, 8)))
    out_weight = noise(seeds[5], (D, D), (max(D // 96, 1)) ** -0.5, 2.0, ((0, 4), (1, 8)))
    up_weight = noise(seeds[6], (D, FF), D ** -0.5, 0.21875, ((0, 4), (1, 8)))
    down_weight = noise(seeds[7], (FF, D), FF ** -0.5, 0.109375, ((0, 4), (1, 8)))
    vectors = noise(seeds[8], (8, D), 0.3, 1.75, ((0, 4), (1, 8)))
    lead_table = noise(seeds[9], (LEADS, D), 0.5, 3.0, ((0, 4), (1, 8)))
    up_bias = noise(seeds[10], (4, FF // 4), 0.3, 1.75, ((0, 4), (1, 8)))
    return {"tokens": tokens, "lengths": lengths, "lead_index": lead_index, "cotangent": cotangent, "qkv_weight": qkv_weight, "out_weight": out_weight, "up_weight": up_weight, "down_weight": down_weight, "vectors": vectors, "lead_table": lead_table, "up_bias": up_bias}


@jax.custom_vjp
def low(v):
    return lax.optimization_barrier(v.astype(jnp.bfloat16)).astype(jnp.float32)

@jax.custom_vjp
def low_back(v):
    return v

def low_keep(v):
    return (low(v), None)

def low_pass(kept, grad):
    return (grad,)

def back_keep(v):
    return (v, None)

def back_low(kept, grad):
    return (low(grad),)
low.defvjp(low_keep, low_pass)
low_back.defvjp(back_keep, back_low)
EPSILON = 1e-05
MASKED = -1e+30
HIGHEST = lax.Precision.HIGHEST

def matmul(left_side, right_side):
    return jnp.dot(left_side, right_side, precision=HIGHEST, preferred_element_type=jnp.float32)

def layer_norm(values, gain_off, shift_by):
    center = values - lax.optimization_barrier(jnp.mean(values, axis=-1, keepdims=True))
    spread = lax.optimization_barrier(jnp.mean(center * center, axis=-1, keepdims=True))
    return center * lax.rsqrt(spread + EPSILON) * (1.0 + gain_off) + shift_by

def window_index(lengths):
    bounds = jnp.cumsum(lengths).astype(jnp.int32)
    places = jnp.arange(L, dtype=jnp.int32)
    return lax.optimization_barrier(jnp.sum((places[:, None] >= bounds[None, :]).astype(jnp.int32), axis=1)).astype(jnp.int32)

def lead_onehot(windows, lead_index):
    chosen = windows[:, None] == jnp.arange(WIN, dtype=jnp.int32)[None, :]
    lead_token = lax.optimization_barrier(jnp.sum(jnp.where(chosen, lead_index[None, :], 0), axis=1)).astype(jnp.int32)
    lead_token = jnp.where(windows < WIN, lead_token, -1)
    return (lead_token[:, None] == jnp.arange(LEADS, dtype=jnp.int32)[None, :]).astype(jnp.float32)

def row_forward(values, windows, onehot, params):
    qkv_weight, out_weight, up_weight, down_weight, vectors, lead_table, up_bias = params
    normed = low(layer_norm(values, vectors[0], vectors[1]) + matmul(onehot, lead_table))
    qkv_bias = jnp.concatenate([vectors[4], jnp.zeros((D,), jnp.float32), vectors[5]])
    packed = low(low_back(matmul(normed, qkv_weight) + qkv_bias))
    query_heads = packed[:, :D].reshape(L, HEADS, HD)
    key_heads = packed[:, D:2 * D].reshape(L, HEADS, HD)
    value_heads = packed[:, 2 * D:].reshape(L, HEADS, HD)
    scores = low_back(jnp.einsum('qhd,khd->hqk', query_heads, key_heads, precision=HIGHEST) * HD ** (-0.5))
    visible = windows[:, None] == windows[None, :]
    scores = jnp.where(visible[None], scores, MASKED)
    row_max = lax.optimization_barrier(jnp.max(scores, axis=-1, keepdims=True))
    exponent = jnp.exp(scores - row_max)
    softmaxed = low(exponent / lax.optimization_barrier(jnp.sum(exponent, axis=-1, keepdims=True)))
    mixture = jnp.einsum('hqk,khd->qhd', softmaxed, value_heads, precision=HIGHEST).reshape(L, D)
    attended = low_back(matmul(low(low_back(mixture)), out_weight) + vectors[6])
    middle = values + attended
    normed_two = low(layer_norm(middle, vectors[2], vectors[3]))
    hidden = low_back(matmul(normed_two, up_weight) + up_bias)
    active = low(jax.nn.gelu(hidden, approximate=False))
    return middle + low_back(matmul(active, down_weight) + vectors[7])

def reference(tokens, lengths, lead_index, cotangent, qkv_weight, out_weight, up_weight, down_weight, vectors, lead_table, up_bias):
    params = (qkv_weight.astype(jnp.float32), out_weight.astype(jnp.float32), up_weight.astype(jnp.float32), down_weight.astype(jnp.float32), vectors.astype(jnp.float32), lead_table.astype(jnp.float32), up_bias.astype(jnp.float32).reshape(FF))
    windows = jax.vmap(window_index)(lengths)
    onehots = jax.vmap(lead_onehot)(windows, lead_index)
    inputs = tokens.astype(jnp.float32)
    checked = jax.checkpoint(row_forward)

    def forward(inputs, params):

        def scan_step(running, scanned):
            values, window_row, onehot_row = scanned
            return (running, checked(values, window_row, onehot_row, params))
        _, outputs = lax.scan(scan_step, jnp.zeros((), jnp.float32), (inputs, windows, onehots))
        return outputs
    outputs, pullback = jax.vjp(forward, inputs, params)
    grad_input, gradients = pullback(cotangent.astype(jnp.float32))
    return (outputs.astype(jnp.bfloat16), grad_input, gradients[0], gradients[1], gradients[2], gradients[3], gradients[4], gradients[5], gradients[6].reshape(4, FF // 4))
```

```python
import functools

import jax
import jax.numpy as jnp
from jax import lax
from jax.experimental import pallas as pl
from jax.experimental.pallas import tpu as pltpu
from jax.sharding import PartitionSpec as P

D = 768
HEADS = 12
HD = 64
FF = 3072
LEADS = 20
WIN = 8
L = 1024
EPSILON = 1e-05
MASKED = -1e30
ROWS = 256
TILES = L // ROWS
BLK = 128
PAIRS = HEADS // 2
SCALE = HD ** (-0.5)
VMEM_BYTES = 56 * 1024 * 1024

F32 = jnp.float32
BF16 = jnp.bfloat16


def params(limit=VMEM_BYTES):
    return pltpu.CompilerParams(vmem_limit_bytes=limit)


def dot_nn(a, b):
    return lax.dot_general(a, b, (((1,), (0,)), ((), ())), preferred_element_type=F32)


def dot_nt(a, b):
    return lax.dot_general(a, b, (((1,), (1,)), ((), ())), preferred_element_type=F32)


def whole(shape, space=pltpu.VMEM):
    return pl.BlockSpec(shape, lambda *_: (0,) * len(shape), memory_space=space)


def smem():
    return pl.BlockSpec(memory_space=pltpu.SMEM)


def rows_of(width):
    return pl.BlockSpec((ROWS, width), lambda i: (i, 0))


def norm_parts(values):
    center = values - jnp.mean(values, axis=-1, keepdims=True)
    spread = jnp.mean(center * center, axis=-1, keepdims=True)
    inv = lax.rsqrt(spread + EPSILON)
    return center * inv, inv


def bounds_of(lengths_ref):
    found, total = [], 0
    for w in range(WIN):
        total = total + lengths_ref[0, w]
        found.append(total)
    return found


def lead_of(places, bounds, lead_ref):
    lead = jnp.full(places.shape, -1, jnp.int32)
    for w in reversed(range(WIN)):
        lead = jnp.where(places < bounds[w], lead_ref[0, w], lead)
    return lead


def qkv_kernel(len_ref, lead_ref, x_ref, vec_ref, table_ref, w_ref, n1_ref, qkv_ref):
    step = pl.program_id(0)
    bounds = bounds_of(len_ref)
    hat, _ = norm_parts(x_ref[...].astype(F32))
    normed = hat * (1.0 + vec_ref[0:1, :]) + vec_ref[1:2, :]
    shape = (ROWS, table_ref.shape[0])
    places = step * ROWS + lax.broadcasted_iota(jnp.int32, shape, 0)
    hot = lead_of(places, bounds, lead_ref) == lax.broadcasted_iota(jnp.int32, shape, 1)
    n1 = (normed + dot_nn(hot.astype(BF16), table_ref[...])).astype(BF16)
    n1_ref[...] = n1
    for third in range(3):
        cols = slice(third * D, (third + 1) * D)
        part = dot_nn(n1, w_ref[:, cols])
        if third == 0:
            part = (part + vec_ref[4:5, :]).astype(BF16) * jnp.asarray(SCALE, BF16)
        elif third == 2:
            part = part + vec_ref[5:6, :]
        qkv_ref[:, cols] = part.astype(BF16)


def qkv_call(lengths, leads, x, vec, table, w):
    return pl.pallas_call(
        qkv_kernel,
        grid=(TILES,),
        in_specs=[smem(), smem(), rows_of(D), whole(vec.shape), whole(table.shape), whole(w.shape)],
        out_specs=[rows_of(D), rows_of(3 * D)],
        out_shape=[jax.ShapeDtypeStruct((L, D), BF16), jax.ShapeDtypeStruct((L, 3 * D), BF16)],
        compiler_params=params(),
        cost_estimate=pl.CostEstimate(flops=2 * L * D * 3 * D, bytes_accessed=12_000_000, transcendentals=0),
        name="norm_qkv",
    )(lengths, leads, x, vec, table, w)


def block_range(bounds, block):
    first, last = block * BLK, block * BLK + BLK - 1
    start, end = jnp.int32(0), jnp.int32(L)
    for w in range(WIN):
        start = jnp.where(bounds[w] <= first, bounds[w], start)
    for w in reversed(range(WIN)):
        end = jnp.where(bounds[w] > last, bounds[w], end)
    return start // BLK, (end + BLK - 1) // BLK


def window_at(places, bounds):
    found = jnp.zeros(places.shape, jnp.int32)
    for w in range(WIN):
        found = found + (places >= bounds[w]).astype(jnp.int32)
    return found


def hide(bounds, key_block, query_block):
    shape = (BLK, BLK)
    keys = window_at(key_block * BLK + lax.broadcasted_iota(jnp.int32, (BLK, 1), 0), bounds)
    queries = window_at(query_block * BLK + lax.broadcasted_iota(jnp.int32, (1, BLK), 1), bounds)
    one = jnp.where(jnp.broadcast_to(keys, shape) == jnp.broadcast_to(queries, shape), 0.0, MASKED)
    return jnp.concatenate([one, one], axis=1)


def split_pair(two):
    lanes = lax.broadcasted_iota(jnp.int32, two.shape, 1)
    zero = jnp.zeros_like(two)
    return jnp.concatenate([jnp.where(lanes < HD, two, zero), jnp.where(lanes < HD, zero, two)], axis=0)


def attend_kernel(len_ref, qkv_ref, o_ref, lse_ref, vt, qm, acc, top, tot):
    bounds = bounds_of(len_ref)
    for p in range(PAIRS):
        vt[p * BLK:(p + 1) * BLK, :] = qkv_ref[:, 2 * D + p * BLK:2 * D + (p + 1) * BLK].T
    lse_ref[HEADS:, :] = jnp.zeros((lse_ref.shape[0] - HEADS, L), F32)

    def query_step(block, carry):
        at = pl.multiple_of(block * BLK, BLK)
        first, last = block_range(bounds, block)
        for p in range(PAIRS):
            qm[p] = split_pair(qkv_ref[pl.ds(at, BLK), p * BLK:(p + 1) * BLK])
        acc[...] = jnp.zeros_like(acc)
        top[...] = jnp.full_like(top, MASKED)
        tot[...] = jnp.zeros_like(tot)

        def key_step(key_block, carry):
            key_at = pl.multiple_of(key_block * BLK, BLK)
            hidden = hide(bounds, key_block, block)
            for p in range(PAIRS):
                keys = qkv_ref[pl.ds(key_at, BLK), D + p * BLK:D + (p + 1) * BLK]
                scores = dot_nt(keys, qm[p]) + hidden
                old = top[p, 0:1, :]
                new = jnp.maximum(old, jnp.max(scores, axis=0, keepdims=True))
                expo = jnp.exp(scores - new)
                fade = jnp.exp(old - new)
                top[p, 0:1, :] = new
                tot[p, 0:1, :] = tot[p, 0:1, :] * fade + jnp.sum(expo, axis=0, keepdims=True)
                soft = expo.astype(BF16)
                for side in range(2):
                    rows = slice(side * HD, (side + 1) * HD)
                    cols = slice(side * BLK, (side + 1) * BLK)
                    vals = vt[p * BLK + side * HD:p * BLK + (side + 1) * HD, pl.ds(key_at, BLK)]
                    acc[p, rows, :] = acc[p, rows, :] * fade[:, cols] + dot_nn(vals, soft[:, cols])
            return carry

        lax.fori_loop(first, last, key_step, 0)
        for p in range(PAIRS):
            total = tot[p, 0:1, :]
            inv = 1.0 / total
            log_total = top[p, 0:1, :] + jnp.log(total)
            mixed = jnp.concatenate([acc[p, :HD, :] * inv[:, :BLK], acc[p, HD:, :] * inv[:, BLK:]], axis=0)
            o_ref[pl.ds(at, BLK), p * BLK:(p + 1) * BLK] = mixed.T.astype(BF16)
            lse_ref[2 * p:2 * p + 1, pl.ds(at, BLK)] = log_total[:, :BLK]
            lse_ref[2 * p + 1:2 * p + 2, pl.ds(at, BLK)] = log_total[:, BLK:]
        return carry

    lax.fori_loop(0, L // BLK, query_step, 0)


def attend_call(lengths, qkv):
    return pl.pallas_call(
        attend_kernel,
        in_specs=[smem(), pl.BlockSpec(memory_space=pltpu.VMEM)],
        out_specs=[pl.BlockSpec(memory_space=pltpu.VMEM)] * 2,
        out_shape=[jax.ShapeDtypeStruct((L, D), BF16), jax.ShapeDtypeStruct((16, L), F32)],
        scratch_shapes=[
            pltpu.VMEM((D, L), BF16),
            pltpu.VMEM((PAIRS, 2 * BLK, BLK), BF16),
            pltpu.VMEM((PAIRS, BLK, BLK), F32),
            pltpu.VMEM((PAIRS, 8, 2 * BLK), F32),
            pltpu.VMEM((PAIRS, 8, 2 * BLK), F32),
        ],
        compiler_params=params(),
        cost_estimate=pl.CostEstimate(flops=4 * L * L * D, bytes_accessed=8_000_000, transcendentals=0),
        name="attend",
    )(lengths, qkv)


def attend_back_kernel(len_ref, qkv_ref, o_ref, go_ref, lse_ref, g_ref, sums_ref, kt, qm, gm, stat, dq, dk, dv):
    bounds = bounds_of(len_ref)
    for p in range(PAIRS):
        kt[p * BLK:(p + 1) * BLK, :] = qkv_ref[:, D + p * BLK:D + (p + 1) * BLK].T
    dk[...] = jnp.zeros_like(dk)
    dv[...] = jnp.zeros_like(dv)
    sums_ref[...] = jnp.zeros_like(sums_ref)

    def query_step(block, carry):
        at = pl.multiple_of(block * BLK, BLK)
        first, last = block_range(bounds, block)
        for p in range(PAIRS):
            cols = slice(p * BLK, (p + 1) * BLK)
            qm[p] = split_pair(qkv_ref[pl.ds(at, BLK), cols])
            grads = go_ref[pl.ds(at, BLK), cols]
            gm[p] = split_pair(grads)
            prod = (grads.astype(F32) * o_ref[pl.ds(at, BLK), cols].astype(F32)).T
            stat[p, 0:1, :BLK] = lse_ref[2 * p:2 * p + 1, pl.ds(at, BLK)]
            stat[p, 0:1, BLK:] = lse_ref[2 * p + 1:2 * p + 2, pl.ds(at, BLK)]
            stat[p, 1:2, :BLK] = jnp.sum(prod[:HD], axis=0, keepdims=True)
            stat[p, 1:2, BLK:] = jnp.sum(prod[HD:], axis=0, keepdims=True)
        dq[...] = jnp.zeros_like(dq)

        def key_step(key_block, carry):
            key_at = pl.multiple_of(key_block * BLK, BLK)
            hidden = hide(bounds, key_block, block)
            for p in range(PAIRS):
                cols = slice(p * BLK, (p + 1) * BLK)
                keys = qkv_ref[pl.ds(key_at, BLK), D + p * BLK:D + (p + 1) * BLK]
                vals = qkv_ref[pl.ds(key_at, BLK), 2 * D + p * BLK:2 * D + (p + 1) * BLK]
                soft = jnp.exp(dot_nt(keys, qm[p]) + (hidden - stat[p, 0:1, :]))
                grad_soft = dot_nt(vals, gm[p])
                grad_scores = (soft * (grad_soft - stat[p, 1:2, :])).astype(BF16)
                dv[pl.ds(key_at, BLK), cols] += dot_nn(soft.astype(BF16), gm[p])
                dk[pl.ds(key_at, BLK), cols] += dot_nn(grad_scores, qm[p])
                for side in range(2):
                    rows = slice(side * HD, (side + 1) * HD)
                    kside = kt[p * BLK + side * HD:p * BLK + (side + 1) * HD, pl.ds(key_at, BLK)]
                    dq[p, rows, :] += dot_nn(kside, grad_scores[:, side * BLK:(side + 1) * BLK])
            return carry

        lax.fori_loop(first, last, key_step, 0)
        for p in range(PAIRS):
            cols = slice(p * BLK, (p + 1) * BLK)
            done = (dq[p] * SCALE).T.astype(BF16)
            g_ref[pl.ds(at, BLK), cols] = done
            sums_ref[0:1, cols] += jnp.sum(done.astype(F32), axis=0, keepdims=True)
        return carry

    lax.fori_loop(0, L // BLK, query_step, 0)
    g_ref[:, D:2 * D] = dk[...].astype(BF16)
    gv = dv[...].astype(BF16)
    g_ref[:, 2 * D:] = gv
    sums_ref[1:2, :] = jnp.sum(gv.astype(F32), axis=0, keepdims=True)


def attend_back_call(lengths, qkv, o, go, lse):
    return pl.pallas_call(
        attend_back_kernel,
        in_specs=[smem()] + [pl.BlockSpec(memory_space=pltpu.VMEM)] * 4,
        out_specs=[pl.BlockSpec(memory_space=pltpu.VMEM)] * 2,
        out_shape=[jax.ShapeDtypeStruct((L, 3 * D), BF16), jax.ShapeDtypeStruct((8, D), F32)],
        scratch_shapes=[
            pltpu.VMEM((D, L), BF16),
            pltpu.VMEM((PAIRS, 2 * BLK, BLK), BF16),
            pltpu.VMEM((PAIRS, 2 * BLK, BLK), BF16),
            pltpu.VMEM((PAIRS, 8, 2 * BLK), F32),
            pltpu.VMEM((PAIRS, BLK, BLK), F32),
            pltpu.VMEM((L, D), F32),
            pltpu.VMEM((L, D), F32),
        ],
        compiler_params=params(),
        cost_estimate=pl.CostEstimate(flops=10 * L * L * D, bytes_accessed=15_000_000, transcendentals=0),
        name="attend_back",
    )(lengths, qkv, o, go, lse)


def gate_pair(h):
    size = jnp.abs(h)
    t = 1.0 / (1.0 + (0.3275911 * 0.7071067811865476) * size)
    bell = jnp.exp(-0.5 * h * h)
    poly = t * (0.127414796 + t * (-0.142248368 + t * (0.7107068705 + t * (-0.7265760135 + t * 0.5307027145))))
    tail = poly * bell
    cdf = jnp.where(h >= 0.0, 1.0 - tail, tail)
    return h * cdf, cdf + h * (0.3989422804014327 * bell)


def up_kernel(o_ref, x_ref, vec_ref, wo_ref, wu_ref, bu_ref, mid_ref, n2_ref, a_ref, slope_ref):
    middle = x_ref[...].astype(F32) + (dot_nn(o_ref[...], wo_ref[...]) + vec_ref[6:7, :])
    mid_ref[...] = middle
    hat, _ = norm_parts(middle)
    n2 = (hat * (1.0 + vec_ref[2:3, :]) + vec_ref[3:4, :]).astype(BF16)
    n2_ref[...] = n2
    width = 512
    for c in range(FF // width):
        cols = slice(c * width, (c + 1) * width)
        h = dot_nn(n2, wu_ref[:, cols]) + bu_ref[:, cols]
        act, slope = gate_pair(h)
        a_ref[:, cols] = act.astype(BF16)
        slope_ref[:, cols] = slope.astype(BF16)


def up_call(o, x, vec, wo, wu, bu):
    return pl.pallas_call(
        up_kernel,
        grid=(TILES,),
        in_specs=[rows_of(D), rows_of(D), whole(vec.shape), whole(wo.shape), whole(wu.shape), whole(bu.shape)],
        out_specs=[rows_of(D), rows_of(D), rows_of(FF), rows_of(FF)],
        out_shape=[
            jax.ShapeDtypeStruct((L, D), F32),
            jax.ShapeDtypeStruct((L, D), BF16),
            jax.ShapeDtypeStruct((L, FF), BF16),
            jax.ShapeDtypeStruct((L, FF), BF16),
        ],
        compiler_params=params(),
        cost_estimate=pl.CostEstimate(flops=2 * L * D * (FF + D), bytes_accessed=25_000_000, transcendentals=2 * L * FF),
        name="feed_up",
    )(o, x, vec, wo, wu, bu)


def down_kernel(a_ref, mid_ref, vec_ref, wdt_ref, y_ref):
    y_ref[...] = (mid_ref[...] + (dot_nt(a_ref[...], wdt_ref[...]) + vec_ref[7:8, :])).astype(BF16)


def down_call(a, middle, vec, wdt):
    return pl.pallas_call(
        down_kernel,
        grid=(TILES,),
        in_specs=[rows_of(FF), rows_of(D), whole(vec.shape), whole(wdt.shape)],
        out_specs=rows_of(D),
        out_shape=jax.ShapeDtypeStruct((L, D), BF16),
        compiler_params=params(),
        cost_estimate=pl.CostEstimate(flops=2 * L * D * FF, bytes_accessed=17_000_000, transcendentals=0),
        name="feed_down",
    )(a, middle, vec, wdt)


def norm_back(grad, hat, inv, gain):
    scaled = grad * (1.0 + gain)
    both = jnp.mean(scaled * hat, axis=-1, keepdims=True)
    return inv * (scaled - jnp.mean(scaled, axis=-1, keepdims=True) - hat * both)


def feed_back_kernel(gy_ref, slope_ref, mid_ref, vec_ref, wdt_ref, wu_ref, wo_ref,
                     gh_ref, gmid_ref, gatt_ref, go_ref, sums_ref, bup_ref):
    @pl.when(pl.program_id(0) == 0)
    def _():
        sums_ref[...] = jnp.zeros_like(sums_ref)
        bup_ref[...] = jnp.zeros_like(bup_ref)

    gm = gy_ref[...]
    gy = gm.astype(F32)
    width = 768
    gn2 = None
    for c in range(FF // width):
        cols = slice(c * width, (c + 1) * width)
        ga = dot_nn(gm, wdt_ref[:, cols])
        gh = (ga * slope_ref[:, cols].astype(F32)).astype(BF16)
        gh_ref[:, cols] = gh
        bup_ref[0:1, cols] += jnp.sum(gh.astype(F32), axis=0, keepdims=True)
        part = dot_nt(gh, wu_ref[:, cols])
        gn2 = part if gn2 is None else gn2 + part
    hat, inv = norm_parts(mid_ref[...])
    sums_ref[0:1, :] += jnp.sum(gn2 * hat, axis=0, keepdims=True)
    sums_ref[1:2, :] += jnp.sum(gn2, axis=0, keepdims=True)
    gmid = gy + norm_back(gn2, hat, inv, vec_ref[2:3, :])
    gmid_ref[...] = gmid
    gatt = gmid.astype(BF16)
    gatt_ref[...] = gatt
    sums_ref[2:3, :] += jnp.sum(gatt.astype(F32), axis=0, keepdims=True)
    sums_ref[3:4, :] += jnp.sum(gy, axis=0, keepdims=True)
    go_ref[...] = dot_nt(gatt, wo_ref[...]).astype(BF16)


def feed_back_call(gy, slope, middle, vec, wdt, wu, wo):
    return pl.pallas_call(
        feed_back_kernel,
        grid=(TILES,),
        in_specs=[rows_of(D), rows_of(FF), rows_of(D), whole(vec.shape), whole(wdt.shape), whole(wu.shape), whole(wo.shape)],
        out_specs=[rows_of(FF), rows_of(D), rows_of(D), rows_of(D), whole((8, D)), whole((8, FF))],
        out_shape=[
            jax.ShapeDtypeStruct((L, FF), BF16),
            jax.ShapeDtypeStruct((L, D), F32),
            jax.ShapeDtypeStruct((L, D), BF16),
            jax.ShapeDtypeStruct((L, D), BF16),
            jax.ShapeDtypeStruct((8, D), F32),
            jax.ShapeDtypeStruct((8, FF), F32),
        ],
        compiler_params=params(),
        cost_estimate=pl.CostEstimate(flops=2 * L * D * (2 * FF + D), bytes_accessed=35_000_000, transcendentals=0),
        name="feed_back",
    )(gy, slope, middle, vec, wdt, wu, wo)


def outer_kernel(left_ref, right_ref, out_ref, turned):
    @pl.when(pl.program_id(0) == 0)
    def _():
        turned[...] = left_ref[...].T

    out_ref[...] = dot_nn(turned[...], right_ref[...]).astype(BF16)


def outer_call(left, right, name):
    wide = right.shape[1]
    width = 768
    return pl.pallas_call(
        outer_kernel,
        grid=(wide // width,),
        in_specs=[whole(left.shape), pl.BlockSpec((L, width), lambda i: (0, i))],
        out_specs=pl.BlockSpec((D, width), lambda i: (0, i)),
        out_shape=jax.ShapeDtypeStruct((D, wide), BF16),
        scratch_shapes=[pltpu.VMEM((D, L), BF16)],
        compiler_params=params(),
        cost_estimate=pl.CostEstimate(flops=2 * L * D * wide, bytes_accessed=4 * L * D + 4 * D * wide, transcendentals=0),
        name=name,
    )(left, right)


def first_back_kernel(len_ref, lead_ref, x_ref, gmid_ref, g_ref, vec_ref, w_ref, out_ref, sums_ref, table_ref):
    step = pl.program_id(0)

    @pl.when(step == 0)
    def _():
        sums_ref[...] = jnp.zeros_like(sums_ref)
        table_ref[...] = jnp.zeros_like(table_ref)

    gn1 = dot_nt(g_ref[...], w_ref[...])
    hat, inv = norm_parts(x_ref[...].astype(F32))
    sums_ref[0:1, :] += jnp.sum(gn1 * hat, axis=0, keepdims=True)
    sums_ref[1:2, :] += jnp.sum(gn1, axis=0, keepdims=True)
    shape = (table_ref.shape[0], ROWS)
    places = step * ROWS + lax.broadcasted_iota(jnp.int32, shape, 1)
    hot = lead_of(places, bounds_of(len_ref), lead_ref) == lax.broadcasted_iota(jnp.int32, shape, 0)
    hot = hot.astype(BF16)
    high = gn1.astype(BF16)
    low = (gn1 - high.astype(F32)).astype(BF16)
    table_ref[...] += dot_nn(hot, high) + dot_nn(hot, low)
    out_ref[...] = gmid_ref[...] + norm_back(gn1, hat, inv, vec_ref[0:1, :])


def first_back_call(lengths, leads, x, gmid, gqkv, vec, w):
    return pl.pallas_call(
        first_back_kernel,
        grid=(TILES,),
        in_specs=[smem(), smem(), rows_of(D), rows_of(D), rows_of(3 * D), whole(vec.shape), whole(w.shape)],
        out_specs=[rows_of(D), whole((8, D)), whole((32, D))],
        out_shape=[
            jax.ShapeDtypeStruct((L, D), F32),
            jax.ShapeDtypeStruct((8, D), F32),
            jax.ShapeDtypeStruct((32, D), F32),
        ],
        compiler_params=params(),
        cost_estimate=pl.CostEstimate(flops=2 * L * D * 3 * D, bytes_accessed=17_000_000, transcendentals=0),
        name="first_back",
    )(lengths, leads, x, gmid, gqkv, vec, w)


def hop_dp(value, flip, ranks):
    return lax.ppermute(value, "dp", [(i, i ^ flip) for i in range(ranks)])


def hop_fsdp(value, flip, ranks):
    return lax.ppermute(value, "fsdp", [(i, i ^ flip) for i in range(ranks)])


def after(value, *others):
    return lax.optimization_barrier((value,) + others)[0]


def gather_shards(piece, sizes):
    dps, fss = sizes
    deep = fss // 2
    along = [piece] + [hop_fsdp(piece, 2 * z, fss) for z in range(1, deep)]
    half = max(deep // 2, 1)
    first, second = jnp.stack(along[:half]), jnp.stack(along[half:])
    by_x = [hop_dp(first, 2, dps), hop_dp(second, 2, dps)]
    by_y = [hop_fsdp(first, 1, fss), hop_fsdp(second, 1, fss)]
    corner = [hop_fsdp(by_x[0], 1, fss), hop_dp(by_y[1], 2, dps)]
    found = []
    for x, y, pair in ((0, 0, (first, second)), (1, 0, by_x), (0, 1, by_y), (1, 1, corner)):
        for base, part in ((0, pair[0]), (half, pair[1])):
            found.append((2 * x, 2 * base + y, part))
            found.append((2 * x + 1, 2 * base + y, hop_dp(part, 1, dps)))
    return found, along[-1]


def slots(found):
    return [
        (at, k, dp, fs + 2 * k)
        for at, (dp, fs, part) in enumerate(found)
        for k in range(part.shape[0])
    ]


def any_space():
    return pl.BlockSpec(memory_space=pl.ANY)


def in_vmem():
    return pl.BlockSpec(memory_space=pltpu.VMEM)


def lay_first_kernel(plan, count, ids_ref, *refs):
    parts, (w_ref, vec_ref, table_ref, bias_ref, stage, table_f32, sem) = refs[:count], refs[count:]
    copies = []
    for at, k, dp, fs in plan:
        copies.append(pltpu.make_async_copy(parts[at].at[k], stage.at[ids_ref[0] ^ dp, ids_ref[1] ^ fs], sem))
    for copy in copies:
        copy.start()
    for copy in copies:
        copy.wait()
    table_f32[...] = jnp.zeros_like(table_f32)
    for d in range(stage.shape[0]):
        for f in range(stage.shape[1]):
            rows, cols = stage.shape[2], 3 * D // stage.shape[1]
            w_ref[d * rows:(d + 1) * rows, f * cols:(f + 1) * cols] = stage[d, f, :, :cols]
            wide = D // stage.shape[1]
            small = stage[d, f, 0:16, cols:cols + wide].astype(F32)
            at = slice(f * wide, (f + 1) * wide)
            vec_ref[2 * d:2 * d + 2, at] = small[0:2]
            table_f32[5 * d:5 * d + 5, at] = small[2:7]
            bias_ref[0:1, d * D + f * wide:d * D + (f + 1) * wide] = small[7:8]
    table_ref[...] = table_f32[...].astype(BF16)


def lay_first(found, ids, sizes):
    parts = [part for _, _, part in found]
    rows, cols = parts[0].shape[1:]
    return pl.pallas_call(
        functools.partial(lay_first_kernel, slots(found), len(parts)),
        in_specs=[smem()] + [any_space()] * len(parts),
        out_specs=[in_vmem()] * 4,
        out_shape=[
            jax.ShapeDtypeStruct((D, 3 * D), BF16),
            jax.ShapeDtypeStruct((8, D), F32),
            jax.ShapeDtypeStruct((32, D), BF16),
            jax.ShapeDtypeStruct((1, FF), F32),
        ],
        scratch_shapes=[
            pltpu.VMEM(sizes + (rows, cols), BF16),
            pltpu.VMEM((32, D), F32),
            pltpu.SemaphoreType.DMA,
        ],
        compiler_params=params(),
        cost_estimate=pl.CostEstimate(flops=0, bytes_accessed=12_000_000, transcendentals=0),
        name="lay_first",
    )(ids, *parts)


def lay_up_kernel(plan, count, ids_ref, *refs):
    parts, (wu_ref, wo_ref, stage, sem) = refs[:count], refs[count:]
    dps, fss, rows, _ = stage.shape
    tall, wide = D // dps, FF // fss
    copies = []
    for at, k, dp, fs in plan:
        d, f = ids_ref[0] ^ dp, ids_ref[1] ^ fs
        rest = parts[at].at[k, pl.ds(tall, rows), :]
        copies.append(pltpu.make_async_copy(rest, stage.at[d, f], sem))
        there = wu_ref.at[pl.ds(pl.multiple_of(d * tall, tall), tall), pl.ds(pl.multiple_of(f * wide, wide), wide)]
        copies.append(pltpu.make_async_copy(parts[at].at[k, pl.ds(0, tall), :], there, sem))
    for copy in copies:
        copy.start()
    for copy in copies:
        copy.wait()
    narrow = D // fss
    for d in range(dps):
        for f in range(fss):
            for h in range(tall // rows):
                at = d * tall + h * rows
                wo_ref[at:at + rows, f * narrow:(f + 1) * narrow] = stage[d, f, :, h * narrow:(h + 1) * narrow]


def lay_up(found, ids, sizes):
    parts = [part for _, _, part in found]
    rows, cols = parts[0].shape[1:]
    return pl.pallas_call(
        functools.partial(lay_up_kernel, slots(found), len(parts)),
        in_specs=[smem()] + [any_space()] * len(parts),
        out_specs=[in_vmem()] * 2,
        out_shape=[jax.ShapeDtypeStruct((D, FF), BF16), jax.ShapeDtypeStruct((D, D), BF16)],
        scratch_shapes=[
            pltpu.VMEM(sizes + (rows - D // sizes[0], cols), BF16),
            pltpu.SemaphoreType.DMA,
        ],
        compiler_params=params(),
        cost_estimate=pl.CostEstimate(flops=0, bytes_accessed=12_000_000, transcendentals=0),
        name="lay_up",
    )(ids, *parts)


def lay_down_kernel(plan, count, ids_ref, *refs):
    parts, (wd_ref, sem) = refs[:count], refs[count:]
    tall, wide = parts[0].shape[1:]
    copies = []
    for at, k, dp, fs in plan:
        d, f = ids_ref[0] ^ dp, ids_ref[1] ^ fs
        there = wd_ref.at[pl.ds(pl.multiple_of(f * tall, tall), tall), pl.ds(pl.multiple_of(d * wide, wide), wide)]
        copies.append(pltpu.make_async_copy(parts[at].at[k], there, sem))
    for copy in copies:
        copy.start()
    for copy in copies:
        copy.wait()


def lay_down(found, ids):
    parts = [part for _, _, part in found]
    return pl.pallas_call(
        functools.partial(lay_down_kernel, slots(found), len(parts)),
        in_specs=[smem()] + [any_space()] * len(parts),
        out_specs=in_vmem(),
        out_shape=jax.ShapeDtypeStruct((D, FF), BF16),
        scratch_shapes=[pltpu.SemaphoreType.DMA],
        compiler_params=params(),
        cost_estimate=pl.CostEstimate(flops=0, bytes_accessed=10_000_000, transcendentals=0),
        name="lay_down",
    )(ids, *parts)


def order_rows(left_ref, plain, ordered, mine, count):
    plain[...] = left_ref[...].T
    tall = ordered.shape[0] // count
    for k in range(count):
        at = pl.multiple_of((mine ^ k) * tall, tall)
        ordered[k * tall:(k + 1) * tall, :] = plain[pl.ds(at, tall), :]


def cut_up_kernel(sizes, ids_ref, n2_ref, gh_ref, o_ref, gatt_ref, mine_ref, theirs_ref, plain, left, packed, full):
    dps, fss = sizes
    tall = D // dps
    step = pl.program_id(0)
    rows = mine_ref.shape[3] - tall
    narrow = D // fss

    @pl.when(step == 0)
    def _():
        order_rows(o_ref, plain, left, ids_ref[0], dps)
        full[...] = dot_nn(left[...], gatt_ref[...]).astype(BF16)
        for f in range(fss):
            for d in range(dps):
                for h in range(tall // rows):
                    at = d * tall + h * rows
                    packed[ids_ref[1] ^ f, d, :, h * narrow:(h + 1) * narrow] = full[at:at + rows, f * narrow:(f + 1) * narrow]
        order_rows(n2_ref, plain, left, ids_ref[0], dps)

    grad = dot_nn(left[...], gh_ref[...]).astype(BF16)
    for d in range(dps):
        ref = theirs_ref if d & 1 else mine_ref
        ref[d >> 1, 0, 0, :tall, :] = grad[d * tall:(d + 1) * tall]
        ref[d >> 1, 0, 0, tall:, :] = packed[step, d]


def cut_up(n2, gh, o, gatt, ids, sizes):
    dps, fss = sizes
    wide, tall = FF // fss, D // dps
    rows = tall * (D // fss) // wide
    shape = jax.ShapeDtypeStruct((dps // 2, 2, fss // 2, tall + rows, wide), BF16)
    block = pl.BlockSpec((dps // 2, 1, 1, tall + rows, wide), lambda i, ids: (0, i & 1, i >> 1, 0, 0))
    fixed = pl.BlockSpec((L, D), lambda i, ids: (0, 0))
    return pl.pallas_call(
        functools.partial(cut_up_kernel, sizes),
        grid_spec=pltpu.PrefetchScalarGridSpec(
            num_scalar_prefetch=1,
            grid=(fss,),
            in_specs=[fixed, pl.BlockSpec((L, wide), lambda i, ids: (0, i ^ ids[1])), fixed, fixed],
            out_specs=[block, block],
            scratch_shapes=[
                pltpu.VMEM((D, L), BF16),
                pltpu.VMEM((D, L), BF16),
                pltpu.VMEM((fss, dps, rows, wide), BF16),
                pltpu.VMEM((D, D), BF16),
            ],
        ),
        out_shape=[shape, shape],
        compiler_params=params(),
        cost_estimate=pl.CostEstimate(flops=2 * L * D * (FF + D), bytes_accessed=20_000_000, transcendentals=0),
        name="cut_up",
    )(ids, n2, gh, o, gatt)


def cut_down_kernel(sizes, ids_ref, gm_ref, a_ref, mine_ref, theirs_ref, plain, left):
    dps, fss = sizes
    step = pl.program_id(0)
    tall = D // fss

    @pl.when(step == 0)
    def _():
        order_rows(gm_ref, plain, left, ids_ref[1], fss)

    grad = dot_nn(left[...], a_ref[...]).astype(BF16)

    def store(ref):
        for f in range(fss):
            ref[0, f & 1, f >> 1] = grad[f * tall:(f + 1) * tall]

    @pl.when(step < dps // 2)
    def _():
        store(mine_ref)

    @pl.when(step >= dps // 2)
    def _():
        store(theirs_ref)


def cut_down(gm, a, ids, sizes):
    dps, fss = sizes
    half = dps // 2
    wide, tall = FF // dps, D // fss
    shape = jax.ShapeDtypeStruct((half, 2, fss // 2, tall, wide), BF16)
    block = (1, 2, fss // 2, tall, wide)

    def flip(i):
        return 2 * (i % half) + i // half

    return pl.pallas_call(
        functools.partial(cut_down_kernel, sizes),
        grid_spec=pltpu.PrefetchScalarGridSpec(
            num_scalar_prefetch=1,
            grid=(dps,),
            in_specs=[
                pl.BlockSpec((L, D), lambda i, ids: (0, 0)),
                pl.BlockSpec((L, wide), lambda i, ids: (0, flip(i) ^ ids[0])),
            ],
            out_specs=[
                pl.BlockSpec(block, lambda i, ids: (jnp.minimum(i, half - 1), 0, 0, 0, 0)),
                pl.BlockSpec(block, lambda i, ids: (jnp.maximum(i - half, 0), 0, 0, 0, 0)),
            ],
            scratch_shapes=[pltpu.VMEM((D, L), BF16), pltpu.VMEM((D, L), BF16)],
        ),
        out_shape=[shape, shape],
        compiler_params=params(),
        cost_estimate=pl.CostEstimate(flops=2 * L * D * FF, bytes_accessed=14_000_000, transcendentals=0),
        name="cut_down",
    )(ids, gm, a)


def cut_qkv_kernel(sizes, ids_ref, n1_ref, g_ref, small_ref, mine_ref, theirs_ref, plain, left, full):
    dps, fss = sizes
    tall, cols, wide = D // dps, 3 * D // fss, D // fss
    order_rows(n1_ref, plain, left, ids_ref[0], dps)
    for third in range(3):
        at = slice(third * D, (third + 1) * D)
        full[:, at] = dot_nn(left[...], g_ref[:, at]).astype(BF16)
    for f in range(fss):
        flip = ids_ref[1] ^ f
        for d in range(dps):
            ref = theirs_ref if d & 1 else mine_ref
            rows = slice(d * tall, (d + 1) * tall)
            ref[d >> 1, flip & 1, flip >> 1, :, :cols] = full[rows, f * cols:(f + 1) * cols]
            own = small_ref[ids_ref[0] ^ d, :, f * wide:(f + 1) * wide].astype(BF16)
            ref[d >> 1, flip & 1, flip >> 1, :, cols:] = jnp.zeros((tall, wide), BF16)
            ref[d >> 1, flip & 1, flip >> 1, 0:16, cols:] = own


def cut_qkv(n1, gqkv, small, ids, sizes):
    dps, fss = sizes
    shape = jax.ShapeDtypeStruct((dps // 2, 2, fss // 2, D // dps, 4 * D // fss), BF16)
    return pl.pallas_call(
        functools.partial(cut_qkv_kernel, sizes),
        in_specs=[smem()] + [in_vmem()] * 3,
        out_specs=[in_vmem()] * 2,
        out_shape=[shape, shape],
        scratch_shapes=[pltpu.VMEM((D, L), BF16), pltpu.VMEM((D, L), BF16), pltpu.VMEM((D, 3 * D), BF16)],
        compiler_params=params(),
        cost_estimate=pl.CostEstimate(flops=2 * L * D * 3 * D, bytes_accessed=12_000_000, transcendentals=0),
        name="cut_qkv",
    )(ids, n1, gqkv, small)


def plus(*terms):
    return sum(term.astype(F32) for term in terms)


def reduce_shards(mine, theirs, sizes):
    dps, fss = sizes
    deep = fss // 2
    half = deep // 2
    both = plus(mine, hop_dp(theirs, 1, dps)).astype(BF16)
    first, second = both[:, :, :half], both[:, :, half:]
    got_x = hop_dp(first[1], 2, dps)
    got_y = hop_fsdp(second[:, 1], 1, fss)
    first = plus(first[0], got_x).astype(BF16)
    second = plus(second[:, 0], got_y).astype(BF16)
    got_y = hop_fsdp(first[1], 1, fss)
    got_x = hop_dp(second[1], 2, dps)
    first = plus(first[0], got_y).astype(BF16)
    second = plus(second[0], got_x).astype(BF16)
    apart = [first[k] for k in range(half)] + [second[k] for k in range(deep - half)]
    return plus(apart[0], *[hop_fsdp(apart[z], 2 * z, fss) for z in range(1, deep)])


def compute(tokens, lengths, lead_index, cotangent, weights, reduce_down, reduce_up, reduce_qkv):
    w_qkv, vec, table, bias, w_up, w_out, w_down_t = weights
    x, gy = tokens.reshape(L, D), cotangent.reshape(L, D)
    n1, qkv = qkv_call(lengths, lead_index, x, vec, table, w_qkv)
    o, lse = attend_call(lengths, qkv)
    middle, n2, a, slope = up_call(o, x, vec, w_out, w_up, bias)
    down = reduce_down(gy, a)
    gh, gmid, gatt, go, sums, bup = feed_back_call(gy, slope, middle, vec, w_down_t, w_up, w_out)
    up, out = reduce_up(n2, gh, o, gatt)
    gqkv, qsums = attend_back_call(lengths, qkv, o, go, lse)
    gx, first_sums, gtable = first_back_call(lengths, lead_index, x, gmid, gqkv, vec, w_qkv)
    gvec = jnp.concatenate([first_sums[:2], sums[:2], qsums[:2], sums[2:4]], axis=0)
    qkv_grad, gvec, gtable, gbias = reduce_qkv(n1, gqkv, gvec, gtable[:LEADS], bup[0].reshape(FF // D, D))
    y = down_call(a, middle, vec, w_down_t)
    return y.reshape(1, L, D), gx.reshape(1, L, D), qkv_grad, out, up, down, gvec, gtable, gbias


def per_device(sizes, tokens, lengths, lead_index, cotangent, w_qkv, w_out, w_up, w_down, vectors, table, bias):
    dps, fss = sizes
    ids = jnp.stack([lax.axis_index("dp"), lax.axis_index("fsdp")]).astype(jnp.int32)
    narrow, wide, tall = D // fss, FF // fss, D // dps
    fold = wide // narrow
    small = jnp.concatenate([vectors, table, bias], axis=0)
    piece = jnp.concatenate([w_qkv, jnp.pad(small, ((0, tall - small.shape[0]), (0, 0)))], axis=1)
    found, done = gather_shards(piece, sizes)
    w_qkv, vec, table, bias = lay_first(found, ids, sizes)
    rows = tall // fold
    folded = jnp.concatenate([w_out[k * rows:(k + 1) * rows] for k in range(fold)], axis=1)
    piece = after(jnp.concatenate([w_up, folded], axis=0), done)
    found, done = gather_shards(piece, sizes)
    w_up, w_out = lay_up(found, ids, sizes)
    piece = after(w_down.T, done)
    found, done = gather_shards(piece, sizes)
    w_down_t = lay_down(found, ids)

    def reduce_down(gm, a):
        return reduce_shards(*cut_down(gm, a, ids, sizes), sizes).T

    def reduce_up(n2, gh, o, gatt):
        got = reduce_shards(*cut_up(n2, gh, o, gatt, ids, sizes), sizes)
        out = jnp.concatenate([got[tall:, k * narrow:(k + 1) * narrow] for k in range(fold)], axis=0)
        return got[:tall], out

    def reduce_qkv(n1, gqkv, gvec, gtable, gbias):
        parts = [gvec.reshape(dps, -1, D), gtable.reshape(dps, -1, D), gbias.reshape(dps, -1, D)]
        parts = jnp.concatenate(parts, axis=1)
        parts = jnp.pad(parts, ((0, 0), (0, 16 - parts.shape[1]), (0, 0)))
        got = reduce_shards(*cut_qkv(n1, gqkv, parts, ids, sizes), sizes)
        cols = 3 * narrow
        return got[:, :cols], got[0:2, cols:], got[2:7, cols:], got[7:8, cols:]

    weights = (w_qkv, vec, table, bias, w_up, w_out, w_down_t)
    return compute(tokens, lengths, lead_index, cotangent, weights, reduce_down, reduce_up, reduce_qkv)


def per_device_plain(sizes, tokens, lengths, lead_index, cotangent, w_qkv, w_out, w_up, w_down, vectors, table, bias):
    def full(shard):
        return lax.all_gather(lax.all_gather(shard, "fsdp", axis=1, tiled=True), "dp", axis=0, tiled=True)

    def share(grad):
        part = lax.psum_scatter(grad.astype(F32), "fsdp", scatter_dimension=1, tiled=True)
        return lax.psum_scatter(part, "dp", scatter_dimension=0, tiled=True)

    weights = (
        full(w_qkv),
        full(vectors).astype(F32),
        jnp.pad(full(table), ((0, 32 - LEADS), (0, 0))),
        full(bias).astype(F32).reshape(1, FF),
        full(w_up),
        full(w_out),
        full(w_down).T,
    )

    def reduce_down(gm, a):
        return share(outer_call(gm, a, "grad_down").T)

    def reduce_up(n2, gh, o, gatt):
        return share(outer_call(n2, gh, "grad_up")), share(outer_call(o, gatt, "grad_out"))

    def reduce_qkv(n1, gqkv, gvec, gtable, gbias):
        return share(outer_call(n1, gqkv, "grad_qkv")), share(gvec), share(gtable), share(gbias)

    return compute(tokens, lengths, lead_index, cotangent, weights, reduce_down, reduce_up, reduce_qkv)


def solution(mesh):
    sizes = (mesh.shape["dp"], mesh.shape["fsdp"])
    lanes = FF // sizes[1]
    plan = per_device if lanes % 128 == 0 and sizes[0] == 4 and sizes[1] % 4 == 0 else per_device_plain
    rows, both = P(("dp", "fsdp"), None, None), P("dp", "fsdp")
    index = P(("dp", "fsdp"), None)
    return jax.shard_map(
        functools.partial(plan, sizes),
        mesh=mesh,
        in_specs=(rows, index, index, rows) + (both,) * 7,
        out_specs=(rows, rows) + (both,) * 7,
        check_vma=False,
    )
```

```python
import functools

import jax
import jax.numpy as jnp
from jax import lax
from jax.experimental import pallas as pl
from jax.experimental.pallas import tpu as pltpu
from jax.sharding import PartitionSpec as P

D = 768
HEADS = 12
HD = 64
FF = 3072
LEADS = 20
WIN = 8
L = 1024
EPSILON = 1e-05
MASKED = -1e30
ROWS = 256
TILES = L // ROWS
BLK = 128
PAIRS = HEADS // 2
SCALE = HD ** (-0.5)
VMEM_BYTES = 56 * 1024 * 1024

F32 = jnp.float32
BF16 = jnp.bfloat16


def params(limit=VMEM_BYTES):
    return pltpu.CompilerParams(vmem_limit_bytes=limit)


def dot_nn(a, b):
    return lax.dot_general(a, b, (((1,), (0,)), ((), ())), preferred_element_type=F32)


def dot_nt(a, b):
    return lax.dot_general(a, b, (((1,), (1,)), ((), ())), preferred_element_type=F32)


def whole(shape, space=pltpu.VMEM):
    return pl.BlockSpec(shape, lambda *_: (0,) * len(shape), memory_space=space)


def smem():
    return pl.BlockSpec(memory_space=pltpu.SMEM)


def rows_of(width):
    return pl.BlockSpec((ROWS, width), lambda i: (i, 0))


def norm_parts(values):
    center = values - jnp.mean(values, axis=-1, keepdims=True)
    spread = jnp.mean(center * center, axis=-1, keepdims=True)
    inv = lax.rsqrt(spread + EPSILON)
    return center * inv, inv


def bounds_of(lengths_ref):
    found, total = [], 0
    for w in range(WIN):
        total = total + lengths_ref[0, w]
        found.append(total)
    return found


def lead_of(places, bounds, lead_ref):
    lead = jnp.full(places.shape, -1, jnp.int32)
    for w in reversed(range(WIN)):
        lead = jnp.where(places < bounds[w], lead_ref[0, w], lead)
    return lead


def qkv_kernel(len_ref, lead_ref, x_ref, vec_ref, table_ref, w_ref, n1_ref, qkv_ref):
    step = pl.program_id(0)
    bounds = bounds_of(len_ref)
    hat, _ = norm_parts(x_ref[...].astype(F32))
    normed = hat * (1.0 + vec_ref[0:1, :]) + vec_ref[1:2, :]
    shape = (ROWS, table_ref.shape[0])
    places = step * ROWS + lax.broadcasted_iota(jnp.int32, shape, 0)
    hot = lead_of(places, bounds, lead_ref) == lax.broadcasted_iota(jnp.int32, shape, 1)
    n1 = (normed + dot_nn(hot.astype(BF16), table_ref[...])).astype(BF16)
    n1_ref[...] = n1
    for third in range(3):
        cols = slice(third * D, (third + 1) * D)
        part = dot_nn(n1, w_ref[:, cols])
        if third == 0:
            part = (part + vec_ref[4:5, :]).astype(BF16) * jnp.asarray(SCALE, BF16)
        elif third == 2:
            part = part + vec_ref[5:6, :]
        qkv_ref[:, cols] = part.astype(BF16)


def qkv_call(lengths, leads, x, vec, table, w):
    return pl.pallas_call(
        qkv_kernel,
        grid=(TILES,),
        in_specs=[smem(), smem(), rows_of(D), whole(vec.shape), whole(table.shape), whole(w.shape)],
        out_specs=[rows_of(D), rows_of(3 * D)],
        out_shape=[jax.ShapeDtypeStruct((L, D), BF16), jax.ShapeDtypeStruct((L, 3 * D), BF16)],
        compiler_params=params(),
        cost_estimate=pl.CostEstimate(flops=2 * L * D * 3 * D, bytes_accessed=12_000_000, transcendentals=0),
        name="norm_qkv",
    )(lengths, leads, x, vec, table, w)


def block_range(bounds, block):
    first, last = block * BLK, block * BLK + BLK - 1
    start, end = jnp.int32(0), jnp.int32(L)
    for w in range(WIN):
        start = jnp.where(bounds[w] <= first, bounds[w], start)
    for w in reversed(range(WIN)):
        end = jnp.where(bounds[w] > last, bounds[w], end)
    return start // BLK, (end + BLK - 1) // BLK


def window_at(places, bounds):
    found = jnp.zeros(places.shape, jnp.int32)
    for w in range(WIN):
        found = found + (places >= bounds[w]).astype(jnp.int32)
    return found


def hide(bounds, key_block, query_block):
    shape = (BLK, BLK)
    keys = window_at(key_block * BLK + lax.broadcasted_iota(jnp.int32, (BLK, 1), 0), bounds)
    queries = window_at(query_block * BLK + lax.broadcasted_iota(jnp.int32, (1, BLK), 1), bounds)
    one = jnp.where(jnp.broadcast_to(keys, shape) == jnp.broadcast_to(queries, shape), 0.0, MASKED)
    return jnp.concatenate([one, one], axis=1)


def split_pair(two):
    lanes = lax.broadcasted_iota(jnp.int32, two.shape, 1)
    zero = jnp.zeros_like(two)
    return jnp.concatenate([jnp.where(lanes < HD, two, zero), jnp.where(lanes < HD, zero, two)], axis=0)


def attend_kernel(len_ref, qkv_ref, o_ref, lse_ref, vt, qm, acc, top, tot):
    bounds = bounds_of(len_ref)
    for p in range(PAIRS):
        vt[p * BLK:(p + 1) * BLK, :] = qkv_ref[:, 2 * D + p * BLK:2 * D + (p + 1) * BLK].T
    lse_ref[HEADS:, :] = jnp.zeros((lse_ref.shape[0] - HEADS, L), F32)

    def query_step(block, carry):
        at = pl.multiple_of(block * BLK, BLK)
        first, last = block_range(bounds, block)
        for p in range(PAIRS):
            qm[p] = split_pair(qkv_ref[pl.ds(at, BLK), p * BLK:(p + 1) * BLK])
        acc[...] = jnp.zeros_like(acc)
        top[...] = jnp.full_like(top, MASKED)
        tot[...] = jnp.zeros_like(tot)

        def key_step(key_block, carry):
            key_at = pl.multiple_of(key_block * BLK, BLK)
            hidden = hide(bounds, key_block, block)
            for p in range(PAIRS):
                keys = qkv_ref[pl.ds(key_at, BLK), D + p * BLK:D + (p + 1) * BLK]
                scores = dot_nt(keys, qm[p]) + hidden
                old = top[p, 0:1, :]
                new = jnp.maximum(old, jnp.max(scores, axis=0, keepdims=True))
                expo = jnp.exp(scores - new)
                fade = jnp.exp(old - new)
                top[p, 0:1, :] = new
                tot[p, 0:1, :] = tot[p, 0:1, :] * fade + jnp.sum(expo, axis=0, keepdims=True)
                soft = expo.astype(BF16)
                for side in range(2):
                    rows = slice(side * HD, (side + 1) * HD)
                    cols = slice(side * BLK, (side + 1) * BLK)
                    vals = vt[p * BLK + side * HD:p * BLK + (side + 1) * HD, pl.ds(key_at, BLK)]
                    acc[p, rows, :] = acc[p, rows, :] * fade[:, cols] + dot_nn(vals, soft[:, cols])
            return carry

        lax.fori_loop(first, last, key_step, 0)
        for p in range(PAIRS):
            total = tot[p, 0:1, :]
            inv = 1.0 / total
            log_total = top[p, 0:1, :] + jnp.log(total)
            mixed = jnp.concatenate([acc[p, :HD, :] * inv[:, :BLK], acc[p, HD:, :] * inv[:, BLK:]], axis=0)
            o_ref[pl.ds(at, BLK), p * BLK:(p + 1) * BLK] = mixed.T.astype(BF16)
            lse_ref[2 * p:2 * p + 1, pl.ds(at, BLK)] = log_total[:, :BLK]
            lse_ref[2 * p + 1:2 * p + 2, pl.ds(at, BLK)] = log_total[:, BLK:]
        return carry

    lax.fori_loop(0, L // BLK, query_step, 0)


def attend_call(lengths, qkv):
    return pl.pallas_call(
        attend_kernel,
        in_specs=[smem(), pl.BlockSpec(memory_space=pltpu.VMEM)],
        out_specs=[pl.BlockSpec(memory_space=pltpu.VMEM)] * 2,
        out_shape=[jax.ShapeDtypeStruct((L, D), BF16), jax.ShapeDtypeStruct((16, L), F32)],
        scratch_shapes=[
            pltpu.VMEM((D, L), BF16),
            pltpu.VMEM((PAIRS, 2 * BLK, BLK), BF16),
            pltpu.VMEM((PAIRS, BLK, BLK), F32),
            pltpu.VMEM((PAIRS, 8, 2 * BLK), F32),
            pltpu.VMEM((PAIRS, 8, 2 * BLK), F32),
        ],
        compiler_params=params(),
        cost_estimate=pl.CostEstimate(flops=4 * L * L * D, bytes_accessed=8_000_000, transcendentals=0),
        name="attend",
    )(lengths, qkv)


def attend_back_kernel(len_ref, qkv_ref, o_ref, go_ref, lse_ref, g_ref, sums_ref, kt, qm, gm, stat, dq, dk, dv):
    bounds = bounds_of(len_ref)
    for p in range(PAIRS):
        kt[p * BLK:(p + 1) * BLK, :] = qkv_ref[:, D + p * BLK:D + (p + 1) * BLK].T
    dk[...] = jnp.zeros_like(dk)
    dv[...] = jnp.zeros_like(dv)
    sums_ref[...] = jnp.zeros_like(sums_ref)

    def query_step(block, carry):
        at = pl.multiple_of(block * BLK, BLK)
        first, last = block_range(bounds, block)
        for p in range(PAIRS):
            cols = slice(p * BLK, (p + 1) * BLK)
            qm[p] = split_pair(qkv_ref[pl.ds(at, BLK), cols])
            grads = go_ref[pl.ds(at, BLK), cols]
            gm[p] = split_pair(grads)
            prod = (grads.astype(F32) * o_ref[pl.ds(at, BLK), cols].astype(F32)).T
            stat[p, 0:1, :BLK] = lse_ref[2 * p:2 * p + 1, pl.ds(at, BLK)]
            stat[p, 0:1, BLK:] = lse_ref[2 * p + 1:2 * p + 2, pl.ds(at, BLK)]
            stat[p, 1:2, :BLK] = jnp.sum(prod[:HD], axis=0, keepdims=True)
            stat[p, 1:2, BLK:] = jnp.sum(prod[HD:], axis=0, keepdims=True)
        dq[...] = jnp.zeros_like(dq)

        def key_step(key_block, carry):
            key_at = pl.multiple_of(key_block * BLK, BLK)
            hidden = hide(bounds, key_block, block)
            for p in range(PAIRS):
                cols = slice(p * BLK, (p + 1) * BLK)
                keys = qkv_ref[pl.ds(key_at, BLK), D + p * BLK:D + (p + 1) * BLK]
                vals = qkv_ref[pl.ds(key_at, BLK), 2 * D + p * BLK:2 * D + (p + 1) * BLK]
                soft = jnp.exp(dot_nt(keys, qm[p]) + (hidden - stat[p, 0:1, :]))
                grad_soft = dot_nt(vals, gm[p])
                grad_scores = (soft * (grad_soft - stat[p, 1:2, :])).astype(BF16)
                dv[pl.ds(key_at, BLK), cols] += dot_nn(soft.astype(BF16), gm[p])
                dk[pl.ds(key_at, BLK), cols] += dot_nn(grad_scores, qm[p])
                for side in range(2):
                    rows = slice(side * HD, (side + 1) * HD)
                    kside = kt[p * BLK + side * HD:p * BLK + (side + 1) * HD, pl.ds(key_at, BLK)]
                    dq[p, rows, :] += dot_nn(kside, grad_scores[:, side * BLK:(side + 1) * BLK])
            return carry

        lax.fori_loop(first, last, key_step, 0)
        for p in range(PAIRS):
            cols = slice(p * BLK, (p + 1) * BLK)
            done = (dq[p] * SCALE).T.astype(BF16)
            g_ref[pl.ds(at, BLK), cols] = done
            sums_ref[0:1, cols] += jnp.sum(done.astype(F32), axis=0, keepdims=True)
        return carry

    lax.fori_loop(0, L // BLK, query_step, 0)
    g_ref[:, D:2 * D] = dk[...].astype(BF16)
    gv = dv[...].astype(BF16)
    g_ref[:, 2 * D:] = gv
    sums_ref[1:2, :] = jnp.sum(gv.astype(F32), axis=0, keepdims=True)


def attend_back_call(lengths, qkv, o, go, lse):
    return pl.pallas_call(
        attend_back_kernel,
        in_specs=[smem()] + [pl.BlockSpec(memory_space=pltpu.VMEM)] * 4,
        out_specs=[pl.BlockSpec(memory_space=pltpu.VMEM)] * 2,
        out_shape=[jax.ShapeDtypeStruct((L, 3 * D), BF16), jax.ShapeDtypeStruct((8, D), F32)],
        scratch_shapes=[
            pltpu.VMEM((D, L), BF16),
            pltpu.VMEM((PAIRS, 2 * BLK, BLK), BF16),
            pltpu.VMEM((PAIRS, 2 * BLK, BLK), BF16),
            pltpu.VMEM((PAIRS, 8, 2 * BLK), F32),
            pltpu.VMEM((PAIRS, BLK, BLK), F32),
            pltpu.VMEM((L, D), F32),
            pltpu.VMEM((L, D), F32),
        ],
        compiler_params=params(),
        cost_estimate=pl.CostEstimate(flops=10 * L * L * D, bytes_accessed=15_000_000, transcendentals=0),
        name="attend_back",
    )(lengths, qkv, o, go, lse)


def up_kernel(o_ref, x_ref, vec_ref, wo_ref, wu_ref, bu_ref, mid_ref, n2_ref, a_ref, slope_ref):
    middle = x_ref[...].astype(F32) + (dot_nn(o_ref[...], wo_ref[...]) + vec_ref[6:7, :])
    mid_ref[...] = middle
    hat, _ = norm_parts(middle)
    n2 = (hat * (1.0 + vec_ref[2:3, :]) + vec_ref[3:4, :]).astype(BF16)
    n2_ref[...] = n2
    width = 512
    for c in range(FF // width):
        cols = slice(c * width, (c + 1) * width)
        h = dot_nn(n2, wu_ref[:, cols]) + bu_ref[:, cols]
        act, slope = gate_pair(h)
        a_ref[:, cols] = act.astype(BF16)
        slope_ref[:, cols] = slope.astype(BF16)


def up_call(o, x, vec, wo, wu, bu):
    return pl.pallas_call(
        up_kernel,
        grid=(TILES,),
        in_specs=[rows_of(D), rows_of(D), whole(vec.shape), whole(wo.shape), whole(wu.shape), whole(bu.shape)],
        out_specs=[rows_of(D), rows_of(D), rows_of(FF), rows_of(FF)],
        out_shape=[
            jax.ShapeDtypeStruct((L, D), F32),
            jax.ShapeDtypeStruct((L, D), BF16),
            jax.ShapeDtypeStruct((L, FF), BF16),
            jax.ShapeDtypeStruct((L, FF), BF16),
        ],
        compiler_params=params(),
        cost_estimate=pl.CostEstimate(flops=2 * L * D * (FF + D), bytes_accessed=25_000_000, transcendentals=2 * L * FF),
        name="feed_up",
    )(o, x, vec, wo, wu, bu)


def down_kernel(a_ref, mid_ref, vec_ref, wdt_ref, y_ref):
    y_ref[...] = (mid_ref[...] + (dot_nt(a_ref[...], wdt_ref[...]) + vec_ref[7:8, :])).astype(BF16)


def down_call(a, middle, vec, wdt):
    return pl.pallas_call(
        down_kernel,
        grid=(TILES,),
        in_specs=[rows_of(FF), rows_of(D), whole(vec.shape), whole(wdt.shape)],
        out_specs=rows_of(D),
        out_shape=jax.ShapeDtypeStruct((L, D), BF16),
        compiler_params=params(),
        cost_estimate=pl.CostEstimate(flops=2 * L * D * FF, bytes_accessed=17_000_000, transcendentals=0),
        name="feed_down",
    )(a, middle, vec, wdt)


def feed_back_kernel(gy_ref, slope_ref, mid_ref, vec_ref, wdt_ref, wu_ref, wo_ref,
                     gh_ref, gmid_ref, gatt_ref, go_ref, sums_ref, bup_ref):
    @pl.when(pl.program_id(0) == 0)
    def _():
        sums_ref[...] = jnp.zeros_like(sums_ref)
        bup_ref[...] = jnp.zeros_like(bup_ref)

    gm = gy_ref[...]
    gy = gm.astype(F32)
    width = 768
    gn2 = None
    for c in range(FF // width):
        cols = slice(c * width, (c + 1) * width)
        ga = dot_nn(gm, wdt_ref[:, cols])
        gh = (ga * slope_ref[:, cols].astype(F32)).astype(BF16)
        gh_ref[:, cols] = gh
        bup_ref[0:1, cols] += jnp.sum(gh.astype(F32), axis=0, keepdims=True)
        part = dot_nt(gh, wu_ref[:, cols])
        gn2 = part if gn2 is None else gn2 + part
    hat, inv = norm_parts(mid_ref[...])
    sums_ref[0:1, :] += jnp.sum(gn2 * hat, axis=0, keepdims=True)
    sums_ref[1:2, :] += jnp.sum(gn2, axis=0, keepdims=True)
    gmid = gy + norm_back(gn2, hat, inv, vec_ref[2:3, :])
    gmid_ref[...] = gmid
    gatt = gmid.astype(BF16)
    gatt_ref[...] = gatt
    sums_ref[2:3, :] += jnp.sum(gatt.astype(F32), axis=0, keepdims=True)
    sums_ref[3:4, :] += jnp.sum(gy, axis=0, keepdims=True)
    go_ref[...] = dot_nt(gatt, wo_ref[...]).astype(BF16)


def feed_back_call(gy, slope, middle, vec, wdt, wu, wo):
    return pl.pallas_call(
        feed_back_kernel,
        grid=(TILES,),
        in_specs=[rows_of(D), rows_of(FF), rows_of(D), whole(vec.shape), whole(wdt.shape), whole(wu.shape), whole(wo.shape)],
        out_specs=[rows_of(FF), rows_of(D), rows_of(D), rows_of(D), whole((8, D)), whole((8, FF))],
        out_shape=[
            jax.ShapeDtypeStruct((L, FF), BF16),
            jax.ShapeDtypeStruct((L, D), F32),
            jax.ShapeDtypeStruct((L, D), BF16),
            jax.ShapeDtypeStruct((L, D), BF16),
            jax.ShapeDtypeStruct((8, D), F32),
            jax.ShapeDtypeStruct((8, FF), F32),
        ],
        compiler_params=params(),
        cost_estimate=pl.CostEstimate(flops=2 * L * D * (2 * FF + D), bytes_accessed=35_000_000, transcendentals=0),
        name="feed_back",
    )(gy, slope, middle, vec, wdt, wu, wo)


def outer_kernel(left_ref, right_ref, out_ref, turned):
    @pl.when(pl.program_id(0) == 0)
    def _():
        turned[...] = left_ref[...].T

    out_ref[...] = dot_nn(turned[...], right_ref[...]).astype(BF16)


def outer_call(left, right, name):
    wide = right.shape[1]
    width = 768
    return pl.pallas_call(
        outer_kernel,
        grid=(wide // width,),
        in_specs=[whole(left.shape), pl.BlockSpec((L, width), lambda i: (0, i))],
        out_specs=pl.BlockSpec((D, width), lambda i: (0, i)),
        out_shape=jax.ShapeDtypeStruct((D, wide), BF16),
        scratch_shapes=[pltpu.VMEM((D, L), BF16)],
        compiler_params=params(),
        cost_estimate=pl.CostEstimate(flops=2 * L * D * wide, bytes_accessed=4 * L * D + 4 * D * wide, transcendentals=0),
        name=name,
    )(left, right)


def first_back_kernel(len_ref, lead_ref, x_ref, gmid_ref, g_ref, vec_ref, w_ref, out_ref, sums_ref, table_ref):
    step = pl.program_id(0)

    @pl.when(step == 0)
    def _():
        sums_ref[...] = jnp.zeros_like(sums_ref)
        table_ref[...] = jnp.zeros_like(table_ref)

    gn1 = dot_nt(g_ref[...], w_ref[...])
    hat, inv = norm_parts(x_ref[...].astype(F32))
    sums_ref[0:1, :] += jnp.sum(gn1 * hat, axis=0, keepdims=True)
    sums_ref[1:2, :] += jnp.sum(gn1, axis=0, keepdims=True)
    shape = (table_ref.shape[0], ROWS)
    places = step * ROWS + lax.broadcasted_iota(jnp.int32, shape, 1)
    hot = lead_of(places, bounds_of(len_ref), lead_ref) == lax.broadcasted_iota(jnp.int32, shape, 0)
    hot = hot.astype(BF16)
    high = gn1.astype(BF16)
    low = (gn1 - high.astype(F32)).astype(BF16)
    table_ref[...] += dot_nn(hot, high) + dot_nn(hot, low)
    out_ref[...] = gmid_ref[...] + norm_back(gn1, hat, inv, vec_ref[0:1, :])


def first_back_call(lengths, leads, x, gmid, gqkv, vec, w):
    return pl.pallas_call(
        first_back_kernel,
        grid=(TILES,),
        in_specs=[smem(), smem(), rows_of(D), rows_of(D), rows_of(3 * D), whole(vec.shape), whole(w.shape)],
        out_specs=[rows_of(D), whole((8, D)), whole((32, D))],
        out_shape=[
            jax.ShapeDtypeStruct((L, D), F32),
            jax.ShapeDtypeStruct((8, D), F32),
            jax.ShapeDtypeStruct((32, D), F32),
        ],
        compiler_params=params(),
        cost_estimate=pl.CostEstimate(flops=2 * L * D * 3 * D, bytes_accessed=17_000_000, transcendentals=0),
        name="first_back",
    )(lengths, leads, x, gmid, gqkv, vec, w)


def slots(found):
    return [
        (at, k, dp, fs + 2 * k)
        for at, (dp, fs, part) in enumerate(found)
        for k in range(part.shape[0])
    ]

def chunk_cols(chunk, wide):
    third = wide // 3
    return (2 * third, third) if chunk == 0 else (0, 2 * third)


def any_space():
    return pl.BlockSpec(memory_space=pl.ANY)


def in_vmem():
    return pl.BlockSpec(memory_space=pltpu.VMEM)


def kept(shape):
    return pl.BlockSpec(shape, lambda *_: (0,) * len(shape), pipeline_mode=pl.Buffered(1))


def pack_first(w_qkv, small):
    tall, cols = w_qkv.shape
    left = cols - 256
    fold = 128 // left
    rows = tall // fold
    rest = jnp.concatenate([w_qkv[k * rows:(k + 1) * rows, 256:] for k in range(fold)], axis=1)
    small = jnp.pad(small, ((0, 16 - small.shape[0]), (0, 128 - small.shape[1])))
    return jnp.concatenate([w_qkv[:, :128], w_qkv[:, 128:256], rest, small], axis=0)


def pack_chunk(chunk, w_up, w_down_t):
    wide = w_up.shape[1]
    start, count = chunk_cols(chunk, wide)
    parts = [w_up[:, start:start + count]]
    for k in range(w_down_t.shape[1] // wide):
        parts.append(w_down_t[:, k * wide + start:k * wide + start + count])
    return jnp.concatenate(parts, axis=0)


def fold_out(w_out):
    tall, narrow = w_out.shape
    rows = tall // 4
    wide = jnp.concatenate([w_out[k * rows:(k + 1) * rows] for k in range(4)], axis=1)
    return jnp.concatenate([wide[:, k * 128:(k + 1) * 128] for k in range(4 * narrow // 128)], axis=0)


def start_all(copies):
    for copy in copies:
        copy.start()
    for copy in copies:
        copy.wait()


def open_kernel(plan, count, ids_ref, len_ref, lead_ref, x_ref, *refs):
    parts = refs[:count]
    n1_ref, qkv_ref, w_ref, vec_ref, table_ref, bias0_ref, bias1_ref, stage, table, bias, sem = refs[count:]
    step = pl.program_id(0)
    dps, fss = stage.shape[0], stage.shape[1]
    tall, cols, narrow, wide = D // dps, 3 * D // fss, D // fss, FF // fss

    @pl.when(step == 0)
    def _():
        start_all([
            pltpu.make_async_copy(parts[at].at[k], stage.at[ids_ref[0] ^ dp, ids_ref[1] ^ fs], sem)
            for at, k, dp, fs in plan
        ])
        table[...] = jnp.zeros_like(table)
        left = cols - 256
        fold = 128 // left
        rows = tall // fold
        for d in range(dps):
            for f in range(fss):
                at = slice(d * tall, (d + 1) * tall)
                w_ref[at, f * cols:f * cols + 128] = stage[d, f, :tall]
                w_ref[at, f * cols + 128:f * cols + 256] = stage[d, f, tall:2 * tall]
                for k in range(fold):
                    w_ref[d * tall + k * rows:d * tall + (k + 1) * rows, f * cols + 256:(f + 1) * cols] = (
                        stage[d, f, 2 * tall:2 * tall + rows, k * left:(k + 1) * left]
                    )
                small = stage[d, f, 2 * tall + rows:, :narrow].astype(F32)
                at = slice(f * narrow, (f + 1) * narrow)
                vec_ref[2 * d:2 * d + 2, at] = small[0:2]
                table[5 * d:5 * d + 5, at] = small[2:7]
                bias[0:1, d * D + f * narrow:d * D + (f + 1) * narrow] = small[7:8]
        table_ref[...] = table[...].astype(BF16)
        for chunk, ref in ((0, bias0_ref), (1, bias1_ref)):
            start, many = chunk_cols(chunk, wide)
            for f in range(fss):
                ref[:, f * many:(f + 1) * many] = bias[:, f * wide + start:f * wide + start + many]

    qkv_tile(step, len_ref, lead_ref, x_ref, vec_ref, table_ref, w_ref, n1_ref, qkv_ref)


def qkv_tile(step, len_ref, lead_ref, x_ref, vec_ref, table_ref, w_ref, n1_ref, qkv_ref):
    bounds = bounds_of(len_ref)
    hat, _ = norm_parts(x_ref[...].astype(F32))
    normed = hat * (1.0 + vec_ref[0:1, :]) + vec_ref[1:2, :]
    shape = (ROWS, table_ref.shape[0])
    places = step * ROWS + lax.broadcasted_iota(jnp.int32, shape, 0)
    hot = lead_of(places, bounds, lead_ref) == lax.broadcasted_iota(jnp.int32, shape, 1)
    n1 = (normed + dot_nn(hot.astype(BF16), table_ref[...])).astype(BF16)
    n1_ref[...] = n1
    for third in range(3):
        cols = slice(third * D, (third + 1) * D)
        part = dot_nn(n1, w_ref[:, cols])
        if third == 0:
            part = (part + vec_ref[4:5, :]).astype(BF16) * jnp.asarray(SCALE, BF16)
        elif third == 2:
            part = part + vec_ref[5:6, :]
        qkv_ref[:, cols] = part.astype(BF16)


def open_call(found, ids, lengths, leads, x, sizes):
    parts = [part for _, _, part in found]
    rows = parts[0].shape[1]
    dps, fss = sizes
    sides = [fss * chunk_cols(chunk, FF // fss)[1] for chunk in range(2)]
    shapes = [((L, D), BF16), ((L, 3 * D), BF16), ((D, 3 * D), BF16), ((8, D), F32), ((32, D), BF16)]
    shapes += [((1, side), F32) for side in sides]
    return pl.pallas_call(
        functools.partial(open_kernel, slots(found), len(parts)),
        grid=(TILES,),
        in_specs=[smem(), smem(), smem(), rows_of(D)] + [any_space()] * len(parts),
        out_specs=[rows_of(D), rows_of(3 * D)] + [kept(shape) for shape, _ in shapes[2:]],
        out_shape=[jax.ShapeDtypeStruct(shape, kind) for shape, kind in shapes],
        scratch_shapes=[
            pltpu.VMEM((dps, fss, rows, 128), BF16),
            pltpu.VMEM((32, D), F32),
            pltpu.VMEM((1, FF), F32),
            pltpu.SemaphoreType.DMA,
        ],
        compiler_params=params(),
        cost_estimate=pl.CostEstimate(flops=2 * L * D * 3 * D, bytes_accessed=18_000_000, transcendentals=0),
        name="open",
    )(ids, lengths, leads, x, *parts)


def lay_chunk(plan, ids_ref, parts, wu, wd, wo, stage, sem, sizes):
    dps, fss = sizes
    tall, thin = D // dps, D // fss
    many = wu.shape[1] // fss
    copies = []
    for at, k, dp, fs in plan:
        d, f = ids_ref[0] ^ dp, ids_ref[1] ^ fs
        part = parts[at]

        def place(ref, row, rows, col):
            return ref.at[pl.ds(pl.multiple_of(row, 16), rows), pl.ds(pl.multiple_of(col, 128), many)]

        copies.append(pltpu.make_async_copy(part.at[k, pl.ds(0, tall), :], place(wu, d * tall, tall, f * many), sem))
        for side in range(fss // dps):
            rows = part.at[k, pl.ds(tall + side * thin, thin), :]
            copies.append(pltpu.make_async_copy(rows, place(wd, f * thin, thin, (d * (fss // dps) + side) * many), sem))
        if wo is not None:
            rows = part.at[k, pl.ds(tall + fss // dps * thin, stage.shape[2]), :]
            copies.append(pltpu.make_async_copy(rows, stage.at[d, f], sem))
    start_all(copies)
    if wo is None:
        return
    rows = tall // 4
    for d in range(dps):
        for f in range(fss):
            flat = jnp.concatenate([stage[d, f, k * rows:(k + 1) * rows] for k in range(thin * 4 // 128)], axis=1)
            for k in range(4):
                wo[d * tall + k * rows:d * tall + (k + 1) * rows, f * thin:(f + 1) * thin] = flat[:, k * thin:(k + 1) * thin]


def turn(ref, plain, ordered, mine, count):
    plain[...] = ref[...].T
    tall = ordered.shape[0] // count
    for k in range(count):
        at = pl.multiple_of((mine ^ k) * tall, tall)
        ordered[k * tall:(k + 1) * tall, :] = plain[pl.ds(at, tall), :]


def gate_pair(h):
    cdf = 0.5 + 0.5 * lax.erf(h * 0.7071067811865476)
    return h * cdf, cdf + h * (0.3989422804014327 * jnp.exp(h * h * -0.5))


def norm_back(grad, hat, inv, gain):
    scaled = grad * (1.0 + gain)
    both = jnp.mean(scaled * hat, axis=-1, keepdims=True)
    return inv * (scaled - jnp.mean(scaled, axis=-1, keepdims=True) - hat * both)


def feed_step(step, gm_ref, n2, n2_t, gm_t, wu, wd, bias, a_ref, bup_ref, gh, gn2, grads, ids_ref, sizes):
    dps, fss = sizes
    pair = fss // dps
    width = a_ref.shape[1]
    many = width // pair
    tall, thin = D // dps, D // fss
    block = step ^ (ids_ref[1] // pair)
    cols = pl.ds(pl.multiple_of(block * width, width), width)
    own_u, own_d = wu[:, cols], wd[:, cols]
    shift = bias[:, cols]
    bup = jnp.zeros((1, width), F32)
    for r in range(TILES):
        rows = slice(r * ROWS, (r + 1) * ROWS)
        act, slope = gate_pair(dot_nn(n2[rows, :], own_u) + shift)
        a_ref[rows, :] = act.astype(BF16)
        part = (dot_nn(gm_ref[rows, :], own_d) * slope).astype(BF16)
        gh[rows, :] = part
        bup = bup + jnp.sum(part.astype(F32), axis=0, keepdims=True)
        gn2[rows, :] += dot_nt(part, own_u)
    bup_ref[:, cols] = bup
    grad = dot_nn(gm_t[...], a_ref[...]).astype(BF16)
    d = block ^ ids_ref[0]
    for f in range(fss):
        for side in range(pair):
            at = tall + side * thin
            grads[d & 1, d >> 1, f & 1, f >> 1, at:at + thin, :] = grad[f * thin:(f + 1) * thin, side * many:(side + 1) * many]
    grad = dot_nn(n2_t[...], gh[...]).astype(BF16)
    for side in range(pair):
        y = (ids_ref[1] & 1) ^ side
        for d in range(dps):
            grads[d & 1, d >> 1, y, step, :tall, :] = grad[d * tall:(d + 1) * tall, side * many:(side + 1) * many]


def feed_first_kernel(plan, count, sizes, ids_ref, o_ref, x_ref, gm_ref, vec_ref, bias_ref, *refs):
    parts = refs[:count]
    (a_ref, bup_ref, mid_ref, n2_ref, gn2_ref, wd_ref, wo_ref, mine_ref, theirs_ref,
     wu, stage, plain, n2_t, gm_t, gh, grads, sem) = refs[count:]
    step = pl.program_id(0)

    @pl.when(step == 0)
    def _():
        lay_chunk(plan, ids_ref, parts, wu, wd_ref, wo_ref, stage, sem, sizes)
        turn(gm_ref, plain, gm_t, ids_ref[1], sizes[1])
        for r in range(TILES):
            rows = slice(r * ROWS, (r + 1) * ROWS)
            middle = x_ref[rows, :].astype(F32) + (dot_nn(o_ref[rows, :], wo_ref[...]) + vec_ref[6:7, :])
            mid_ref[rows, :] = middle
            hat, _ = norm_parts(middle)
            n2_ref[rows, :] = (hat * (1.0 + vec_ref[2:3, :]) + vec_ref[3:4, :]).astype(BF16)
        turn(n2_ref, plain, n2_t, ids_ref[0], sizes[0])
        gn2_ref[...] = jnp.zeros_like(gn2_ref)

    feed_step(step, gm_ref, n2_ref, n2_t, gm_t, wu, wd_ref, bias_ref, a_ref, bup_ref, gh, gn2_ref, grads, ids_ref, sizes)

    @pl.when(step == pl.num_programs(0) - 1)
    def _():
        start_all([
            pltpu.make_async_copy(grads.at[0], mine_ref, sem),
            pltpu.make_async_copy(grads.at[1], theirs_ref, sem),
        ])


def feed_first(found, ids, o, x, gm, vec, bias, sizes):
    parts = [part for _, _, part in found]
    dps, fss = sizes
    units = bias.shape[1]
    width, many = units // dps, units // fss
    rows = 2 * (D // dps)
    shape = (dps // 2, 2, fss // 2, rows, many)
    outs = [
        ((L, units), BF16), ((1, units), F32), ((L, D), F32), ((L, D), BF16), ((L, D), F32), ((D, units), BF16), ((D, D), BF16),
        (shape, BF16), (shape, BF16),
    ]
    return pl.pallas_call(
        functools.partial(feed_first_kernel, slots(found), len(parts), sizes),
        grid_spec=pltpu.PrefetchScalarGridSpec(
            num_scalar_prefetch=1,
            grid=(dps,),
            in_specs=[kept((L, D)), kept((L, D)), kept((L, D)), kept((8, D)), kept((1, units))] + [any_space()] * len(parts),
            out_specs=[pl.BlockSpec((L, width), lambda i, ids: (0, i ^ (ids[1] // (fss // dps))))]
            + [kept(s) for s, _ in outs[1:7]] + [any_space()] * 2,
            scratch_shapes=[
                pltpu.VMEM((D, units), BF16),
                pltpu.VMEM((dps, fss, parts[0].shape[1] - rows, 128), BF16),
                pltpu.VMEM((D, L), BF16),
                pltpu.VMEM((D, L), BF16),
                pltpu.VMEM((D, L), BF16),
                pltpu.VMEM((L, width), BF16),
                pltpu.VMEM((2,) + shape, BF16),
                pltpu.SemaphoreType.DMA,
            ],
        ),
        out_shape=[jax.ShapeDtypeStruct(s, kind) for s, kind in outs],
        compiler_params=params(),
        cost_estimate=pl.CostEstimate(flops=2 * L * D * (5 * units + D), bytes_accessed=30_000_000, transcendentals=2 * L * units),
        name="feed_first",
    )(ids, o, x, gm, vec, bias, *parts)


def feed_second_kernel(plan, count, sizes, ids_ref, o_ref, n2_ref, gm_ref, mid_ref, gn2_in_ref, vec_ref, bias_ref, wo_ref, *refs):
    parts = refs[:count]
    (a_ref, bup_ref, wd_ref, gmid_ref, go_ref, sums_ref, mine_ref, theirs_ref,
     wu, plain, n2_t, gm_t, gh, gn2, gatt, full, grads, sem) = refs[count:]
    step = pl.program_id(0)
    dps, fss = sizes

    @pl.when(step == 0)
    def _():
        lay_chunk(plan, ids_ref, parts, wu, wd_ref, None, None, sem, sizes)
        turn(gm_ref, plain, gm_t, ids_ref[1], fss)
        turn(n2_ref, plain, n2_t, ids_ref[0], dps)
        gn2[...] = gn2_in_ref[...]

    feed_step(step, gm_ref, n2_ref, n2_t, gm_t, wu, wd_ref, bias_ref, a_ref, bup_ref, gh, gn2, grads, ids_ref, sizes)

    @pl.when(step == pl.num_programs(0) - 1)
    def _():
        turn(o_ref, plain, n2_t, ids_ref[0], dps)
        sums = [jnp.zeros((1, D), F32)] * 4
        for r in range(TILES):
            rows = slice(r * ROWS, (r + 1) * ROWS)
            grad, gy = gn2[rows, :], gm_ref[rows, :].astype(F32)
            hat, inv = norm_parts(mid_ref[rows, :])
            gmid = gy + norm_back(grad, hat, inv, vec_ref[2:3, :])
            gmid_ref[rows, :] = gmid
            low = gmid.astype(BF16)
            gatt[rows, :] = low
            go_ref[rows, :] = dot_nt(low, wo_ref[...]).astype(BF16)
            for k, term in enumerate((grad * hat, grad, low.astype(F32), gy)):
                sums[k] = sums[k] + jnp.sum(term, axis=0, keepdims=True)
        sums_ref[...] = jnp.concatenate(sums + [jnp.zeros((4, D), F32)], axis=0)
        full[...] = dot_nn(n2_t[...], gatt[...]).astype(BF16)
        tall, thin = D // dps, D // fss
        for f in range(fss):
            flip = ids_ref[1] ^ f
            for d in range(dps):
                for k in range(2):
                    at = 2 * tall
                    grads[d & 1, d >> 1, flip & 1, flip >> 1, at:at + tall // 2, k * thin:(k + 1) * thin] = (
                        full[d * tall + k * (tall // 2):d * tall + (k + 1) * (tall // 2), f * thin:(f + 1) * thin]
                    )
                grads[d & 1, d >> 1, flip & 1, flip >> 1, 2 * tall:, 2 * thin:] = jnp.zeros(
                    (tall // 2, grads.shape[5] - 2 * thin), BF16
                )
        start_all([
            pltpu.make_async_copy(grads.at[0], mine_ref, sem),
            pltpu.make_async_copy(grads.at[1], theirs_ref, sem),
        ])


def feed_second(found, ids, o, n2, gm, mid, gn2, vec, bias, wo, sizes):
    parts = [part for _, _, part in found]
    dps, fss = sizes
    units = bias.shape[1]
    width, many = units // dps, units // fss
    tall = D // dps
    shape = (dps // 2, 2, fss // 2, 2 * tall + tall // 2, many)
    outs = [
        ((L, units), BF16), ((1, units), F32), ((D, units), BF16), ((L, D), F32), ((L, D), BF16), ((8, D), F32),
        (shape, BF16), (shape, BF16),
    ]
    ins = [(L, D)] * 5 + [(8, D), (1, units), (D, D)]
    return pl.pallas_call(
        functools.partial(feed_second_kernel, slots(found), len(parts), sizes),
        grid_spec=pltpu.PrefetchScalarGridSpec(
            num_scalar_prefetch=1,
            grid=(dps,),
            in_specs=[kept(s) for s in ins] + [any_space()] * len(parts),
            out_specs=[pl.BlockSpec((L, width), lambda i, ids: (0, i ^ (ids[1] // (fss // dps))))]
            + [kept(s) for s, _ in outs[1:6]] + [any_space()] * 2,
            scratch_shapes=[
                pltpu.VMEM((D, units), BF16),
                pltpu.VMEM((D, L), BF16),
                pltpu.VMEM((D, L), BF16),
                pltpu.VMEM((D, L), BF16),
                pltpu.VMEM((L, width), BF16),
                pltpu.VMEM((L, D), F32),
                pltpu.VMEM((L, D), BF16),
                pltpu.VMEM((D, D), BF16),
                pltpu.VMEM((2,) + shape, BF16),
                pltpu.SemaphoreType.DMA,
            ],
        ),
        out_shape=[jax.ShapeDtypeStruct(s, kind) for s, kind in outs],
        compiler_params=params(58 * 1024 * 1024),
        cost_estimate=pl.CostEstimate(flops=2 * L * D * (5 * units + 2 * D), bytes_accessed=35_000_000, transcendentals=2 * L * units),
        name="feed_second",
    )(ids, o, n2, gm, mid, gn2, vec, bias, wo, *parts)


def last_kernel(a0_ref, a1_ref, mid_ref, vec_ref, w0_ref, w1_ref, y_ref):
    total = dot_nt(a0_ref[...], w0_ref[...]) + dot_nt(a1_ref[...], w1_ref[...])
    y_ref[...] = (mid_ref[...] + (total + vec_ref[7:8, :])).astype(BF16)


def last_call(a0, a1, middle, vec, w0, w1):
    return pl.pallas_call(
        last_kernel,
        grid=(TILES,),
        in_specs=[rows_of(a0.shape[1]), rows_of(a1.shape[1]), rows_of(D), kept((8, D)), kept(w0.shape), kept(w1.shape)],
        out_specs=rows_of(D),
        out_shape=jax.ShapeDtypeStruct((L, D), BF16),
        compiler_params=params(),
        cost_estimate=pl.CostEstimate(flops=2 * L * D * FF, bytes_accessed=17_000_000, transcendentals=0),
        name="feed_down",
    )(a0, a1, middle, vec, w0, w1)


def close_kernel(sizes, ids_ref, len_ref, lead_ref, x_ref, gmid_ref, n1_ref, g_ref, vec_ref, w_ref, sums_ref, qsums_ref,
                 bup0_ref, bup1_ref, out_ref, mine_ref, theirs_ref, plain, left, full, gvec, table, bup, grads, sem):
    dps, fss = sizes
    step = pl.program_id(0)
    tall, cols, thin, wide = D // dps, 3 * D // fss, D // fss, FF // fss

    @pl.when(step == 0)
    def _():
        turn(n1_ref, plain, left, ids_ref[0], dps)
        table[...] = jnp.zeros_like(table)
        gvec[0:2, :] = jnp.zeros((2, D), F32)
        gvec[2:4, :] = sums_ref[0:2, :]
        gvec[4:6, :] = qsums_ref[0:2, :]
        gvec[6:8, :] = sums_ref[2:4, :]
        for chunk, ref in ((0, bup0_ref), (1, bup1_ref)):
            start, many = chunk_cols(chunk, wide)
            for f in range(fss):
                bup[:, f * wide + start:f * wide + start + many] = ref[:, f * many:(f + 1) * many]

    rows = pl.ds(pl.multiple_of(step * ROWS, ROWS), ROWS)
    grad = dot_nt(g_ref[rows, :], w_ref[...])
    hat, inv = norm_parts(x_ref[...].astype(F32))
    gvec[0:1, :] += jnp.sum(grad * hat, axis=0, keepdims=True)
    gvec[1:2, :] += jnp.sum(grad, axis=0, keepdims=True)
    shape = (table.shape[0], ROWS)
    places = step * ROWS + lax.broadcasted_iota(jnp.int32, shape, 1)
    hot = lead_of(places, bounds_of(len_ref), lead_ref) == lax.broadcasted_iota(jnp.int32, shape, 0)
    hot = hot.astype(BF16)
    high = grad.astype(BF16)
    low = (grad - high.astype(F32)).astype(BF16)
    table[...] += dot_nn(hot, high) + dot_nn(hot, low)
    out_ref[...] = gmid_ref[...] + norm_back(grad, hat, inv, vec_ref[0:1, :])

    @pl.when(step < 3)
    def _():
        at = pl.ds(pl.multiple_of(step * D, D), D)
        full[:, at] = dot_nn(left[...], g_ref[:, at]).astype(BF16)

    @pl.when(step == pl.num_programs(0) - 1)
    def _():
        rest = cols - 256
        fold = 128 // rest
        some = tall // fold
        for f in range(fss):
            flip = ids_ref[1] ^ f
            y, z = flip & 1, flip >> 1
            for d in range(dps):
                c, x = d & 1, d >> 1
                own = slice(d * tall, (d + 1) * tall)
                grads[c, x, y, z, 0:tall, :] = full[own, f * cols:f * cols + 128]
                grads[c, x, y, z, tall:2 * tall, :] = full[own, f * cols + 128:f * cols + 256]
                for k in range(fold):
                    grads[c, x, y, z, 2 * tall:2 * tall + some, k * rest:(k + 1) * rest] = (
                        full[d * tall + k * some:d * tall + (k + 1) * some, f * cols + 256:(f + 1) * cols]
                    )
                at = slice(f * thin, (f + 1) * thin)
                small = jnp.concatenate([
                    gvec[2 * d:2 * d + 2, at],
                    table[5 * d:5 * d + 5, at],
                    bup[0:1, d * D + f * thin:d * D + (f + 1) * thin],
                    jnp.zeros((8, thin), F32),
                ], axis=0)
                small = jnp.concatenate([small, jnp.zeros((16, 128 - thin), F32)], axis=1).astype(BF16)
                away = ids_ref[0] ^ d
                grads[away & 1, away >> 1, y, z, 2 * tall + some:, :] = small
        start_all([
            pltpu.make_async_copy(grads.at[0], mine_ref, sem),
            pltpu.make_async_copy(grads.at[1], theirs_ref, sem),
        ])


def close_call(ids, lengths, leads, x, gmid, n1, gqkv, vec, w, sums, qsums, bup0, bup1, sizes):
    dps, fss = sizes
    tall = D // dps
    rows = 2 * tall + tall // (128 // (3 * D // fss - 256)) + 16
    shape = (dps // 2, 2, fss // 2, rows, 128)
    return pl.pallas_call(
        functools.partial(close_kernel, sizes),
        grid=(TILES,),
        in_specs=[smem()] * 3 + [rows_of(D), rows_of(D), kept((L, D)), kept((L, 3 * D)), kept((8, D)), kept((D, 3 * D)),
                                 kept((8, D)), kept((8, D)), kept(bup0.shape), kept(bup1.shape)],
        out_specs=[rows_of(D), any_space(), any_space()],
        out_shape=[jax.ShapeDtypeStruct((L, D), F32), jax.ShapeDtypeStruct(shape, BF16), jax.ShapeDtypeStruct(shape, BF16)],
        scratch_shapes=[
            pltpu.VMEM((D, L), BF16),
            pltpu.VMEM((D, L), BF16),
            pltpu.VMEM((D, 3 * D), BF16),
            pltpu.VMEM((8, D), F32),
            pltpu.VMEM((32, D), F32),
            pltpu.VMEM((1, FF), F32),
            pltpu.VMEM((2,) + shape, BF16),
            pltpu.SemaphoreType.DMA,
        ],
        compiler_params=params(),
        cost_estimate=pl.CostEstimate(flops=4 * L * D * 3 * D, bytes_accessed=25_000_000, transcendentals=0),
        name="close",
    )(ids, lengths, leads, x, gmid, n1, gqkv, vec, w, sums, qsums, bup0, bup1)


def hop_dp(value, flip, ranks):
    return lax.ppermute(value, "dp", [(i, i ^ flip) for i in range(ranks)])


def hop_fsdp(value, flip, ranks):
    return lax.ppermute(value, "fsdp", [(i, i ^ flip) for i in range(ranks)])


def tie(values, *others):
    flat, tree = jax.tree.flatten(values)
    more = jax.tree.leaves(others)
    done = lax.optimization_barrier(tuple(flat) + tuple(more))
    return jax.tree.unflatten(tree, done[:len(flat)])


def gather_depth(piece, sizes):
    return [piece] + [hop_fsdp(piece, 2 * z, sizes[1]) for z in range(1, sizes[1] // 2)]


def gather_sides(column, sizes):
    return hop_dp(column, 2, sizes[0]), hop_fsdp(column, 1, sizes[1])


def gather_corner(sides, sizes):
    by_x, by_y = sides
    half = by_x.shape[0] // 2
    return hop_fsdp(by_x[:half], 1, sizes[1]), hop_dp(by_y[half:], 2, sizes[0])


def cross(parts, sizes):
    return [hop_dp(part, 1, sizes[0]) for part in parts]


def name_parts(parts, others):
    half = parts[0].shape[0] // 2
    flips = ((0, 0), (2, 0), (0, 1), (2, 1), (2, 1 + 2 * half))
    own = [(dp, fs, part) for (dp, fs), part in zip(flips, parts)]
    return own + [(dp | 1, fs, part) for (dp, fs), part in zip(flips, others)]


def plus(*terms):
    return sum(term.astype(F32) for term in terms)


def reduce_core(mine, theirs, sizes):
    return mine, hop_dp(theirs, 1, sizes[0])


def reduce_sides(cored, sizes):
    both = plus(*cored).astype(BF16)
    half = both.shape[2] // 2
    first, second = both[:, :, :half], both[:, :, half:]
    got = hop_dp(first[1], 2, sizes[0]), hop_fsdp(second[:, 1], 1, sizes[1])
    return first[0], second[:, 0], got


def reduce_corner(sided, sizes):
    first, second, got = sided
    first, second = plus(first, got[0]).astype(BF16), plus(second, got[1]).astype(BF16)
    got = hop_fsdp(first[1], 1, sizes[1]), hop_dp(second[1], 2, sizes[0])
    return first[0], second[0], got


def reduce_depth(cornered, sizes):
    first, second, got = cornered
    first, second = plus(first, got[0]).astype(BF16), plus(second, got[1]).astype(BF16)
    apart = [first[k] for k in range(first.shape[0])] + [second[k] for k in range(second.shape[0])]
    return [apart[0]] + [hop_fsdp(apart[z], 2 * z, sizes[1]) for z in range(1, len(apart))]


def per_device(sizes, tokens, lengths, lead_index, cotangent, w_qkv, w_out, w_up, w_down, vectors, lead_table, up_bias):
    dps, fss = sizes
    ids = jnp.stack([lax.axis_index("dp"), lax.axis_index("fsdp")]).astype(jnp.int32)
    thin, wide, tall = D // fss, FF // fss, D // dps
    x, gy = tokens.reshape(L, D), cotangent.reshape(L, D)

    piece0 = pack_first(w_qkv, jnp.concatenate([vectors, lead_table, up_bias], axis=0))
    w_down_t = w_down.T
    piece1 = jnp.concatenate([pack_chunk(0, w_up, w_down_t), fold_out(w_out)], axis=0)
    piece2 = pack_chunk(1, w_up, w_down_t)

    depth0 = gather_depth(piece0, sizes)
    depth0, piece1 = tie((depth0, piece1))
    column0 = jnp.stack(depth0)
    sides0, depth1 = gather_sides(column0, sizes), gather_depth(piece1, sizes)
    column0, sides0, depth1, piece2 = tie((column0, sides0, depth1, piece2))
    corner0, other0 = gather_corner(sides0, sizes), cross((column0,) + sides0, sizes)
    column0, sides0, corner0, other0, depth1, piece2 = tie((column0, sides0, corner0, other0, depth1, piece2))
    last0 = cross(corner0, sizes)
    last0, depth1, piece2 = tie((last0, depth1, piece2))

    column1 = jnp.stack(depth1)
    sides1, depth2 = gather_sides(column1, sizes), gather_depth(piece2, sizes)
    found = name_parts((column0,) + sides0 + corner0, other0 + last0)
    opened = open_call(found, ids, lengths, lead_index, x, sizes)
    column1, sides1, depth2, opened = tie((column1, sides1, depth2, opened))
    n1, qkv, w_qkv, vec, table, bias0, bias1 = opened

    column2 = jnp.stack(depth2)
    corner1, other1, sides2 = gather_corner(sides1, sizes), cross((column1,), sizes), gather_sides(column2, sizes)
    attended = attend_call(lengths, qkv)
    column1, sides1, corner1, other1, column2, sides2, attended = tie(
        (column1, sides1, corner1, other1, column2, sides2, attended)
    )
    o, lse = attended

    last1 = cross(sides1 + corner1, sizes)
    last1, column2, sides2 = tie((last1, column2, sides2))

    corner2, other2 = gather_corner(sides2, sizes), cross((column2,) + sides2, sizes)
    found = name_parts((column1,) + sides1 + corner1, other1 + last1)
    first = feed_first(found, ids, o, x, gy, vec, bias0, sizes)
    column2, sides2, corner2, other2, first = tie((column2, sides2, corner2, other2, first))
    a0, bup0, middle, n2, gn2, wd0, w_out, mine0, theirs0 = first

    last2 = cross(corner2, sizes)
    last2, theirs0 = tie((last2, theirs0))

    grads0 = reduce_core(mine0, theirs0, sizes)
    found = name_parts((column2,) + sides2 + corner2, other2 + last2)
    second = feed_second(found, ids, o, n2, gy, middle, gn2, vec, bias1, w_out, sizes)
    grads0, second = tie((grads0, second))
    a1, bup1, wd1, gmid, go, sums, mine1, theirs1 = second

    grads0, grads1 = reduce_sides(grads0, sizes), reduce_core(mine1, theirs1, sizes)
    back = attend_back_call(lengths, qkv, o, go, lse)
    grads0, grads1, back = tie((grads0, grads1, back))
    gqkv, qsums = back

    grads0, grads1 = reduce_corner(grads0, sizes), reduce_sides(grads1, sizes)
    closed = close_call(
        ids, lengths, lead_index, x, gmid, n1, gqkv, vec, w_qkv, sums, qsums, bup0, bup1, sizes
    )
    grads0, grads1, closed, a0 = tie((grads0, grads1, closed, a0))
    gx, mine2, theirs2 = closed

    grads0, grads1, grads2 = reduce_depth(grads0, sizes), reduce_corner(grads1, sizes), reduce_core(mine2, theirs2, sizes)
    grads0, grads1, grads2, a0 = tie((grads0, grads1, grads2, a0))
    grads1, grads2 = reduce_depth(grads1, sizes), reduce_sides(grads2, sizes)
    y = last_call(a0, a1, middle, vec, wd0, wd1)
    grads0, grads1, grads2, y = tie((grads0, grads1, grads2, y))
    grads2 = reduce_corner(grads2, sizes)
    grads2 = reduce_depth(grads2, sizes)
    got0, got1, got2 = plus(*grads0), plus(*grads1), plus(*grads2)

    many = wide // 3
    up = jnp.concatenate([got1[:tall], got0[:tall]], axis=1)
    down = []
    for side in range(fss // dps):
        rows = slice(tall + side * thin, tall + (side + 1) * thin)
        down += [got1[rows], got0[rows]]
    down = jnp.concatenate(down, axis=1).T
    out = jnp.concatenate([got1[2 * tall:, :thin], got1[2 * tall:, thin:2 * thin]], axis=0)
    rest = 3 * thin - 256
    fold = 128 // rest
    some = tall // fold
    tail = got2[2 * tall:2 * tall + some]
    tail = jnp.concatenate([tail[:, k * rest:(k + 1) * rest] for k in range(fold)], axis=0)
    qkv_grad = jnp.concatenate([got2[:tall], got2[tall:2 * tall], tail], axis=1)
    small = got2[2 * tall + some:, :thin]
    return (
        y.reshape(1, L, D), gx.reshape(1, L, D), qkv_grad, out, up, down, small[0:2], small[2:7], small[7:8],
    )


def per_device_plain(sizes, tokens, lengths, lead_index, cotangent, w_qkv, w_out, w_up, w_down, vectors, table, bias):
    def full(shard):
        return lax.all_gather(lax.all_gather(shard, "fsdp", axis=1, tiled=True), "dp", axis=0, tiled=True)

    def share(grad):
        part = lax.psum_scatter(grad.astype(F32), "fsdp", scatter_dimension=1, tiled=True)
        return lax.psum_scatter(part, "dp", scatter_dimension=0, tiled=True)

    x, gy = tokens.reshape(L, D), cotangent.reshape(L, D)
    w_qkv, w_out, w_up, w_down_t = full(w_qkv), full(w_out), full(w_up), full(w_down).T
    vec, bias = full(vectors).astype(F32), full(bias).astype(F32).reshape(1, FF)
    table = jnp.pad(full(table), ((0, 32 - LEADS), (0, 0)))
    n1, qkv = qkv_call(lengths, lead_index, x, vec, table, w_qkv)
    o, lse = attend_call(lengths, qkv)
    middle, n2, a, slope = up_call(o, x, vec, w_out, w_up, bias)
    gh, gmid, gatt, go, sums, bup = feed_back_call(gy, slope, middle, vec, w_down_t, w_up, w_out)
    gqkv, qsums = attend_back_call(lengths, qkv, o, go, lse)
    gx, first_sums, gtable = first_back_call(lengths, lead_index, x, gmid, gqkv, vec, w_qkv)
    gvec = jnp.concatenate([first_sums[:2], sums[:2], qsums[:2], sums[2:4]], axis=0)
    y = down_call(a, middle, vec, w_down_t)
    return (
        y.reshape(1, L, D),
        gx.reshape(1, L, D),
        share(outer_call(n1, gqkv, "grad_qkv")),
        share(outer_call(o, gatt, "grad_out")),
        share(outer_call(n2, gh, "grad_up")),
        share(outer_call(gy, a, "grad_down").T),
        share(gvec),
        share(gtable[:LEADS]),
        share(bup[0].reshape(FF // D, D)),
    )


def solution(mesh):
    sizes = (mesh.shape["dp"], mesh.shape["fsdp"])
    whole_tiles = FF // sizes[1] == 384 and sizes[1] == 2 * sizes[0]
    plan = per_device if whole_tiles else per_device_plain
    rows, both = P(("dp", "fsdp"), None, None), P("dp", "fsdp")
    index = P(("dp", "fsdp"), None)
    return jax.shard_map(
        functools.partial(plan, sizes),
        mesh=mesh,
        in_specs=(rows, index, index, rows) + (both,) * 7,
        out_specs=(rows, rows) + (both,) * 7,
        check_vma=False,
    )
```

```python
import functools

import jax
import jax.numpy as jnp
from jax import lax
from jax.experimental import pallas as pl
from jax.experimental.pallas import tpu as pltpu
from jax.sharding import PartitionSpec as P

D = 768
HEADS = 12
HD = 64
FF = 3072
LEADS = 20
WIN = 8
L = 1024
EPSILON = 1e-05
MASKED = -1e30
ROWS = 256
TILES = L // ROWS
BLK = 128
PAIRS = HEADS // 2
SCALE = HD ** (-0.5)
VMEM_BYTES = 56 * 1024 * 1024

F32 = jnp.float32
BF16 = jnp.bfloat16


def params(limit=VMEM_BYTES):
    return pltpu.CompilerParams(vmem_limit_bytes=limit)


def dot_nn(a, b):
    return lax.dot_general(a, b, (((1,), (0,)), ((), ())), preferred_element_type=F32)


def dot_nt(a, b):
    return lax.dot_general(a, b, (((1,), (1,)), ((), ())), preferred_element_type=F32)


def whole(shape, space=pltpu.VMEM):
    return pl.BlockSpec(shape, lambda *_: (0,) * len(shape), memory_space=space)


def smem():
    return pl.BlockSpec(memory_space=pltpu.SMEM)


def rows_of(width):
    return pl.BlockSpec((ROWS, width), lambda i: (i, 0))


def norm_parts(values):
    center = values - jnp.mean(values, axis=-1, keepdims=True)
    spread = jnp.mean(center * center, axis=-1, keepdims=True)
    inv = lax.rsqrt(spread + EPSILON)
    return center * inv, inv


def bounds_of(lengths_ref):
    found, total = [], 0
    for w in range(WIN):
        total = total + lengths_ref[0, w]
        found.append(total)
    return found


def lead_of(places, bounds, lead_ref):
    lead = jnp.full(places.shape, -1, jnp.int32)
    for w in reversed(range(WIN)):
        lead = jnp.where(places < bounds[w], lead_ref[0, w], lead)
    return lead


def qkv_kernel(len_ref, lead_ref, x_ref, vec_ref, table_ref, w_ref, n1_ref, qkv_ref):
    step = pl.program_id(0)
    bounds = bounds_of(len_ref)
    hat, _ = norm_parts(x_ref[...].astype(F32))
    normed = hat * (1.0 + vec_ref[0:1, :]) + vec_ref[1:2, :]
    shape = (ROWS, table_ref.shape[0])
    places = step * ROWS + lax.broadcasted_iota(jnp.int32, shape, 0)
    hot = lead_of(places, bounds, lead_ref) == lax.broadcasted_iota(jnp.int32, shape, 1)
    n1 = (normed + dot_nn(hot.astype(BF16), table_ref[...])).astype(BF16)
    n1_ref[...] = n1
    for third in range(3):
        cols = slice(third * D, (third + 1) * D)
        part = dot_nn(n1, w_ref[:, cols])
        if third == 0:
            part = (part + vec_ref[4:5, :]).astype(BF16) * jnp.asarray(SCALE, BF16)
        elif third == 2:
            part = part + vec_ref[5:6, :]
        qkv_ref[:, cols] = part.astype(BF16)


def qkv_call(lengths, leads, x, vec, table, w):
    return pl.pallas_call(
        qkv_kernel,
        grid=(TILES,),
        in_specs=[smem(), smem(), rows_of(D), whole(vec.shape), whole(table.shape), whole(w.shape)],
        out_specs=[rows_of(D), rows_of(3 * D)],
        out_shape=[jax.ShapeDtypeStruct((L, D), BF16), jax.ShapeDtypeStruct((L, 3 * D), BF16)],
        compiler_params=params(),
        cost_estimate=pl.CostEstimate(flops=2 * L * D * 3 * D, bytes_accessed=12_000_000, transcendentals=0),
        name="norm_qkv",
    )(lengths, leads, x, vec, table, w)


SPANS = (1, 2, 3, 4, 6)


def dot_tn(a, b):
    return lax.dot_general(a, b, (((0,), (0,)), ((), ())), preferred_element_type=F32)


def key_span(bounds, block):
    first, last = block * BLK, block * BLK + BLK - 1
    start, end = jnp.int32(0), jnp.int32(L)
    for w in range(WIN):
        start = jnp.where(bounds[w] <= first, bounds[w], start)
    for w in reversed(range(WIN)):
        end = jnp.where(bounds[w] > last, bounds[w], end)
    return start // 16 * 16, end


def window_at(places, bounds):
    found = jnp.zeros(places.shape, jnp.int32)
    for w in range(WIN):
        found = found + (places >= bounds[w]).astype(jnp.int32)
    return found


def hide(bounds, start, rows, block):
    shape = (rows, 2 * BLK)
    keys = window_at(start + lax.broadcasted_iota(jnp.int32, (rows, 1), 0), bounds)
    lanes = lax.broadcasted_iota(jnp.int32, (1, 2 * BLK), 1)
    queries = window_at(block * BLK + jnp.where(lanes < BLK, lanes, lanes - BLK), bounds)
    return jnp.where(jnp.broadcast_to(keys, shape) == jnp.broadcast_to(queries, shape), 0.0, MASKED)


def split_pair(two):
    lanes = lax.broadcasted_iota(jnp.int32, two.shape, 1)
    zero = jnp.zeros_like(two)
    return jnp.concatenate([jnp.where(lanes < HD, two, zero), jnp.where(lanes < HD, zero, two)], axis=0)


def join_pair(both):
    lanes = lax.broadcasted_iota(jnp.int32, (BLK, BLK), 1)
    return jnp.where(lanes < HD, both[:BLK], both[BLK:])


def by_span(bounds, block, body):
    start, end = key_span(bounds, block)
    need = (end - start + BLK - 1) // BLK
    below = 0
    for span in SPANS:
        @pl.when((need > below) & (need <= span))
        def _(span=span):
            body(pl.multiple_of(jnp.minimum(start, L - span * BLK), 16), span * BLK)

        below = span


def attend_kernel(len_ref, qkv_ref, o_ref, lse_ref, hidden):
    bounds = bounds_of(len_ref)
    lse_ref[HEADS:, :] = jnp.zeros((lse_ref.shape[0] - HEADS, L), F32)

    def query_step(block, carry):
        at = pl.multiple_of(block * BLK, BLK)

        def body(start, rows):
            hidden[:rows] = hide(bounds, start, rows, block)
            def score(p):
                cols = slice(p * BLK, (p + 1) * BLK)
                keys = qkv_ref[pl.ds(start, rows), D + p * BLK:D + (p + 1) * BLK]
                return dot_nt(keys, split_pair(qkv_ref[pl.ds(at, BLK), cols])) + hidden[:rows]

            following = score(0)
            for p in range(PAIRS):
                scores = following
                if p + 1 < PAIRS:
                    following = score(p + 1)
                cols = slice(p * BLK, (p + 1) * BLK)
                vals = qkv_ref[pl.ds(start, rows), 2 * D + p * BLK:2 * D + (p + 1) * BLK]
                top = jnp.max(scores, axis=0, keepdims=True)
                expo = jnp.exp(scores - top)
                total = jnp.sum(expo, axis=0, keepdims=True)
                soft = (expo * (1.0 / total)).astype(BF16)
                o_ref[pl.ds(at, BLK), cols] = join_pair(dot_tn(soft, vals)).astype(BF16)
                log_total = top + jnp.log(total)
                lse_ref[2 * p:2 * p + 1, pl.ds(at, BLK)] = log_total[:, :BLK]
                lse_ref[2 * p + 1:2 * p + 2, pl.ds(at, BLK)] = log_total[:, BLK:]

        by_span(bounds, block, body)
        return carry

    lax.fori_loop(0, L // BLK, query_step, 0)


def attend_call(lengths, qkv):
    return pl.pallas_call(
        attend_kernel,
        in_specs=[smem(), pl.BlockSpec(memory_space=pltpu.VMEM)],
        out_specs=[pl.BlockSpec(memory_space=pltpu.VMEM)] * 2,
        out_shape=[jax.ShapeDtypeStruct((L, D), BF16), jax.ShapeDtypeStruct((16, L), F32)],
        scratch_shapes=[pltpu.VMEM((SPANS[-1] * BLK, 2 * BLK), F32)],
        compiler_params=params(),
        cost_estimate=pl.CostEstimate(flops=4 * L * L * D, bytes_accessed=8_000_000, transcendentals=0),
        name="attend",
    )(lengths, qkv)


def attend_back_kernel(len_ref, qkv_ref, o_ref, go_ref, lse_ref, g_ref, sums_ref, hidden, dk, dv):
    bounds = bounds_of(len_ref)
    dk[...] = jnp.zeros_like(dk)
    dv[...] = jnp.zeros_like(dv)
    sums_ref[...] = jnp.zeros_like(sums_ref)

    def query_step(block, carry):
        at = pl.multiple_of(block * BLK, BLK)

        def body(start, rows):
            hidden[:rows] = hide(bounds, start, rows, block)
            for p in range(PAIRS):
                cols = slice(p * BLK, (p + 1) * BLK)
                keys = qkv_ref[pl.ds(start, rows), D + p * BLK:D + (p + 1) * BLK]
                vals = qkv_ref[pl.ds(start, rows), 2 * D + p * BLK:2 * D + (p + 1) * BLK]
                grads = go_ref[pl.ds(at, BLK), cols]
                prod = (grads.astype(F32) * o_ref[pl.ds(at, BLK), cols].astype(F32)).T
                dots = jnp.concatenate(
                    [jnp.sum(prod[:HD], axis=0, keepdims=True), jnp.sum(prod[HD:], axis=0, keepdims=True)], axis=1
                )
                logs = jnp.concatenate(
                    [lse_ref[2 * p:2 * p + 1, pl.ds(at, BLK)], lse_ref[2 * p + 1:2 * p + 2, pl.ds(at, BLK)]], axis=1
                )
                queries, grads = split_pair(qkv_ref[pl.ds(at, BLK), cols]), split_pair(grads)
                soft = jnp.exp(dot_nt(keys, queries) + hidden[:rows] - logs)
                grad_scores = (soft * (dot_nt(vals, grads) - dots)).astype(BF16)
                dv[pl.ds(start, rows), cols] += dot_nn(soft.astype(BF16), grads)
                dk[pl.ds(start, rows), cols] += dot_nn(grad_scores, queries)
                done = (join_pair(dot_tn(grad_scores, keys)) * SCALE).astype(BF16)
                g_ref[pl.ds(at, BLK), cols] = done
                sums_ref[0:1, cols] += jnp.sum(done.astype(F32), axis=0, keepdims=True)

        by_span(bounds, block, body)
        return carry

    lax.fori_loop(0, L // BLK, query_step, 0)
    g_ref[:, D:2 * D] = dk[...].astype(BF16)
    gv = dv[...].astype(BF16)
    g_ref[:, 2 * D:] = gv
    sums_ref[1:2, :] = jnp.sum(gv.astype(F32), axis=0, keepdims=True)


def attend_back_call(lengths, qkv, o, go, lse):
    return pl.pallas_call(
        attend_back_kernel,
        in_specs=[smem()] + [pl.BlockSpec(memory_space=pltpu.VMEM)] * 4,
        out_specs=[pl.BlockSpec(memory_space=pltpu.VMEM)] * 2,
        out_shape=[jax.ShapeDtypeStruct((L, 3 * D), BF16), jax.ShapeDtypeStruct((8, D), F32)],
        scratch_shapes=[
            pltpu.VMEM((SPANS[-1] * BLK, 2 * BLK), F32),
            pltpu.VMEM((L, D), F32),
            pltpu.VMEM((L, D), F32),
        ],
        compiler_params=params(),
        cost_estimate=pl.CostEstimate(flops=10 * L * L * D, bytes_accessed=15_000_000, transcendentals=0),
        name="attend_back",
    )(lengths, qkv, o, go, lse)


def up_kernel(o_ref, x_ref, vec_ref, wo_ref, wu_ref, bu_ref, mid_ref, n2_ref, a_ref, slope_ref):
    middle = x_ref[...].astype(F32) + (dot_nn(o_ref[...], wo_ref[...]) + vec_ref[6:7, :])
    mid_ref[...] = middle
    hat, _ = norm_parts(middle)
    n2 = (hat * (1.0 + vec_ref[2:3, :]) + vec_ref[3:4, :]).astype(BF16)
    n2_ref[...] = n2
    width = 512
    for c in range(FF // width):
        cols = slice(c * width, (c + 1) * width)
        h = dot_nn(n2, wu_ref[:, cols]) + bu_ref[:, cols]
        act, slope = gate_pair(h)
        a_ref[:, cols] = act.astype(BF16)
        slope_ref[:, cols] = slope.astype(BF16)


def up_call(o, x, vec, wo, wu, bu):
    return pl.pallas_call(
        up_kernel,
        grid=(TILES,),
        in_specs=[rows_of(D), rows_of(D), whole(vec.shape), whole(wo.shape), whole(wu.shape), whole(bu.shape)],
        out_specs=[rows_of(D), rows_of(D), rows_of(FF), rows_of(FF)],
        out_shape=[
            jax.ShapeDtypeStruct((L, D), F32),
            jax.ShapeDtypeStruct((L, D), BF16),
            jax.ShapeDtypeStruct((L, FF), BF16),
            jax.ShapeDtypeStruct((L, FF), BF16),
        ],
        compiler_params=params(),
        cost_estimate=pl.CostEstimate(flops=2 * L * D * (FF + D), bytes_accessed=25_000_000, transcendentals=2 * L * FF),
        name="feed_up",
    )(o, x, vec, wo, wu, bu)


def down_kernel(a_ref, mid_ref, vec_ref, wdt_ref, y_ref):
    y_ref[...] = (mid_ref[...] + (dot_nt(a_ref[...], wdt_ref[...]) + vec_ref[7:8, :])).astype(BF16)


def down_call(a, middle, vec, wdt):
    return pl.pallas_call(
        down_kernel,
        grid=(TILES,),
        in_specs=[rows_of(FF), rows_of(D), whole(vec.shape), whole(wdt.shape)],
        out_specs=rows_of(D),
        out_shape=jax.ShapeDtypeStruct((L, D), BF16),
        compiler_params=params(),
        cost_estimate=pl.CostEstimate(flops=2 * L * D * FF, bytes_accessed=17_000_000, transcendentals=0),
        name="feed_down",
    )(a, middle, vec, wdt)


def feed_back_kernel(gy_ref, slope_ref, mid_ref, vec_ref, wdt_ref, wu_ref, wo_ref,
                     gh_ref, gmid_ref, gatt_ref, go_ref, sums_ref, bup_ref):
    @pl.when(pl.program_id(0) == 0)
    def _():
        sums_ref[...] = jnp.zeros_like(sums_ref)
        bup_ref[...] = jnp.zeros_like(bup_ref)

    gm = gy_ref[...]
    gy = gm.astype(F32)
    width = 768
    gn2 = None
    for c in range(FF // width):
        cols = slice(c * width, (c + 1) * width)
        ga = dot_nn(gm, wdt_ref[:, cols])
        gh = (ga * slope_ref[:, cols].astype(F32)).astype(BF16)
        gh_ref[:, cols] = gh
        bup_ref[0:1, cols] += jnp.sum(gh.astype(F32), axis=0, keepdims=True)
        part = dot_nt(gh, wu_ref[:, cols])
        gn2 = part if gn2 is None else gn2 + part
    hat, inv = norm_parts(mid_ref[...])
    sums_ref[0:1, :] += jnp.sum(gn2 * hat, axis=0, keepdims=True)
    sums_ref[1:2, :] += jnp.sum(gn2, axis=0, keepdims=True)
    gmid = gy + norm_back(gn2, hat, inv, vec_ref[2:3, :])
    gmid_ref[...] = gmid
    gatt = gmid.astype(BF16)
    gatt_ref[...] = gatt
    sums_ref[2:3, :] += jnp.sum(gatt.astype(F32), axis=0, keepdims=True)
    sums_ref[3:4, :] += jnp.sum(gy, axis=0, keepdims=True)
    go_ref[...] = dot_nt(gatt, wo_ref[...]).astype(BF16)


def feed_back_call(gy, slope, middle, vec, wdt, wu, wo):
    return pl.pallas_call(
        feed_back_kernel,
        grid=(TILES,),
        in_specs=[rows_of(D), rows_of(FF), rows_of(D), whole(vec.shape), whole(wdt.shape), whole(wu.shape), whole(wo.shape)],
        out_specs=[rows_of(FF), rows_of(D), rows_of(D), rows_of(D), whole((8, D)), whole((8, FF))],
        out_shape=[
            jax.ShapeDtypeStruct((L, FF), BF16),
            jax.ShapeDtypeStruct((L, D), F32),
            jax.ShapeDtypeStruct((L, D), BF16),
            jax.ShapeDtypeStruct((L, D), BF16),
            jax.ShapeDtypeStruct((8, D), F32),
            jax.ShapeDtypeStruct((8, FF), F32),
        ],
        compiler_params=params(),
        cost_estimate=pl.CostEstimate(flops=2 * L * D * (2 * FF + D), bytes_accessed=35_000_000, transcendentals=0),
        name="feed_back",
    )(gy, slope, middle, vec, wdt, wu, wo)


def outer_kernel(left_ref, right_ref, out_ref, turned):
    @pl.when(pl.program_id(0) == 0)
    def _():
        turned[...] = left_ref[...].T

    out_ref[...] = dot_nn(turned[...], right_ref[...]).astype(BF16)


def outer_call(left, right, name):
    wide = right.shape[1]
    width = 768
    return pl.pallas_call(
        outer_kernel,
        grid=(wide // width,),
        in_specs=[whole(left.shape), pl.BlockSpec((L, width), lambda i: (0, i))],
        out_specs=pl.BlockSpec((D, width), lambda i: (0, i)),
        out_shape=jax.ShapeDtypeStruct((D, wide), BF16),
        scratch_shapes=[pltpu.VMEM((D, L), BF16)],
        compiler_params=params(),
        cost_estimate=pl.CostEstimate(flops=2 * L * D * wide, bytes_accessed=4 * L * D + 4 * D * wide, transcendentals=0),
        name=name,
    )(left, right)


def first_back_kernel(len_ref, lead_ref, x_ref, gmid_ref, g_ref, vec_ref, w_ref, out_ref, sums_ref, table_ref):
    step = pl.program_id(0)

    @pl.when(step == 0)
    def _():
        sums_ref[...] = jnp.zeros_like(sums_ref)
        table_ref[...] = jnp.zeros_like(table_ref)

    gn1 = dot_nt(g_ref[...], w_ref[...])
    hat, inv = norm_parts(x_ref[...].astype(F32))
    sums_ref[0:1, :] += jnp.sum(gn1 * hat, axis=0, keepdims=True)
    sums_ref[1:2, :] += jnp.sum(gn1, axis=0, keepdims=True)
    shape = (table_ref.shape[0], ROWS)
    places = step * ROWS + lax.broadcasted_iota(jnp.int32, shape, 1)
    hot = lead_of(places, bounds_of(len_ref), lead_ref) == lax.broadcasted_iota(jnp.int32, shape, 0)
    hot = hot.astype(BF16)
    high = gn1.astype(BF16)
    low = (gn1 - high.astype(F32)).astype(BF16)
    table_ref[...] += dot_nn(hot, high) + dot_nn(hot, low)
    out_ref[...] = gmid_ref[...] + norm_back(gn1, hat, inv, vec_ref[0:1, :])


def first_back_call(lengths, leads, x, gmid, gqkv, vec, w):
    return pl.pallas_call(
        first_back_kernel,
        grid=(TILES,),
        in_specs=[smem(), smem(), rows_of(D), rows_of(D), rows_of(3 * D), whole(vec.shape), whole(w.shape)],
        out_specs=[rows_of(D), whole((8, D)), whole((32, D))],
        out_shape=[
            jax.ShapeDtypeStruct((L, D), F32),
            jax.ShapeDtypeStruct((8, D), F32),
            jax.ShapeDtypeStruct((32, D), F32),
        ],
        compiler_params=params(),
        cost_estimate=pl.CostEstimate(flops=2 * L * D * 3 * D, bytes_accessed=17_000_000, transcendentals=0),
        name="first_back",
    )(lengths, leads, x, gmid, gqkv, vec, w)


def slots(found):
    return [
        (at, k, dp, fs + 2 * k)
        for at, (dp, fs, part) in enumerate(found)
        for k in range(part.shape[0])
    ]

def chunk_cols(chunk, wide):
    third = wide // 3
    return (2 * third, third) if chunk == 0 else (0, 2 * third)


def any_space():
    return pl.BlockSpec(memory_space=pl.ANY)


def in_vmem():
    return pl.BlockSpec(memory_space=pltpu.VMEM)


def kept(shape):
    return pl.BlockSpec(shape, lambda *_: (0,) * len(shape), pipeline_mode=pl.Buffered(1))


def pack_first(w_qkv, small):
    tall, cols = w_qkv.shape
    left = cols - 256
    fold = 128 // left
    rows = tall // fold
    rest = jnp.concatenate([w_qkv[k * rows:(k + 1) * rows, 256:] for k in range(fold)], axis=1)
    small = jnp.pad(small, ((0, 16 - small.shape[0]), (0, 128 - small.shape[1])))
    return jnp.concatenate([w_qkv[:, :128], w_qkv[:, 128:256], rest, small], axis=0)


def pack_chunk(chunk, w_up, w_down_t):
    wide = w_up.shape[1]
    start, count = chunk_cols(chunk, wide)
    parts = [w_up[:, start:start + count]]
    for k in range(w_down_t.shape[1] // wide):
        parts.append(w_down_t[:, k * wide + start:k * wide + start + count])
    return jnp.concatenate(parts, axis=0)


def fold_out(w_out):
    tall, narrow = w_out.shape
    rows = tall // 4
    wide = jnp.concatenate([w_out[k * rows:(k + 1) * rows] for k in range(4)], axis=1)
    return jnp.concatenate([wide[:, k * 128:(k + 1) * 128] for k in range(4 * narrow // 128)], axis=0)


def start_all(copies):
    for copy in copies:
        copy.start()
    for copy in copies:
        copy.wait()


def open_kernel(plan, count, ids_ref, len_ref, lead_ref, x_ref, *refs):
    parts = refs[:count]
    n1_ref, qkv_ref, w_ref, vec_ref, table_ref, bias0_ref, bias1_ref, stage, table, bias, sem = refs[count:]
    step = pl.program_id(0)
    dps, fss = stage.shape[0], stage.shape[1]
    tall, cols, narrow, wide = D // dps, 3 * D // fss, D // fss, FF // fss

    @pl.when(step == 0)
    def _():
        start_all([
            pltpu.make_async_copy(parts[at].at[k], stage.at[ids_ref[0] ^ dp, ids_ref[1] ^ fs], sem)
            for at, k, dp, fs in plan
        ])
        table[...] = jnp.zeros_like(table)
        left = cols - 256
        fold = 128 // left
        rows = tall // fold
        for d in range(dps):
            for f in range(fss):
                at = slice(d * tall, (d + 1) * tall)
                w_ref[at, f * cols:f * cols + 128] = stage[d, f, :tall]
                w_ref[at, f * cols + 128:f * cols + 256] = stage[d, f, tall:2 * tall]
                for k in range(fold):
                    w_ref[d * tall + k * rows:d * tall + (k + 1) * rows, f * cols + 256:(f + 1) * cols] = (
                        stage[d, f, 2 * tall:2 * tall + rows, k * left:(k + 1) * left]
                    )
                small = stage[d, f, 2 * tall + rows:, :narrow].astype(F32)
                at = slice(f * narrow, (f + 1) * narrow)
                vec_ref[2 * d:2 * d + 2, at] = small[0:2]
                table[5 * d:5 * d + 5, at] = small[2:7]
                bias[0:1, d * D + f * narrow:d * D + (f + 1) * narrow] = small[7:8]
        table_ref[...] = table[...].astype(BF16)
        for chunk, ref in ((0, bias0_ref), (1, bias1_ref)):
            start, many = chunk_cols(chunk, wide)
            for f in range(fss):
                ref[:, f * many:(f + 1) * many] = bias[:, f * wide + start:f * wide + start + many]

    qkv_tile(step, len_ref, lead_ref, x_ref, vec_ref, table_ref, w_ref, n1_ref, qkv_ref)


def qkv_tile(step, len_ref, lead_ref, x_ref, vec_ref, table_ref, w_ref, n1_ref, qkv_ref):
    bounds = bounds_of(len_ref)
    hat, _ = norm_parts(x_ref[...].astype(F32))
    normed = hat * (1.0 + vec_ref[0:1, :]) + vec_ref[1:2, :]
    shape = (ROWS, table_ref.shape[0])
    places = step * ROWS + lax.broadcasted_iota(jnp.int32, shape, 0)
    hot = lead_of(places, bounds, lead_ref) == lax.broadcasted_iota(jnp.int32, shape, 1)
    n1 = (normed + dot_nn(hot.astype(BF16), table_ref[...])).astype(BF16)
    n1_ref[...] = n1
    for third in range(3):
        cols = slice(third * D, (third + 1) * D)
        part = dot_nn(n1, w_ref[:, cols])
        if third == 0:
            part = (part + vec_ref[4:5, :]).astype(BF16) * jnp.asarray(SCALE, BF16)
        elif third == 2:
            part = part + vec_ref[5:6, :]
        qkv_ref[:, cols] = part.astype(BF16)


def open_call(found, ids, lengths, leads, x, sizes):
    parts = [part for _, _, part in found]
    rows = parts[0].shape[1]
    dps, fss = sizes
    sides = [fss * chunk_cols(chunk, FF // fss)[1] for chunk in range(2)]
    shapes = [((L, D), BF16), ((L, 3 * D), BF16), ((D, 3 * D), BF16), ((8, D), F32), ((32, D), BF16)]
    shapes += [((1, side), F32) for side in sides]
    return pl.pallas_call(
        functools.partial(open_kernel, slots(found), len(parts)),
        grid=(TILES,),
        in_specs=[smem(), smem(), smem(), rows_of(D)] + [any_space()] * len(parts),
        out_specs=[rows_of(D), rows_of(3 * D)] + [kept(shape) for shape, _ in shapes[2:]],
        out_shape=[jax.ShapeDtypeStruct(shape, kind) for shape, kind in shapes],
        scratch_shapes=[
            pltpu.VMEM((dps, fss, rows, 128), BF16),
            pltpu.VMEM((32, D), F32),
            pltpu.VMEM((1, FF), F32),
            pltpu.SemaphoreType.DMA,
        ],
        compiler_params=params(),
        cost_estimate=pl.CostEstimate(flops=2 * L * D * 3 * D, bytes_accessed=18_000_000, transcendentals=0),
        name="open",
    )(ids, lengths, leads, x, *parts)


def chunk_copies(plan, ids_ref, parts, wu, wd, stage, sem, sizes):
    dps, fss = sizes
    tall, thin = D // dps, D // fss
    many = wu.shape[1] // fss
    copies = []
    for at, k, dp, fs in plan:
        d, f = ids_ref[0] ^ dp, ids_ref[1] ^ fs
        part = parts[at]

        def place(ref, row, rows, col):
            return ref.at[pl.ds(pl.multiple_of(row, 16), rows), pl.ds(pl.multiple_of(col, 128), many)]

        copies.append(pltpu.make_async_copy(part.at[k, pl.ds(0, tall), :], place(wu, d * tall, tall, f * many), sem))
        for side in range(fss // dps):
            rows = part.at[k, pl.ds(tall + side * thin, thin), :]
            copies.append(pltpu.make_async_copy(rows, place(wd, f * thin, thin, (d * (fss // dps) + side) * many), sem))
        if stage is not None:
            rows = part.at[k, pl.ds(tall + fss // dps * thin, stage.shape[2]), :]
            copies.append(pltpu.make_async_copy(rows, stage.at[d, f], sem))
    return copies


def unfold_out(stage, wo, sizes):
    dps, fss = sizes
    tall, thin = D // dps, D // fss
    rows = tall // 4
    for d in range(dps):
        for f in range(fss):
            flat = jnp.concatenate([stage[d, f, k * rows:(k + 1) * rows] for k in range(thin * 4 // 128)], axis=1)
            for k in range(4):
                wo[d * tall + k * rows:d * tall + (k + 1) * rows, f * thin:(f + 1) * thin] = flat[:, k * thin:(k + 1) * thin]


def start(copies):
    for copy in copies:
        copy.start()


def wait(copies):
    for copy in copies:
        copy.wait()


def turn(ref, plain, ordered, mine, count):
    plain[...] = ref[...].T
    tall = ordered.shape[0] // count
    for k in range(count):
        at = pl.multiple_of((mine ^ k) * tall, tall)
        ordered[k * tall:(k + 1) * tall, :] = plain[pl.ds(at, tall), :]


def gate_pair(h):
    cdf = 0.5 + 0.5 * lax.erf(h * 0.7071067811865476)
    return h * cdf, cdf + h * (0.3989422804014327 * jnp.exp(h * h * -0.5))


def norm_back(grad, hat, inv, gain):
    scaled = grad * (1.0 + gain)
    both = jnp.mean(scaled * hat, axis=-1, keepdims=True)
    return inv * (scaled - jnp.mean(scaled, axis=-1, keepdims=True) - hat * both)


def feed_step(step, gm_ref, n2, n2_t, gm_t, wu, wd, bias, a_ref, bup_ref, gh, gn2, grads, ids_ref, sizes):
    dps, fss = sizes
    pair = fss // dps
    width = a_ref.shape[1]
    many = width // pair
    tall, thin = D // dps, D // fss
    block = step ^ (ids_ref[1] // pair)
    cols = pl.ds(pl.multiple_of(block * width, width), width)
    own_u, own_d = wu[:, cols], wd[:, cols]
    shift = bias[:, cols]
    bup = jnp.zeros((1, width), F32)
    for r in range(TILES):
        rows = slice(r * ROWS, (r + 1) * ROWS)
        act, slope = gate_pair(dot_nn(n2[rows, :], own_u) + shift)
        a_ref[rows, :] = act.astype(BF16)
        part = (dot_nn(gm_ref[rows, :], own_d) * slope).astype(BF16)
        gh[rows, :] = part
        bup = bup + jnp.sum(part.astype(F32), axis=0, keepdims=True)
        gn2[rows, :] += dot_nt(part, own_u)
    bup_ref[:, cols] = bup
    grad = dot_nn(gm_t[...], a_ref[...]).astype(BF16)
    d = block ^ ids_ref[0]
    for f in range(fss):
        for side in range(pair):
            at = tall + side * thin
            grads[d & 1, d >> 1, f & 1, f >> 1, at:at + thin, :] = grad[f * thin:(f + 1) * thin, side * many:(side + 1) * many]
    grad = dot_nn(n2_t[...], gh[...]).astype(BF16)
    for side in range(pair):
        y = (ids_ref[1] & 1) ^ side
        for d in range(dps):
            grads[d & 1, d >> 1, y, step, :tall, :] = grad[d * tall:(d + 1) * tall, side * many:(side + 1) * many]


def up_copies(step, grads, mine_ref, theirs_ref, tall, sem):
    return [
        pltpu.make_async_copy(grads.at[c, :, :, step, pl.ds(0, tall), :], ref.at[:, :, step, pl.ds(0, tall), :], sem)
        for c, ref in ((0, mine_ref), (1, theirs_ref))
    ]


def down_copy(c, x, grads, ref, tall, sem):
    return pltpu.make_async_copy(
        grads.at[c, x, :, :, pl.ds(tall, tall), :], ref.at[x, :, :, pl.ds(tall, tall), :], sem
    )


def send_grads(step, ids_ref, grads, mine_ref, theirs_ref, up_sem, down_sem, sizes):
    tall = D // sizes[0]
    start(up_copies(step, grads, mine_ref, theirs_ref, tall, up_sem))
    away = step ^ (ids_ref[1] // (sizes[1] // sizes[0])) ^ ids_ref[0]
    for c, ref in ((0, mine_ref), (1, theirs_ref)):
        @pl.when((away & 1) == c)
        def _(c=c, ref=ref):
            down_copy(c, away >> 1, grads, ref, tall, down_sem).start()


def wait_grads(grads, mine_ref, theirs_ref, up_sem, down_sem, sizes):
    tall = D // sizes[0]
    for step in range(sizes[0]):
        wait(up_copies(step, grads, mine_ref, theirs_ref, tall, up_sem))
        down_copy(0, 0, grads, mine_ref, tall, down_sem).wait()


def feed_first_kernel(plan, count, sizes, ids_ref, vec_ref, bias_ref, o_hbm, x_hbm, gm_hbm, *refs):
    parts = refs[:count]
    (a_ref, bup_ref, mid_hbm, n2_hbm, gn2_hbm, wd_hbm, wo_hbm, mine_ref, theirs_ref,
     o, x, gm, mid, n2, gn2, wd, wo, wu, stage, plain, n2_t, gm_t, gh, grads, sems) = refs[count:]
    step = pl.program_id(0)
    outs = [
        pltpu.make_async_copy(src, dst, sems.at[4 + k])
        for k, (src, dst) in enumerate(((wd, wd_hbm), (wo, wo_hbm), (mid, mid_hbm), (n2, n2_hbm), (gn2, gn2_hbm)))
    ]

    @pl.when(step == 0)
    def _():
        ins = [pltpu.make_async_copy(src, dst, sems.at[1 + k]) for k, (src, dst) in enumerate(((gm_hbm, gm), (o_hbm, o), (x_hbm, x)))]
        lay = chunk_copies(plan, ids_ref, parts, wu, wd, stage, sems.at[0], sizes)
        start(ins[:1] + lay + ins[1:])
        ins[0].wait()
        turn(gm, plain, gm_t, ids_ref[1], sizes[1])
        gn2[...] = jnp.zeros_like(gn2)
        wait(lay)
        unfold_out(stage, wo, sizes)
        start(outs[:2])
        wait(ins[1:])
        for r in range(TILES):
            rows = slice(r * ROWS, (r + 1) * ROWS)
            middle = x[rows, :].astype(F32) + (dot_nn(o[rows, :], wo[...]) + vec_ref[6:7, :])
            mid[rows, :] = middle
            hat, _ = norm_parts(middle)
            n2[rows, :] = (hat * (1.0 + vec_ref[2:3, :]) + vec_ref[3:4, :]).astype(BF16)
        start(outs[2:4])
        turn(n2, plain, n2_t, ids_ref[0], sizes[0])

    feed_step(step, gm, n2, n2_t, gm_t, wu, wd, bias_ref, a_ref, bup_ref, gh, gn2, grads, ids_ref, sizes)
    send_grads(step, ids_ref, grads, mine_ref, theirs_ref, sems.at[9], sems.at[10], sizes)

    @pl.when(step == pl.num_programs(0) - 1)
    def _():
        outs[4].start()
        wait_grads(grads, mine_ref, theirs_ref, sems.at[9], sems.at[10], sizes)
        wait(outs)


def feed_first(found, ids, o, x, gm, vec, bias, sizes):
    parts = [part for _, _, part in found]
    dps, fss = sizes
    units = bias.shape[1]
    width, many = units // dps, units // fss
    rows = 2 * (D // dps)
    shape = (dps // 2, 2, fss // 2, rows, many)
    outs = [
        ((L, units), BF16), ((1, units), F32), ((L, D), F32), ((L, D), BF16), ((L, D), F32), ((D, units), BF16), ((D, D), BF16),
        (shape, BF16), (shape, BF16),
    ]
    return pl.pallas_call(
        functools.partial(feed_first_kernel, slots(found), len(parts), sizes),
        grid_spec=pltpu.PrefetchScalarGridSpec(
            num_scalar_prefetch=1,
            grid=(dps,),
            in_specs=[kept((8, D)), kept((1, units))] + [any_space()] * (3 + len(parts)),
            out_specs=[pl.BlockSpec((L, width), lambda i, ids: (0, i ^ (ids[1] // (fss // dps)))), kept((1, units))]
            + [any_space()] * 7,
            scratch_shapes=[
                pltpu.VMEM((L, D), BF16),
                pltpu.VMEM((L, D), BF16),
                pltpu.VMEM((L, D), BF16),
                pltpu.VMEM((L, D), F32),
                pltpu.VMEM((L, D), BF16),
                pltpu.VMEM((L, D), F32),
                pltpu.VMEM((D, units), BF16),
                pltpu.VMEM((D, D), BF16),
                pltpu.VMEM((D, units), BF16),
                pltpu.VMEM((dps, fss, parts[0].shape[1] - rows, 128), BF16),
                pltpu.VMEM((D, L), BF16),
                pltpu.VMEM((D, L), BF16),
                pltpu.VMEM((D, L), BF16),
                pltpu.VMEM((L, width), BF16),
                pltpu.VMEM((2,) + shape, BF16),
                pltpu.SemaphoreType.DMA((11,)),
            ],
        ),
        out_shape=[jax.ShapeDtypeStruct(s, kind) for s, kind in outs],
        compiler_params=params(),
        cost_estimate=pl.CostEstimate(flops=2 * L * D * (5 * units + D), bytes_accessed=30_000_000, transcendentals=2 * L * units),
        name="feed_first",
    )(ids, vec, bias, o, x, gm, *parts)


def feed_second_kernel(plan, count, sizes, ids_ref, vec_ref, bias_ref, o_hbm, n2_hbm, gm_hbm, mid_hbm, gn2_hbm, wo_hbm, *refs):
    parts = refs[:count]
    (a_ref, bup_ref, sums_ref, wd_hbm, gmid_hbm, go_hbm, mine_ref, theirs_ref,
     o, n2, gm, mid, gn2, wo, wd, wu, plain, n2_t, gm_t, gh, gatt, full, grads, sems) = refs[count:]
    step = pl.program_id(0)
    dps, fss = sizes
    tall, thin = D // dps, D // fss
    ins = [
        pltpu.make_async_copy(src, dst, sems.at[k])
        for k, (src, dst) in enumerate(((gm_hbm, gm), (n2_hbm, n2), (gn2_hbm, gn2), (o_hbm, o), (mid_hbm, mid), (wo_hbm, wo)))
    ]
    wd_out = pltpu.make_async_copy(wd, wd_hbm, sems.at[7])

    @pl.when(step == 0)
    def _():
        lay = chunk_copies(plan, ids_ref, parts, wu, wd, None, sems.at[6], sizes)
        start(ins[:2] + lay + ins[2:])
        ins[0].wait()
        turn(gm, plain, gm_t, ids_ref[1], fss)
        ins[1].wait()
        turn(n2, plain, n2_t, ids_ref[0], dps)
        wait(lay)
        wd_out.start()
        ins[2].wait()

    feed_step(step, gm, n2, n2_t, gm_t, wu, wd, bias_ref, a_ref, bup_ref, gh, gn2, grads, ids_ref, sizes)
    send_grads(step, ids_ref, grads, mine_ref, theirs_ref, sems.at[8], sems.at[9], sizes)

    @pl.when(step == pl.num_programs(0) - 1)
    def _():
        wait(ins[3:])
        turn(o, plain, n2_t, ids_ref[0], dps)
        sums = [jnp.zeros((1, D), F32)] * 4
        outs = []
        for r in range(TILES):
            rows = slice(r * ROWS, (r + 1) * ROWS)
            grad, gy = gn2[rows, :], gm[rows, :].astype(F32)
            hat, inv = norm_parts(mid[rows, :])
            gmid = gy + norm_back(grad, hat, inv, vec_ref[2:3, :])
            mid[rows, :] = gmid
            low = gmid.astype(BF16)
            gatt[rows, :] = low
            n2[rows, :] = dot_nt(low, wo[...]).astype(BF16)
            for k, term in enumerate((grad * hat, grad, low.astype(F32), gy)):
                sums[k] = sums[k] + jnp.sum(term, axis=0, keepdims=True)
        outs = [pltpu.make_async_copy(mid, gmid_hbm, sems.at[10]), pltpu.make_async_copy(n2, go_hbm, sems.at[11])]
        start(outs)
        sums_ref[...] = jnp.concatenate(sums + [jnp.zeros((4, D), F32)], axis=0)
        full[...] = dot_nn(n2_t[...], gatt[...]).astype(BF16)
        for f in range(fss):
            flip = ids_ref[1] ^ f
            for d in range(dps):
                for k in range(2):
                    at = 2 * tall
                    grads[d & 1, d >> 1, flip & 1, flip >> 1, at:at + tall // 2, k * thin:(k + 1) * thin] = (
                        full[d * tall + k * (tall // 2):d * tall + (k + 1) * (tall // 2), f * thin:(f + 1) * thin]
                    )
                grads[d & 1, d >> 1, flip & 1, flip >> 1, 2 * tall:, 2 * thin:] = jnp.zeros(
                    (tall // 2, grads.shape[5] - 2 * thin), BF16
                )
        rows = pl.ds(2 * tall, tall // 2)
        rest = [
            pltpu.make_async_copy(grads.at[c, :, :, :, rows, :], ref.at[:, :, :, rows, :], sems.at[12])
            for c, ref in ((0, mine_ref), (1, theirs_ref))
        ]
        start(rest)
        wait_grads(grads, mine_ref, theirs_ref, sems.at[8], sems.at[9], sizes)
        wait(rest + outs + [wd_out])


def feed_second(found, ids, o, n2, gm, mid, gn2, vec, bias, wo, sizes):
    parts = [part for _, _, part in found]
    dps, fss = sizes
    units = bias.shape[1]
    width, many = units // dps, units // fss
    tall = D // dps
    shape = (dps // 2, 2, fss // 2, 2 * tall + tall // 2, many)
    outs = [
        ((L, units), BF16), ((1, units), F32), ((8, D), F32), ((D, units), BF16), ((L, D), F32), ((L, D), BF16),
        (shape, BF16), (shape, BF16),
    ]
    return pl.pallas_call(
        functools.partial(feed_second_kernel, slots(found), len(parts), sizes),
        grid_spec=pltpu.PrefetchScalarGridSpec(
            num_scalar_prefetch=1,
            grid=(dps,),
            in_specs=[kept((8, D)), kept((1, units))] + [any_space()] * (6 + len(parts)),
            out_specs=[
                pl.BlockSpec((L, width), lambda i, ids: (0, i ^ (ids[1] // (fss // dps)))), kept((1, units)), kept((8, D)),
            ] + [any_space()] * 5,
            scratch_shapes=[
                pltpu.VMEM((L, D), BF16),
                pltpu.VMEM((L, D), BF16),
                pltpu.VMEM((L, D), BF16),
                pltpu.VMEM((L, D), F32),
                pltpu.VMEM((L, D), F32),
                pltpu.VMEM((D, D), BF16),
                pltpu.VMEM((D, units), BF16),
                pltpu.VMEM((D, units), BF16),
                pltpu.VMEM((D, L), BF16),
                pltpu.VMEM((D, L), BF16),
                pltpu.VMEM((D, L), BF16),
                pltpu.VMEM((L, width), BF16),
                pltpu.VMEM((L, D), BF16),
                pltpu.VMEM((D, D), BF16),
                pltpu.VMEM((2,) + shape, BF16),
                pltpu.SemaphoreType.DMA((13,)),
            ],
        ),
        out_shape=[jax.ShapeDtypeStruct(s, kind) for s, kind in outs],
        compiler_params=params(),
        cost_estimate=pl.CostEstimate(flops=2 * L * D * (5 * units + 2 * D), bytes_accessed=35_000_000, transcendentals=2 * L * units),
        name="feed_second",
    )(ids, vec, bias, o, n2, gm, mid, gn2, wo, *parts)


def last_kernel(a0_ref, a1_ref, mid_ref, vec_ref, w0_ref, w1_ref, y_ref):
    total = dot_nt(a0_ref[...], w0_ref[...]) + dot_nt(a1_ref[...], w1_ref[...])
    y_ref[...] = (mid_ref[...] + (total + vec_ref[7:8, :])).astype(BF16)


def last_call(a0, a1, middle, vec, w0, w1):
    return pl.pallas_call(
        last_kernel,
        grid=(TILES,),
        in_specs=[rows_of(a0.shape[1]), rows_of(a1.shape[1]), rows_of(D), kept((8, D)), kept(w0.shape), kept(w1.shape)],
        out_specs=rows_of(D),
        out_shape=jax.ShapeDtypeStruct((L, D), BF16),
        compiler_params=params(),
        cost_estimate=pl.CostEstimate(flops=2 * L * D * FF, bytes_accessed=17_000_000, transcendentals=0),
        name="feed_down",
    )(a0, a1, middle, vec, w0, w1)


def close_kernel(sizes, ids_ref, len_ref, lead_ref, vec_ref, sums_ref, qsums_ref, bup0_ref, bup1_ref,
                 x_hbm, gmid_hbm, n1_hbm, g_hbm, w_hbm, gx_hbm, mine_ref, theirs_ref,
                 x, gmid, n1, g, w, plain, left, full, table, grads, sems):
    dps, fss = sizes
    tall, cols, thin, wide = D // dps, 3 * D // fss, D // fss, FF // fss
    ins = [
        pltpu.make_async_copy(src, dst, sems.at[k])
        for k, (src, dst) in enumerate(((n1_hbm, n1), (g_hbm, g), (w_hbm, w), (x_hbm, x), (gmid_hbm, gmid)))
    ]
    start(ins)
    ins[0].wait()
    turn(n1, plain, left, ids_ref[0], dps)
    ins[1].wait()
    rest = cols - 256
    fold = 128 // rest
    some = tall // fold
    for third in range(3):
        at = slice(third * D, (third + 1) * D)
        full[:, at] = dot_nn(left[...], g[:, at]).astype(BF16)
    for f in range(fss):
        flip = ids_ref[1] ^ f
        y, z = flip & 1, flip >> 1
        for d in range(dps):
            own = slice(d * tall, (d + 1) * tall)
            c, away = d & 1, d >> 1
            grads[c, away, y, z, 0:tall, :] = full[own, f * cols:f * cols + 128]
            grads[c, away, y, z, tall:2 * tall, :] = full[own, f * cols + 128:f * cols + 256]
            for k in range(fold):
                grads[c, away, y, z, 2 * tall:2 * tall + some, k * rest:(k + 1) * rest] = (
                    full[d * tall + k * some:d * tall + (k + 1) * some, f * cols + 256:(f + 1) * cols]
                )
    big, little = pl.ds(0, 2 * tall + some), pl.ds(2 * tall + some, 16)
    sends = [
        [
            pltpu.make_async_copy(grads.at[c, :, :, :, rows, :], ref.at[:, :, :, rows, :], sems.at[at])
            for c, ref in ((0, mine_ref), (1, theirs_ref))
        ]
        for at, rows in ((5, big), (6, little))
    ]
    start(sends[0])
    wait(ins[2:])
    gain, shift = jnp.zeros((1, D), F32), jnp.zeros((1, D), F32)
    table[...] = jnp.zeros_like(table)
    bounds = bounds_of(len_ref)
    outs = []
    for r in range(TILES):
        rows = slice(r * ROWS, (r + 1) * ROWS)
        grad = dot_nt(g[rows, :], w[...])
        hat, inv = norm_parts(x[rows, :].astype(F32))
        gain = gain + jnp.sum(grad * hat, axis=0, keepdims=True)
        shift = shift + jnp.sum(grad, axis=0, keepdims=True)
        shape = (table.shape[0], ROWS)
        places = r * ROWS + lax.broadcasted_iota(jnp.int32, shape, 1)
        hot = lead_of(places, bounds, lead_ref) == lax.broadcasted_iota(jnp.int32, shape, 0)
        hot = hot.astype(BF16)
        high = grad.astype(BF16)
        low = (grad - high.astype(F32)).astype(BF16)
        table[...] += dot_nn(hot, high) + dot_nn(hot, low)
        gmid[rows, :] += norm_back(grad, hat, inv, vec_ref[0:1, :])
    out = pltpu.make_async_copy(gmid, gx_hbm, sems.at[7])
    out.start()
    bup = []
    for f in range(fss):
        for chunk, ref in ((1, bup1_ref), (0, bup0_ref)):
            many = chunk_cols(chunk, wide)[1]
            bup.append(ref[:, f * many:(f + 1) * many])
    bup = jnp.concatenate(bup, axis=1)
    gvec = [gain, shift, sums_ref[0:1, :], sums_ref[1:2, :], qsums_ref[0:1, :], qsums_ref[1:2, :], sums_ref[2:3, :], sums_ref[3:4, :]]
    for d in range(dps):
        small = jnp.concatenate(
            gvec[2 * d:2 * d + 2] + [table[5 * d:5 * d + 5, :], bup[:, d * D:(d + 1) * D], jnp.zeros((8, D), F32)], axis=0
        )
        away = ids_ref[0] ^ d
        for f in range(fss):
            flip = ids_ref[1] ^ f
            part = jnp.concatenate([small[:, f * thin:(f + 1) * thin], jnp.zeros((16, 128 - thin), F32)], axis=1)
            grads[away & 1, away >> 1, flip & 1, flip >> 1, 2 * tall + some:, :] = part.astype(BF16)
    start(sends[1])
    wait(sends[0] + sends[1] + [out])


def close_call(ids, lengths, leads, x, gmid, n1, gqkv, vec, w, sums, qsums, bup0, bup1, sizes):
    dps, fss = sizes
    tall = D // dps
    rows = 2 * tall + tall // (128 // (3 * D // fss - 256)) + 16
    shape = (dps // 2, 2, fss // 2, rows, 128)
    return pl.pallas_call(
        functools.partial(close_kernel, sizes),
        in_specs=[smem()] * 3 + [in_vmem()] * 5 + [any_space()] * 5,
        out_specs=[any_space()] * 3,
        out_shape=[jax.ShapeDtypeStruct((L, D), F32), jax.ShapeDtypeStruct(shape, BF16), jax.ShapeDtypeStruct(shape, BF16)],
        scratch_shapes=[
            pltpu.VMEM((L, D), BF16),
            pltpu.VMEM((L, D), F32),
            pltpu.VMEM((L, D), BF16),
            pltpu.VMEM((L, 3 * D), BF16),
            pltpu.VMEM((D, 3 * D), BF16),
            pltpu.VMEM((D, L), BF16),
            pltpu.VMEM((D, L), BF16),
            pltpu.VMEM((D, 3 * D), BF16),
            pltpu.VMEM((32, D), F32),
            pltpu.VMEM((2,) + shape, BF16),
            pltpu.SemaphoreType.DMA((8,)),
        ],
        compiler_params=params(),
        cost_estimate=pl.CostEstimate(flops=4 * L * D * 3 * D, bytes_accessed=25_000_000, transcendentals=0),
        name="close",
    )(ids, lengths, leads, vec, sums, qsums, bup0, bup1, x, gmid, n1, gqkv, w)


def hop_dp(value, flip, ranks):
    return lax.ppermute(value, "dp", [(i, i ^ flip) for i in range(ranks)])


def hop_fsdp(value, flip, ranks):
    return lax.ppermute(value, "fsdp", [(i, i ^ flip) for i in range(ranks)])


def tie(values, *others):
    flat, tree = jax.tree.flatten(values)
    more = jax.tree.leaves(others)
    done = lax.optimization_barrier(tuple(flat) + tuple(more))
    return jax.tree.unflatten(tree, done[:len(flat)])


def gather_depth(piece, sizes):
    return [piece] + [hop_fsdp(piece, 2 * z, sizes[1]) for z in range(1, sizes[1] // 2)]


def gather_sides(column, sizes):
    return hop_dp(column, 2, sizes[0]), hop_fsdp(column, 1, sizes[1])


def gather_corner(sides, sizes):
    by_x, by_y = sides
    half = by_x.shape[0] // 2
    return hop_fsdp(by_x[:half], 1, sizes[1]), hop_dp(by_y[half:], 2, sizes[0])


def cross(parts, sizes):
    return [hop_dp(part, 1, sizes[0]) for part in parts]


def name_parts(parts, others):
    half = parts[0].shape[0] // 2
    flips = ((0, 0), (2, 0), (0, 1), (2, 1), (2, 1 + 2 * half))
    own = [(dp, fs, part) for (dp, fs), part in zip(flips, parts)]
    return own + [(dp | 1, fs, part) for (dp, fs), part in zip(flips, others)]


def plus(*terms):
    return sum(term.astype(F32) for term in terms)


def reduce_core(mine, theirs, sizes):
    return mine, hop_dp(theirs, 1, sizes[0])


def reduce_sides(cored, sizes):
    both = plus(*cored).astype(BF16)
    half = both.shape[2] // 2
    first, second = both[:, :, :half], both[:, :, half:]
    got = hop_dp(first[1], 2, sizes[0]), hop_fsdp(second[:, 1], 1, sizes[1])
    return first[0], second[:, 0], got


def reduce_corner(sided, sizes):
    first, second, got = sided
    first, second = plus(first, got[0]).astype(BF16), plus(second, got[1]).astype(BF16)
    got = hop_fsdp(first[1], 1, sizes[1]), hop_dp(second[1], 2, sizes[0])
    return first[0], second[0], got


def reduce_depth(cornered, sizes):
    first, second, got = cornered
    first, second = plus(first, got[0]).astype(BF16), plus(second, got[1]).astype(BF16)
    apart = [first[k] for k in range(first.shape[0])] + [second[k] for k in range(second.shape[0])]
    return [apart[0]] + [hop_fsdp(apart[z], 2 * z, sizes[1]) for z in range(1, len(apart))]


def per_device(sizes, tokens, lengths, lead_index, cotangent, w_qkv, w_out, w_up, w_down, vectors, lead_table, up_bias):
    dps, fss = sizes
    ids = jnp.stack([lax.axis_index("dp"), lax.axis_index("fsdp")]).astype(jnp.int32)
    thin, wide, tall = D // fss, FF // fss, D // dps
    x, gy = tokens.reshape(L, D), cotangent.reshape(L, D)

    piece0 = pack_first(w_qkv, jnp.concatenate([vectors, lead_table, up_bias], axis=0))
    w_down_t = w_down.T
    piece1 = jnp.concatenate([pack_chunk(0, w_up, w_down_t), fold_out(w_out)], axis=0)
    piece2 = pack_chunk(1, w_up, w_down_t)

    depth0 = gather_depth(piece0, sizes)
    depth0, piece1 = tie((depth0, piece1))
    column0 = jnp.stack(depth0)
    sides0, depth1 = gather_sides(column0, sizes), gather_depth(piece1, sizes)
    column0, sides0, depth1, piece2 = tie((column0, sides0, depth1, piece2))
    corner0, other0 = gather_corner(sides0, sizes), cross((column0,) + sides0, sizes)
    column0, sides0, corner0, other0, depth1, piece2 = tie((column0, sides0, corner0, other0, depth1, piece2))
    last0 = cross(corner0, sizes)
    last0, depth1, piece2 = tie((last0, depth1, piece2))

    column1 = jnp.stack(depth1)
    sides1, depth2 = gather_sides(column1, sizes), gather_depth(piece2, sizes)
    found = name_parts((column0,) + sides0 + corner0, other0 + last0)
    opened = open_call(found, ids, lengths, lead_index, x, sizes)
    column1, sides1, depth2, opened = tie((column1, sides1, depth2, opened))
    n1, qkv, w_qkv, vec, table, bias0, bias1 = opened

    column2 = jnp.stack(depth2)
    corner1, other1, sides2 = gather_corner(sides1, sizes), cross((column1,), sizes), gather_sides(column2, sizes)
    attended = attend_call(lengths, qkv)
    column1, sides1, corner1, other1, column2, sides2, attended = tie(
        (column1, sides1, corner1, other1, column2, sides2, attended)
    )
    o, lse = attended

    last1 = cross(sides1 + corner1, sizes)
    last1, column2, sides2 = tie((last1, column2, sides2))

    corner2, other2 = gather_corner(sides2, sizes), cross((column2,) + sides2, sizes)
    found = name_parts((column1,) + sides1 + corner1, other1 + last1)
    first = feed_first(found, ids, o, x, gy, vec, bias0, sizes)
    column2, sides2, corner2, other2, first = tie((column2, sides2, corner2, other2, first))
    a0, bup0, middle, n2, gn2, wd0, w_out, mine0, theirs0 = first

    last2 = cross(corner2, sizes)
    last2, theirs0 = tie((last2, theirs0))

    grads0 = reduce_core(mine0, theirs0, sizes)
    found = name_parts((column2,) + sides2 + corner2, other2 + last2)
    second = feed_second(found, ids, o, n2, gy, middle, gn2, vec, bias1, w_out, sizes)
    grads0, second = tie((grads0, second))
    a1, bup1, sums, wd1, gmid, go, mine1, theirs1 = second

    grads0, grads1 = reduce_sides(grads0, sizes), reduce_core(mine1, theirs1, sizes)
    back = attend_back_call(lengths, qkv, o, go, lse)
    grads0, grads1, back = tie((grads0, grads1, back))
    gqkv, qsums = back

    grads0, grads1 = reduce_corner(grads0, sizes), reduce_sides(grads1, sizes)
    closed = close_call(
        ids, lengths, lead_index, x, gmid, n1, gqkv, vec, w_qkv, sums, qsums, bup0, bup1, sizes
    )
    grads0, grads1, closed, a0 = tie((grads0, grads1, closed, a0))
    gx, mine2, theirs2 = closed

    grads0, grads1, grads2 = reduce_depth(grads0, sizes), reduce_corner(grads1, sizes), reduce_core(mine2, theirs2, sizes)
    grads0, grads1, grads2, a0 = tie((grads0, grads1, grads2, a0))
    grads1, grads2 = reduce_depth(grads1, sizes), reduce_sides(grads2, sizes)
    y = last_call(a0, a1, middle, vec, wd0, wd1)
    grads0, grads1, grads2, y = tie((grads0, grads1, grads2, y))
    grads2 = reduce_corner(grads2, sizes)
    grads2 = reduce_depth(grads2, sizes)
    got0, got1, got2 = plus(*grads0), plus(*grads1), plus(*grads2)

    many = wide // 3
    up = jnp.concatenate([got1[:tall], got0[:tall]], axis=1)
    down = []
    for side in range(fss // dps):
        rows = slice(tall + side * thin, tall + (side + 1) * thin)
        down += [got1[rows], got0[rows]]
    down = jnp.concatenate(down, axis=1).T
    out = jnp.concatenate([got1[2 * tall:, :thin], got1[2 * tall:, thin:2 * thin]], axis=0)
    rest = 3 * thin - 256
    fold = 128 // rest
    some = tall // fold
    tail = got2[2 * tall:2 * tall + some]
    tail = jnp.concatenate([tail[:, k * rest:(k + 1) * rest] for k in range(fold)], axis=0)
    qkv_grad = jnp.concatenate([got2[:tall], got2[tall:2 * tall], tail], axis=1)
    small = got2[2 * tall + some:, :thin]
    return (
        y.reshape(1, L, D), gx.reshape(1, L, D), qkv_grad, out, up, down, small[0:2], small[2:7], small[7:8],
    )


def per_device_plain(sizes, tokens, lengths, lead_index, cotangent, w_qkv, w_out, w_up, w_down, vectors, table, bias):
    def full(shard):
        return lax.all_gather(lax.all_gather(shard, "fsdp", axis=1, tiled=True), "dp", axis=0, tiled=True)

    def share(grad):
        part = lax.psum_scatter(grad.astype(F32), "fsdp", scatter_dimension=1, tiled=True)
        return lax.psum_scatter(part, "dp", scatter_dimension=0, tiled=True)

    x, gy = tokens.reshape(L, D), cotangent.reshape(L, D)
    w_qkv, w_out, w_up, w_down_t = full(w_qkv), full(w_out), full(w_up), full(w_down).T
    vec, bias = full(vectors).astype(F32), full(bias).astype(F32).reshape(1, FF)
    table = jnp.pad(full(table), ((0, 32 - LEADS), (0, 0)))
    n1, qkv = qkv_call(lengths, lead_index, x, vec, table, w_qkv)
    o, lse = attend_call(lengths, qkv)
    middle, n2, a, slope = up_call(o, x, vec, w_out, w_up, bias)
    gh, gmid, gatt, go, sums, bup = feed_back_call(gy, slope, middle, vec, w_down_t, w_up, w_out)
    gqkv, qsums = attend_back_call(lengths, qkv, o, go, lse)
    gx, first_sums, gtable = first_back_call(lengths, lead_index, x, gmid, gqkv, vec, w_qkv)
    gvec = jnp.concatenate([first_sums[:2], sums[:2], qsums[:2], sums[2:4]], axis=0)
    y = down_call(a, middle, vec, w_down_t)
    return (
        y.reshape(1, L, D),
        gx.reshape(1, L, D),
        share(outer_call(n1, gqkv, "grad_qkv")),
        share(outer_call(o, gatt, "grad_out")),
        share(outer_call(n2, gh, "grad_up")),
        share(outer_call(gy, a, "grad_down").T),
        share(gvec),
        share(gtable[:LEADS]),
        share(bup[0].reshape(FF // D, D)),
    )


def solution(mesh):
    sizes = (mesh.shape["dp"], mesh.shape["fsdp"])
    whole_tiles = FF // sizes[1] == 384 and sizes[1] == 2 * sizes[0]
    plan = per_device if whole_tiles else per_device_plain
    rows, both = P(("dp", "fsdp"), None, None), P("dp", "fsdp")
    index = P(("dp", "fsdp"), None)
    return jax.shard_map(
        functools.partial(plan, sizes),
        mesh=mesh,
        in_specs=(rows, index, index, rows) + (both,) * 7,
        out_specs=(rows, rows) + (both,) * 7,
        check_vma=False,
    )
```

```python
import functools

import jax
import jax.numpy as jnp
from jax import lax
from jax.experimental import pallas as pl
from jax.experimental.pallas import tpu as pltpu
from jax.sharding import PartitionSpec as P

D = 768
HEADS = 12
HD = 64
FF = 3072
LEADS = 20
WIN = 8
L = 1024
EPSILON = 1e-05
MASKED = -1e30
ROWS = 256
TILES = L // ROWS
BLK = 128
PAIRS = HEADS // 2
SCALE = HD ** (-0.5)
VMEM_BYTES = 56 * 1024 * 1024

F32 = jnp.float32
BF16 = jnp.bfloat16


def params(limit=VMEM_BYTES):
    return pltpu.CompilerParams(vmem_limit_bytes=limit)


def dot_nn(a, b):
    return lax.dot_general(a, b, (((1,), (0,)), ((), ())), preferred_element_type=F32)


def dot_nt(a, b):
    return lax.dot_general(a, b, (((1,), (1,)), ((), ())), preferred_element_type=F32)


def whole(shape, space=pltpu.VMEM):
    return pl.BlockSpec(shape, lambda *_: (0,) * len(shape), memory_space=space)


def smem():
    return pl.BlockSpec(memory_space=pltpu.SMEM)


def rows_of(width):
    return pl.BlockSpec((ROWS, width), lambda i: (i, 0))


def norm_parts(values):
    center = values - jnp.mean(values, axis=-1, keepdims=True)
    spread = jnp.mean(center * center, axis=-1, keepdims=True)
    inv = lax.rsqrt(spread + EPSILON)
    return center * inv, inv


def bounds_of(lengths_ref):
    found, total = [], 0
    for w in range(WIN):
        total = total + lengths_ref[0, w]
        found.append(total)
    return found


def lead_of(places, bounds, lead_ref):
    lead = jnp.full(places.shape, -1, jnp.int32)
    for w in reversed(range(WIN)):
        lead = jnp.where(places < bounds[w], lead_ref[0, w], lead)
    return lead


def qkv_kernel(len_ref, lead_ref, x_ref, vec_ref, table_ref, w_ref, n1_ref, qkv_ref):
    step = pl.program_id(0)
    bounds = bounds_of(len_ref)
    hat, _ = norm_parts(x_ref[...].astype(F32))
    normed = hat * (1.0 + vec_ref[0:1, :]) + vec_ref[1:2, :]
    shape = (ROWS, table_ref.shape[0])
    places = step * ROWS + lax.broadcasted_iota(jnp.int32, shape, 0)
    hot = lead_of(places, bounds, lead_ref) == lax.broadcasted_iota(jnp.int32, shape, 1)
    n1 = (normed + dot_nn(hot.astype(BF16), table_ref[...])).astype(BF16)
    n1_ref[...] = n1
    for third in range(3):
        cols = slice(third * D, (third + 1) * D)
        part = dot_nn(n1, w_ref[:, cols])
        if third == 0:
            part = (part + vec_ref[4:5, :]).astype(BF16) * jnp.asarray(SCALE, BF16)
        elif third == 2:
            part = part + vec_ref[5:6, :]
        qkv_ref[:, cols] = part.astype(BF16)


def qkv_call(lengths, leads, x, vec, table, w):
    return pl.pallas_call(
        qkv_kernel,
        grid=(TILES,),
        in_specs=[smem(), smem(), rows_of(D), whole(vec.shape), whole(table.shape), whole(w.shape)],
        out_specs=[rows_of(D), rows_of(3 * D)],
        out_shape=[jax.ShapeDtypeStruct((L, D), BF16), jax.ShapeDtypeStruct((L, 3 * D), BF16)],
        compiler_params=params(),
        cost_estimate=pl.CostEstimate(flops=2 * L * D * 3 * D, bytes_accessed=12_000_000, transcendentals=0),
        name="norm_qkv",
    )(lengths, leads, x, vec, table, w)


SPANS = (1, 2, 3, 4, 6)


def dot_tn(a, b):
    return lax.dot_general(a, b, (((0,), (0,)), ((), ())), preferred_element_type=F32)


def key_span(bounds, block):
    first, last = block * BLK, block * BLK + BLK - 1
    start, end = jnp.int32(0), jnp.int32(L)
    for w in range(WIN):
        start = jnp.where(bounds[w] <= first, bounds[w], start)
    for w in reversed(range(WIN)):
        end = jnp.where(bounds[w] > last, bounds[w], end)
    return start // 16 * 16, end


def window_at(places, bounds):
    found = jnp.zeros(places.shape, jnp.int32)
    for w in range(WIN):
        found = found + (places >= bounds[w]).astype(jnp.int32)
    return found


def hide(bounds, start, rows, block):
    shape = (rows, 2 * BLK)
    keys = window_at(start + lax.broadcasted_iota(jnp.int32, (rows, 1), 0), bounds)
    lanes = lax.broadcasted_iota(jnp.int32, (1, 2 * BLK), 1)
    queries = window_at(block * BLK + jnp.where(lanes < BLK, lanes, lanes - BLK), bounds)
    return jnp.where(jnp.broadcast_to(keys, shape) == jnp.broadcast_to(queries, shape), 0.0, MASKED)


def split_pair(two):
    lanes = lax.broadcasted_iota(jnp.int32, two.shape, 1)
    zero = jnp.zeros_like(two)
    return jnp.concatenate([jnp.where(lanes < HD, two, zero), jnp.where(lanes < HD, zero, two)], axis=0)


def join_pair(both):
    lanes = lax.broadcasted_iota(jnp.int32, (BLK, BLK), 1)
    return jnp.where(lanes < HD, both[:BLK], both[BLK:])


def by_span(bounds, block, body):
    start, end = key_span(bounds, block)
    need = (end - start + BLK - 1) // BLK
    below = 0
    for span in SPANS:
        @pl.when((need > below) & (need <= span))
        def _(span=span):
            body(pl.multiple_of(jnp.minimum(start, L - span * BLK), 16), span * BLK)

        below = span


def attend_kernel(len_ref, qkv_ref, o_ref, lse_ref, hidden):
    bounds = bounds_of(len_ref)
    lse_ref[HEADS:, :] = jnp.zeros((lse_ref.shape[0] - HEADS, L), F32)

    def query_step(block, carry):
        at = pl.multiple_of(block * BLK, BLK)

        def body(start, rows):
            hidden[:rows] = hide(bounds, start, rows, block)
            def score(p):
                cols = slice(p * BLK, (p + 1) * BLK)
                keys = qkv_ref[pl.ds(start, rows), D + p * BLK:D + (p + 1) * BLK]
                return dot_nt(keys, split_pair(qkv_ref[pl.ds(at, BLK), cols])) + hidden[:rows]

            following = score(0)
            for p in range(PAIRS):
                scores = following
                if p + 1 < PAIRS:
                    following = score(p + 1)
                cols = slice(p * BLK, (p + 1) * BLK)
                vals = qkv_ref[pl.ds(start, rows), 2 * D + p * BLK:2 * D + (p + 1) * BLK]
                top = jnp.max(scores, axis=0, keepdims=True)
                expo = jnp.exp(scores - top)
                total = jnp.sum(expo, axis=0, keepdims=True)
                soft = (expo * (1.0 / total)).astype(BF16)
                o_ref[pl.ds(at, BLK), cols] = join_pair(dot_tn(soft, vals)).astype(BF16)
                log_total = top + jnp.log(total)
                lse_ref[2 * p:2 * p + 1, pl.ds(at, BLK)] = log_total[:, :BLK]
                lse_ref[2 * p + 1:2 * p + 2, pl.ds(at, BLK)] = log_total[:, BLK:]

        by_span(bounds, block, body)
        return carry

    lax.fori_loop(0, L // BLK, query_step, 0)


def attend_call(lengths, qkv):
    return pl.pallas_call(
        attend_kernel,
        in_specs=[smem(), pl.BlockSpec(memory_space=pltpu.VMEM)],
        out_specs=[pl.BlockSpec(memory_space=pltpu.VMEM)] * 2,
        out_shape=[jax.ShapeDtypeStruct((L, D), BF16), jax.ShapeDtypeStruct((16, L), F32)],
        scratch_shapes=[pltpu.VMEM((SPANS[-1] * BLK, 2 * BLK), F32)],
        compiler_params=params(),
        cost_estimate=pl.CostEstimate(flops=4 * L * L * D, bytes_accessed=8_000_000, transcendentals=0),
        name="attend",
    )(lengths, qkv)


def attend_back_kernel(first, len_ref, lse_ref, qkv_hbm, o_hbm, go_hbm, g_ref, sums_ref, q, k, v, o, go, hidden, dk, dv, sems):
    bounds = bounds_of(len_ref)
    wide = q.shape[1]
    at = first * BLK
    copies = [
        pltpu.make_async_copy(src.at[:, col:col + wide], dst, sems.at[n])
        for n, (src, dst, col) in enumerate(
            ((qkv_hbm, k, D + at), (qkv_hbm, q, at), (qkv_hbm, v, 2 * D + at), (go_hbm, go, at), (o_hbm, o, at))
        )
    ]
    for copy in copies:
        copy.start()
    dk[...] = jnp.zeros_like(dk)
    dv[...] = jnp.zeros_like(dv)
    sums_ref[...] = jnp.zeros_like(sums_ref)
    for copy in copies:
        copy.wait()

    def query_step(block, carry):
        at = pl.multiple_of(block * BLK, BLK)

        def body(start, rows):
            hidden[:rows] = hide(bounds, start, rows, block)
            for p in range(wide // BLK):
                head = 2 * (first + p)
                cols = slice(p * BLK, (p + 1) * BLK)
                keys, vals = k[pl.ds(start, rows), cols], v[pl.ds(start, rows), cols]
                grads = go[pl.ds(at, BLK), cols]
                prod = (grads.astype(F32) * o[pl.ds(at, BLK), cols].astype(F32)).T
                dots = jnp.concatenate(
                    [jnp.sum(prod[:HD], axis=0, keepdims=True), jnp.sum(prod[HD:], axis=0, keepdims=True)], axis=1
                )
                logs = jnp.concatenate(
                    [lse_ref[head:head + 1, pl.ds(at, BLK)], lse_ref[head + 1:head + 2, pl.ds(at, BLK)]], axis=1
                )
                queries, grads = split_pair(q[pl.ds(at, BLK), cols]), split_pair(grads)
                soft = jnp.exp(dot_nt(keys, queries) + hidden[:rows] - logs)
                grad_scores = (soft * (dot_nt(vals, grads) - dots)).astype(BF16)
                dv[pl.ds(start, rows), cols] += dot_nn(soft.astype(BF16), grads)
                dk[pl.ds(start, rows), cols] += dot_nn(grad_scores, queries)
                done = (join_pair(dot_tn(grad_scores, keys)) * SCALE).astype(BF16)
                g_ref[pl.ds(at, BLK), cols] = done
                sums_ref[0:1, cols] += jnp.sum(done.astype(F32), axis=0, keepdims=True)

        by_span(bounds, block, body)
        return carry

    lax.fori_loop(0, L // BLK, query_step, 0)
    g_ref[:, wide:2 * wide] = dk[...].astype(BF16)
    gv = dv[...].astype(BF16)
    g_ref[:, 2 * wide:] = gv
    sums_ref[1:2, :] = jnp.sum(gv.astype(F32), axis=0, keepdims=True)


def attend_back_call(lengths, qkv, o, go, lse, first=0, pairs=PAIRS):
    wide = pairs * BLK
    return pl.pallas_call(
        functools.partial(attend_back_kernel, first),
        in_specs=[smem(), pl.BlockSpec(memory_space=pltpu.VMEM)] + [pl.BlockSpec(memory_space=pl.ANY)] * 3,
        out_specs=[pl.BlockSpec(memory_space=pltpu.VMEM)] * 2,
        out_shape=[jax.ShapeDtypeStruct((L, 3 * wide), BF16), jax.ShapeDtypeStruct((8, wide), F32)],
        scratch_shapes=[pltpu.VMEM((L, wide), BF16)] * 5 + [
            pltpu.VMEM((SPANS[-1] * BLK, 2 * BLK), F32),
            pltpu.VMEM((L, wide), F32),
            pltpu.VMEM((L, wide), F32),
            pltpu.SemaphoreType.DMA((5,)),
        ],
        compiler_params=params(),
        cost_estimate=pl.CostEstimate(flops=10 * L * L * wide, bytes_accessed=15_000_000 * pairs // PAIRS, transcendentals=0),
        name="attend_back",
    )(lengths, lse, qkv, o, go)


def up_kernel(o_ref, x_ref, vec_ref, wo_ref, wu_ref, bu_ref, mid_ref, n2_ref, a_ref, slope_ref):
    middle = x_ref[...].astype(F32) + (dot_nn(o_ref[...], wo_ref[...]) + vec_ref[6:7, :])
    mid_ref[...] = middle
    hat, _ = norm_parts(middle)
    n2 = (hat * (1.0 + vec_ref[2:3, :]) + vec_ref[3:4, :]).astype(BF16)
    n2_ref[...] = n2
    width = 512
    for c in range(FF // width):
        cols = slice(c * width, (c + 1) * width)
        h = dot_nn(n2, wu_ref[:, cols]) + bu_ref[:, cols]
        act, slope = gate_pair(h)
        a_ref[:, cols] = act.astype(BF16)
        slope_ref[:, cols] = slope.astype(BF16)


def up_call(o, x, vec, wo, wu, bu):
    return pl.pallas_call(
        up_kernel,
        grid=(TILES,),
        in_specs=[rows_of(D), rows_of(D), whole(vec.shape), whole(wo.shape), whole(wu.shape), whole(bu.shape)],
        out_specs=[rows_of(D), rows_of(D), rows_of(FF), rows_of(FF)],
        out_shape=[
            jax.ShapeDtypeStruct((L, D), F32),
            jax.ShapeDtypeStruct((L, D), BF16),
            jax.ShapeDtypeStruct((L, FF), BF16),
            jax.ShapeDtypeStruct((L, FF), BF16),
        ],
        compiler_params=params(),
        cost_estimate=pl.CostEstimate(flops=2 * L * D * (FF + D), bytes_accessed=25_000_000, transcendentals=2 * L * FF),
        name="feed_up",
    )(o, x, vec, wo, wu, bu)


def down_kernel(a_ref, mid_ref, vec_ref, wdt_ref, y_ref):
    y_ref[...] = (mid_ref[...] + (dot_nt(a_ref[...], wdt_ref[...]) + vec_ref[7:8, :])).astype(BF16)


def down_call(a, middle, vec, wdt):
    return pl.pallas_call(
        down_kernel,
        grid=(TILES,),
        in_specs=[rows_of(FF), rows_of(D), whole(vec.shape), whole(wdt.shape)],
        out_specs=rows_of(D),
        out_shape=jax.ShapeDtypeStruct((L, D), BF16),
        compiler_params=params(),
        cost_estimate=pl.CostEstimate(flops=2 * L * D * FF, bytes_accessed=17_000_000, transcendentals=0),
        name="feed_down",
    )(a, middle, vec, wdt)


def feed_back_kernel(gy_ref, slope_ref, mid_ref, vec_ref, wdt_ref, wu_ref, wo_ref,
                     gh_ref, gmid_ref, gatt_ref, go_ref, sums_ref, bup_ref):
    @pl.when(pl.program_id(0) == 0)
    def _():
        sums_ref[...] = jnp.zeros_like(sums_ref)
        bup_ref[...] = jnp.zeros_like(bup_ref)

    gm = gy_ref[...]
    gy = gm.astype(F32)
    width = 768
    gn2 = None
    for c in range(FF // width):
        cols = slice(c * width, (c + 1) * width)
        ga = dot_nn(gm, wdt_ref[:, cols])
        gh = (ga * slope_ref[:, cols].astype(F32)).astype(BF16)
        gh_ref[:, cols] = gh
        bup_ref[0:1, cols] += jnp.sum(gh.astype(F32), axis=0, keepdims=True)
        part = dot_nt(gh, wu_ref[:, cols])
        gn2 = part if gn2 is None else gn2 + part
    hat, inv = norm_parts(mid_ref[...])
    sums_ref[0:1, :] += jnp.sum(gn2 * hat, axis=0, keepdims=True)
    sums_ref[1:2, :] += jnp.sum(gn2, axis=0, keepdims=True)
    gmid = gy + norm_back(gn2, hat, inv, vec_ref[2:3, :])
    gmid_ref[...] = gmid
    gatt = gmid.astype(BF16)
    gatt_ref[...] = gatt
    sums_ref[2:3, :] += jnp.sum(gatt.astype(F32), axis=0, keepdims=True)
    sums_ref[3:4, :] += jnp.sum(gy, axis=0, keepdims=True)
    go_ref[...] = dot_nt(gatt, wo_ref[...]).astype(BF16)


def feed_back_call(gy, slope, middle, vec, wdt, wu, wo):
    return pl.pallas_call(
        feed_back_kernel,
        grid=(TILES,),
        in_specs=[rows_of(D), rows_of(FF), rows_of(D), whole(vec.shape), whole(wdt.shape), whole(wu.shape), whole(wo.shape)],
        out_specs=[rows_of(FF), rows_of(D), rows_of(D), rows_of(D), whole((8, D)), whole((8, FF))],
        out_shape=[
            jax.ShapeDtypeStruct((L, FF), BF16),
            jax.ShapeDtypeStruct((L, D), F32),
            jax.ShapeDtypeStruct((L, D), BF16),
            jax.ShapeDtypeStruct((L, D), BF16),
            jax.ShapeDtypeStruct((8, D), F32),
            jax.ShapeDtypeStruct((8, FF), F32),
        ],
        compiler_params=params(),
        cost_estimate=pl.CostEstimate(flops=2 * L * D * (2 * FF + D), bytes_accessed=35_000_000, transcendentals=0),
        name="feed_back",
    )(gy, slope, middle, vec, wdt, wu, wo)


def outer_kernel(left_ref, right_ref, out_ref, turned):
    @pl.when(pl.program_id(0) == 0)
    def _():
        turned[...] = left_ref[...].T

    out_ref[...] = dot_nn(turned[...], right_ref[...]).astype(BF16)


def outer_call(left, right, name):
    wide = right.shape[1]
    width = 768
    return pl.pallas_call(
        outer_kernel,
        grid=(wide // width,),
        in_specs=[whole(left.shape), pl.BlockSpec((L, width), lambda i: (0, i))],
        out_specs=pl.BlockSpec((D, width), lambda i: (0, i)),
        out_shape=jax.ShapeDtypeStruct((D, wide), BF16),
        scratch_shapes=[pltpu.VMEM((D, L), BF16)],
        compiler_params=params(),
        cost_estimate=pl.CostEstimate(flops=2 * L * D * wide, bytes_accessed=4 * L * D + 4 * D * wide, transcendentals=0),
        name=name,
    )(left, right)


def first_back_kernel(len_ref, lead_ref, x_ref, gmid_ref, g_ref, vec_ref, w_ref, out_ref, sums_ref, table_ref):
    step = pl.program_id(0)

    @pl.when(step == 0)
    def _():
        sums_ref[...] = jnp.zeros_like(sums_ref)
        table_ref[...] = jnp.zeros_like(table_ref)

    gn1 = dot_nt(g_ref[...], w_ref[...])
    hat, inv = norm_parts(x_ref[...].astype(F32))
    sums_ref[0:1, :] += jnp.sum(gn1 * hat, axis=0, keepdims=True)
    sums_ref[1:2, :] += jnp.sum(gn1, axis=0, keepdims=True)
    shape = (table_ref.shape[0], ROWS)
    places = step * ROWS + lax.broadcasted_iota(jnp.int32, shape, 1)
    hot = lead_of(places, bounds_of(len_ref), lead_ref) == lax.broadcasted_iota(jnp.int32, shape, 0)
    hot = hot.astype(BF16)
    high = gn1.astype(BF16)
    low = (gn1 - high.astype(F32)).astype(BF16)
    table_ref[...] += dot_nn(hot, high) + dot_nn(hot, low)
    out_ref[...] = gmid_ref[...] + norm_back(gn1, hat, inv, vec_ref[0:1, :])


def first_back_call(lengths, leads, x, gmid, gqkv, vec, w):
    return pl.pallas_call(
        first_back_kernel,
        grid=(TILES,),
        in_specs=[smem(), smem(), rows_of(D), rows_of(D), rows_of(3 * D), whole(vec.shape), whole(w.shape)],
        out_specs=[rows_of(D), whole((8, D)), whole((32, D))],
        out_shape=[
            jax.ShapeDtypeStruct((L, D), F32),
            jax.ShapeDtypeStruct((8, D), F32),
            jax.ShapeDtypeStruct((32, D), F32),
        ],
        compiler_params=params(),
        cost_estimate=pl.CostEstimate(flops=2 * L * D * 3 * D, bytes_accessed=17_000_000, transcendentals=0),
        name="first_back",
    )(lengths, leads, x, gmid, gqkv, vec, w)


def slots(found):
    return [
        (at, k, dp, fs + 2 * k)
        for at, (dp, fs, part) in enumerate(found)
        for k in range(part.shape[0])
    ]

def chunk_cols(chunk, wide):
    third = wide // 3
    return (2 * third, third) if chunk == 0 else (0, 2 * third)


def any_space():
    return pl.BlockSpec(memory_space=pl.ANY)


def in_vmem():
    return pl.BlockSpec(memory_space=pltpu.VMEM)


def kept(shape):
    return pl.BlockSpec(shape, lambda *_: (0,) * len(shape), pipeline_mode=pl.Buffered(1))


def pack_first(w_qkv, small):
    tall, cols = w_qkv.shape
    left = cols - 256
    fold = 128 // left
    rows = tall // fold
    rest = jnp.concatenate([w_qkv[k * rows:(k + 1) * rows, 256:] for k in range(fold)], axis=1)
    small = jnp.pad(small, ((0, 16 - small.shape[0]), (0, 128 - small.shape[1])))
    return jnp.concatenate([w_qkv[:, :128], w_qkv[:, 128:256], rest, small], axis=0)


def pack_chunk(chunk, w_up, w_down_t):
    wide = w_up.shape[1]
    start, count = chunk_cols(chunk, wide)
    parts = [w_up[:, start:start + count]]
    for k in range(w_down_t.shape[1] // wide):
        parts.append(w_down_t[:, k * wide + start:k * wide + start + count])
    return jnp.concatenate(parts, axis=0)


def fold_out(w_out):
    tall, narrow = w_out.shape
    rows = tall // 4
    wide = jnp.concatenate([w_out[k * rows:(k + 1) * rows] for k in range(4)], axis=1)
    return jnp.concatenate([wide[:, k * 128:(k + 1) * 128] for k in range(4 * narrow // 128)], axis=0)


def start_all(copies):
    for copy in copies:
        copy.start()
    for copy in copies:
        copy.wait()


def open_kernel(plan, count, ids_ref, len_ref, lead_ref, x_ref, *refs):
    parts = refs[:count]
    n1_ref, qkv_ref, w_ref, vec_ref, table_ref, bias0_ref, bias1_ref, stage, table, bias, sem = refs[count:]
    step = pl.program_id(0)
    dps, fss = stage.shape[0], stage.shape[1]
    tall, cols, narrow, wide = D // dps, 3 * D // fss, D // fss, FF // fss

    @pl.when(step == 0)
    def _():
        start_all([
            pltpu.make_async_copy(parts[at].at[k], stage.at[ids_ref[0] ^ dp, ids_ref[1] ^ fs], sem)
            for at, k, dp, fs in plan
        ])
        table[...] = jnp.zeros_like(table)
        left = cols - 256
        fold = 128 // left
        rows = tall // fold
        for d in range(dps):
            for f in range(fss):
                at = slice(d * tall, (d + 1) * tall)
                w_ref[at, f * cols:f * cols + 128] = stage[d, f, :tall]
                w_ref[at, f * cols + 128:f * cols + 256] = stage[d, f, tall:2 * tall]
                for k in range(fold):
                    w_ref[d * tall + k * rows:d * tall + (k + 1) * rows, f * cols + 256:(f + 1) * cols] = (
                        stage[d, f, 2 * tall:2 * tall + rows, k * left:(k + 1) * left]
                    )
                small = stage[d, f, 2 * tall + rows:, :narrow].astype(F32)
                at = slice(f * narrow, (f + 1) * narrow)
                vec_ref[2 * d:2 * d + 2, at] = small[0:2]
                table[5 * d:5 * d + 5, at] = small[2:7]
                bias[0:1, d * D + f * narrow:d * D + (f + 1) * narrow] = small[7:8]
        table_ref[...] = table[...].astype(BF16)
        for chunk, ref in ((0, bias0_ref), (1, bias1_ref)):
            start, many = chunk_cols(chunk, wide)
            for f in range(fss):
                ref[:, f * many:(f + 1) * many] = bias[:, f * wide + start:f * wide + start + many]

    qkv_tile(step, len_ref, lead_ref, x_ref, vec_ref, table_ref, w_ref, n1_ref, qkv_ref)


def qkv_tile(step, len_ref, lead_ref, x_ref, vec_ref, table_ref, w_ref, n1_ref, qkv_ref):
    bounds = bounds_of(len_ref)
    hat, _ = norm_parts(x_ref[...].astype(F32))
    normed = hat * (1.0 + vec_ref[0:1, :]) + vec_ref[1:2, :]
    shape = (ROWS, table_ref.shape[0])
    places = step * ROWS + lax.broadcasted_iota(jnp.int32, shape, 0)
    hot = lead_of(places, bounds, lead_ref) == lax.broadcasted_iota(jnp.int32, shape, 1)
    n1 = (normed + dot_nn(hot.astype(BF16), table_ref[...])).astype(BF16)
    n1_ref[...] = n1
    for third in range(3):
        cols = slice(third * D, (third + 1) * D)
        part = dot_nn(n1, w_ref[:, cols])
        if third == 0:
            part = (part + vec_ref[4:5, :]).astype(BF16) * jnp.asarray(SCALE, BF16)
        elif third == 2:
            part = part + vec_ref[5:6, :]
        qkv_ref[:, cols] = part.astype(BF16)


def open_call(found, ids, lengths, leads, x, sizes):
    parts = [part for _, _, part in found]
    rows = parts[0].shape[1]
    dps, fss = sizes
    sides = [fss * chunk_cols(chunk, FF // fss)[1] for chunk in range(2)]
    shapes = [((L, D), BF16), ((L, 3 * D), BF16), ((D, 3 * D), BF16), ((8, D), F32), ((32, D), BF16)]
    shapes += [((1, side), F32) for side in sides]
    return pl.pallas_call(
        functools.partial(open_kernel, slots(found), len(parts)),
        grid=(TILES,),
        in_specs=[smem(), smem(), smem(), rows_of(D)] + [any_space()] * len(parts),
        out_specs=[rows_of(D), rows_of(3 * D)] + [kept(shape) for shape, _ in shapes[2:]],
        out_shape=[jax.ShapeDtypeStruct(shape, kind) for shape, kind in shapes],
        scratch_shapes=[
            pltpu.VMEM((dps, fss, rows, 128), BF16),
            pltpu.VMEM((32, D), F32),
            pltpu.VMEM((1, FF), F32),
            pltpu.SemaphoreType.DMA,
        ],
        compiler_params=params(),
        cost_estimate=pl.CostEstimate(flops=2 * L * D * 3 * D, bytes_accessed=18_000_000, transcendentals=0),
        name="open",
    )(ids, lengths, leads, x, *parts)


def chunk_copies(plan, ids_ref, parts, wu, wd, stage, sem, sizes):
    dps, fss = sizes
    tall, thin = D // dps, D // fss
    many = wu.shape[1] // fss
    copies = []
    for at, k, dp, fs in plan:
        d, f = ids_ref[0] ^ dp, ids_ref[1] ^ fs
        part = parts[at]

        def place(ref, row, rows, col):
            return ref.at[pl.ds(pl.multiple_of(row, 16), rows), pl.ds(pl.multiple_of(col, 128), many)]

        copies.append(pltpu.make_async_copy(part.at[k, pl.ds(0, tall), :], place(wu, d * tall, tall, f * many), sem))
        for side in range(fss // dps):
            rows = part.at[k, pl.ds(tall + side * thin, thin), :]
            copies.append(pltpu.make_async_copy(rows, place(wd, f * thin, thin, (d * (fss // dps) + side) * many), sem))
        if stage is not None:
            rows = part.at[k, pl.ds(tall + fss // dps * thin, stage.shape[2]), :]
            copies.append(pltpu.make_async_copy(rows, stage.at[d, f], sem))
    return copies


def unfold_out(stage, wo, sizes):
    dps, fss = sizes
    tall, thin = D // dps, D // fss
    rows = tall // 4
    for d in range(dps):
        for f in range(fss):
            flat = jnp.concatenate([stage[d, f, k * rows:(k + 1) * rows] for k in range(thin * 4 // 128)], axis=1)
            for k in range(4):
                wo[d * tall + k * rows:d * tall + (k + 1) * rows, f * thin:(f + 1) * thin] = flat[:, k * thin:(k + 1) * thin]


def start(copies):
    for copy in copies:
        copy.start()


def wait(copies):
    for copy in copies:
        copy.wait()


def turn(ref, plain, ordered, mine, count):
    plain[...] = ref[...].T
    tall = ordered.shape[0] // count
    for k in range(count):
        at = pl.multiple_of((mine ^ k) * tall, tall)
        ordered[k * tall:(k + 1) * tall, :] = plain[pl.ds(at, tall), :]


def gate_pair(h):
    cdf = 0.5 + 0.5 * lax.erf(h * 0.7071067811865476)
    return h * cdf, cdf + h * (0.3989422804014327 * jnp.exp(h * h * -0.5))


def norm_back(grad, hat, inv, gain):
    scaled = grad * (1.0 + gain)
    both = jnp.mean(scaled * hat, axis=-1, keepdims=True)
    return inv * (scaled - jnp.mean(scaled, axis=-1, keepdims=True) - hat * both)


def feed_step(step, gm_ref, n2, n2_t, gm_t, wu, wd, bias, a_ref, bup_ref, gh, gn2, grads, ids_ref, sizes):
    dps, fss = sizes
    pair = fss // dps
    width = a_ref.shape[1]
    many = width // pair
    tall, thin = D // dps, D // fss
    block = step ^ (ids_ref[1] // pair)
    cols = pl.ds(pl.multiple_of(block * width, width), width)
    own_u, own_d = wu[:, cols], wd[:, cols]
    shift = bias[:, cols]
    bup = jnp.zeros((1, width), F32)
    for r in range(TILES):
        rows = slice(r * ROWS, (r + 1) * ROWS)
        act, slope = gate_pair(dot_nn(n2[rows, :], own_u) + shift)
        a_ref[rows, :] = act.astype(BF16)
        part = (dot_nn(gm_ref[rows, :], own_d) * slope).astype(BF16)
        gh[rows, :] = part
        bup = bup + jnp.sum(part.astype(F32), axis=0, keepdims=True)
        gn2[rows, :] += dot_nt(part, own_u)
    bup_ref[:, cols] = bup
    grad = dot_nn(gm_t[...], a_ref[...]).astype(BF16)
    d = block ^ ids_ref[0]
    for f in range(fss):
        for side in range(pair):
            at = tall + side * thin
            grads[d & 1, d >> 1, f & 1, f >> 1, at:at + thin, :] = grad[f * thin:(f + 1) * thin, side * many:(side + 1) * many]
    grad = dot_nn(n2_t[...], gh[...]).astype(BF16)
    for side in range(pair):
        y = (ids_ref[1] & 1) ^ side
        for d in range(dps):
            grads[d & 1, d >> 1, y, step, :tall, :] = grad[d * tall:(d + 1) * tall, side * many:(side + 1) * many]


def up_copies(step, grads, mine_ref, theirs_ref, tall, sem):
    return [
        pltpu.make_async_copy(grads.at[c, :, :, step, pl.ds(0, tall), :], ref.at[:, :, step, pl.ds(0, tall), :], sem)
        for c, ref in ((0, mine_ref), (1, theirs_ref))
    ]


def down_copy(c, x, grads, ref, tall, sem):
    return pltpu.make_async_copy(
        grads.at[c, x, :, :, pl.ds(tall, tall), :], ref.at[x, :, :, pl.ds(tall, tall), :], sem
    )


def send_grads(step, ids_ref, grads, mine_ref, theirs_ref, up_sem, down_sem, sizes):
    tall = D // sizes[0]
    start(up_copies(step, grads, mine_ref, theirs_ref, tall, up_sem))
    away = step ^ (ids_ref[1] // (sizes[1] // sizes[0])) ^ ids_ref[0]
    for c, ref in ((0, mine_ref), (1, theirs_ref)):
        @pl.when((away & 1) == c)
        def _(c=c, ref=ref):
            down_copy(c, away >> 1, grads, ref, tall, down_sem).start()


def wait_grads(grads, mine_ref, theirs_ref, up_sem, down_sem, sizes):
    tall = D // sizes[0]
    for step in range(sizes[0]):
        wait(up_copies(step, grads, mine_ref, theirs_ref, tall, up_sem))
        down_copy(0, 0, grads, mine_ref, tall, down_sem).wait()


def feed_first_kernel(plan, count, sizes, ids_ref, vec_ref, bias_ref, o_hbm, x_hbm, gm_hbm, *refs):
    parts = refs[:count]
    (a_ref, bup_ref, mid_hbm, n2_hbm, gn2_hbm, wd_hbm, wo_hbm, mine_ref, theirs_ref,
     o, x, gm, mid, n2, gn2, wd, wo, wu, stage, plain, n2_t, gm_t, gh, grads, sems) = refs[count:]
    step = pl.program_id(0)
    outs = [
        pltpu.make_async_copy(src, dst, sems.at[4 + k])
        for k, (src, dst) in enumerate(((wd, wd_hbm), (wo, wo_hbm), (mid, mid_hbm), (n2, n2_hbm), (gn2, gn2_hbm)))
    ]

    @pl.when(step == 0)
    def _():
        ins = [pltpu.make_async_copy(src, dst, sems.at[1 + k]) for k, (src, dst) in enumerate(((gm_hbm, gm), (o_hbm, o), (x_hbm, x)))]
        lay = chunk_copies(plan, ids_ref, parts, wu, wd, stage, sems.at[0], sizes)
        start(ins[:1] + lay + ins[1:])
        ins[0].wait()
        turn(gm, plain, gm_t, ids_ref[1], sizes[1])
        gn2[...] = jnp.zeros_like(gn2)
        wait(lay)
        unfold_out(stage, wo, sizes)
        start(outs[:2])
        wait(ins[1:])
        for r in range(TILES):
            rows = slice(r * ROWS, (r + 1) * ROWS)
            middle = x[rows, :].astype(F32) + (dot_nn(o[rows, :], wo[...]) + vec_ref[6:7, :])
            mid[rows, :] = middle
            hat, _ = norm_parts(middle)
            n2[rows, :] = (hat * (1.0 + vec_ref[2:3, :]) + vec_ref[3:4, :]).astype(BF16)
        start(outs[2:4])
        turn(n2, plain, n2_t, ids_ref[0], sizes[0])

    feed_step(step, gm, n2, n2_t, gm_t, wu, wd, bias_ref, a_ref, bup_ref, gh, gn2, grads, ids_ref, sizes)
    send_grads(step, ids_ref, grads, mine_ref, theirs_ref, sems.at[9], sems.at[10], sizes)

    @pl.when(step == pl.num_programs(0) - 1)
    def _():
        outs[4].start()
        wait_grads(grads, mine_ref, theirs_ref, sems.at[9], sems.at[10], sizes)
        wait(outs)


def feed_first(found, ids, o, x, gm, vec, bias, sizes):
    parts = [part for _, _, part in found]
    dps, fss = sizes
    units = bias.shape[1]
    width, many = units // dps, units // fss
    rows = 2 * (D // dps)
    shape = (dps // 2, 2, fss // 2, rows, many)
    outs = [
        ((L, units), BF16), ((1, units), F32), ((L, D), F32), ((L, D), BF16), ((L, D), F32), ((D, units), BF16), ((D, D), BF16),
        (shape, BF16), (shape, BF16),
    ]
    return pl.pallas_call(
        functools.partial(feed_first_kernel, slots(found), len(parts), sizes),
        grid_spec=pltpu.PrefetchScalarGridSpec(
            num_scalar_prefetch=1,
            grid=(dps,),
            in_specs=[kept((8, D)), kept((1, units))] + [any_space()] * (3 + len(parts)),
            out_specs=[pl.BlockSpec((L, width), lambda i, ids: (0, i ^ (ids[1] // (fss // dps)))), kept((1, units))]
            + [any_space()] * 7,
            scratch_shapes=[
                pltpu.VMEM((L, D), BF16),
                pltpu.VMEM((L, D), BF16),
                pltpu.VMEM((L, D), BF16),
                pltpu.VMEM((L, D), F32),
                pltpu.VMEM((L, D), BF16),
                pltpu.VMEM((L, D), F32),
                pltpu.VMEM((D, units), BF16),
                pltpu.VMEM((D, D), BF16),
                pltpu.VMEM((D, units), BF16),
                pltpu.VMEM((dps, fss, parts[0].shape[1] - rows, 128), BF16),
                pltpu.VMEM((D, L), BF16),
                pltpu.VMEM((D, L), BF16),
                pltpu.VMEM((D, L), BF16),
                pltpu.VMEM((L, width), BF16),
                pltpu.VMEM((2,) + shape, BF16),
                pltpu.SemaphoreType.DMA((11,)),
            ],
        ),
        out_shape=[jax.ShapeDtypeStruct(s, kind) for s, kind in outs],
        compiler_params=params(),
        cost_estimate=pl.CostEstimate(flops=2 * L * D * (5 * units + D), bytes_accessed=30_000_000, transcendentals=2 * L * units),
        name="feed_first",
    )(ids, vec, bias, o, x, gm, *parts)


def feed_second_kernel(plan, count, sizes, ids_ref, vec_ref, bias_ref, o_hbm, n2_hbm, gm_hbm, mid_hbm, gn2_hbm, wo_hbm, *refs):
    parts = refs[:count]
    (a_ref, bup_ref, sums_ref, wd_hbm, gmid_hbm, go_hbm, mine_ref, theirs_ref,
     o, n2, gm, mid, gn2, wo, wd, wu, plain, n2_t, gm_t, gh, gatt, full, grads, sems) = refs[count:]
    step = pl.program_id(0)
    dps, fss = sizes
    tall, thin = D // dps, D // fss
    ins = [
        pltpu.make_async_copy(src, dst, sems.at[k])
        for k, (src, dst) in enumerate(((gm_hbm, gm), (n2_hbm, n2), (gn2_hbm, gn2), (o_hbm, o), (mid_hbm, mid), (wo_hbm, wo)))
    ]
    wd_out = pltpu.make_async_copy(wd, wd_hbm, sems.at[7])

    @pl.when(step == 0)
    def _():
        lay = chunk_copies(plan, ids_ref, parts, wu, wd, None, sems.at[6], sizes)
        start(ins[:2] + lay + ins[2:])
        ins[0].wait()
        turn(gm, plain, gm_t, ids_ref[1], fss)
        ins[1].wait()
        turn(n2, plain, n2_t, ids_ref[0], dps)
        wait(lay)
        wd_out.start()
        ins[2].wait()

    feed_step(step, gm, n2, n2_t, gm_t, wu, wd, bias_ref, a_ref, bup_ref, gh, gn2, grads, ids_ref, sizes)
    send_grads(step, ids_ref, grads, mine_ref, theirs_ref, sems.at[8], sems.at[9], sizes)

    @pl.when(step == pl.num_programs(0) - 1)
    def _():
        wait(ins[3:])
        turn(o, plain, n2_t, ids_ref[0], dps)
        sums = [jnp.zeros((1, D), F32)] * 4
        outs = []
        for r in range(TILES):
            rows = slice(r * ROWS, (r + 1) * ROWS)
            grad, gy = gn2[rows, :], gm[rows, :].astype(F32)
            hat, inv = norm_parts(mid[rows, :])
            gmid = gy + norm_back(grad, hat, inv, vec_ref[2:3, :])
            mid[rows, :] = gmid
            low = gmid.astype(BF16)
            gatt[rows, :] = low
            n2[rows, :] = dot_nt(low, wo[...]).astype(BF16)
            for k, term in enumerate((grad * hat, grad, low.astype(F32), gy)):
                sums[k] = sums[k] + jnp.sum(term, axis=0, keepdims=True)
        outs = [pltpu.make_async_copy(mid, gmid_hbm, sems.at[10]), pltpu.make_async_copy(n2, go_hbm, sems.at[11])]
        start(outs)
        sums_ref[...] = jnp.concatenate(sums + [jnp.zeros((4, D), F32)], axis=0)
        full[...] = dot_nn(n2_t[...], gatt[...]).astype(BF16)
        for f in range(fss):
            flip = ids_ref[1] ^ f
            for d in range(dps):
                for k in range(2):
                    at = 2 * tall
                    grads[d & 1, d >> 1, flip & 1, flip >> 1, at:at + tall // 2, k * thin:(k + 1) * thin] = (
                        full[d * tall + k * (tall // 2):d * tall + (k + 1) * (tall // 2), f * thin:(f + 1) * thin]
                    )
                grads[d & 1, d >> 1, flip & 1, flip >> 1, 2 * tall:, 2 * thin:] = jnp.zeros(
                    (tall // 2, grads.shape[5] - 2 * thin), BF16
                )
        rows = pl.ds(2 * tall, tall // 2)
        rest = [
            pltpu.make_async_copy(grads.at[c, :, :, :, rows, :], ref.at[:, :, :, rows, :], sems.at[12])
            for c, ref in ((0, mine_ref), (1, theirs_ref))
        ]
        start(rest)
        wait_grads(grads, mine_ref, theirs_ref, sems.at[8], sems.at[9], sizes)
        wait(rest + outs + [wd_out])


def feed_second(found, ids, o, n2, gm, mid, gn2, vec, bias, wo, sizes):
    parts = [part for _, _, part in found]
    dps, fss = sizes
    units = bias.shape[1]
    width, many = units // dps, units // fss
    tall = D // dps
    shape = (dps // 2, 2, fss // 2, 2 * tall + tall // 2, many)
    outs = [
        ((L, units), BF16), ((1, units), F32), ((8, D), F32), ((D, units), BF16), ((L, D), F32), ((L, D), BF16),
        (shape, BF16), (shape, BF16),
    ]
    return pl.pallas_call(
        functools.partial(feed_second_kernel, slots(found), len(parts), sizes),
        grid_spec=pltpu.PrefetchScalarGridSpec(
            num_scalar_prefetch=1,
            grid=(dps,),
            in_specs=[kept((8, D)), kept((1, units))] + [any_space()] * (6 + len(parts)),
            out_specs=[
                pl.BlockSpec((L, width), lambda i, ids: (0, i ^ (ids[1] // (fss // dps)))), kept((1, units)), kept((8, D)),
            ] + [any_space()] * 5,
            scratch_shapes=[
                pltpu.VMEM((L, D), BF16),
                pltpu.VMEM((L, D), BF16),
                pltpu.VMEM((L, D), BF16),
                pltpu.VMEM((L, D), F32),
                pltpu.VMEM((L, D), F32),
                pltpu.VMEM((D, D), BF16),
                pltpu.VMEM((D, units), BF16),
                pltpu.VMEM((D, units), BF16),
                pltpu.VMEM((D, L), BF16),
                pltpu.VMEM((D, L), BF16),
                pltpu.VMEM((D, L), BF16),
                pltpu.VMEM((L, width), BF16),
                pltpu.VMEM((L, D), BF16),
                pltpu.VMEM((D, D), BF16),
                pltpu.VMEM((2,) + shape, BF16),
                pltpu.SemaphoreType.DMA((13,)),
            ],
        ),
        out_shape=[jax.ShapeDtypeStruct(s, kind) for s, kind in outs],
        compiler_params=params(),
        cost_estimate=pl.CostEstimate(flops=2 * L * D * (5 * units + 2 * D), bytes_accessed=35_000_000, transcendentals=2 * L * units),
        name="feed_second",
    )(ids, vec, bias, o, n2, gm, mid, gn2, wo, *parts)


def last_kernel(a0_ref, a1_ref, mid_ref, vec_ref, w0_ref, w1_ref, y_ref):
    total = dot_nt(a0_ref[...], w0_ref[...]) + dot_nt(a1_ref[...], w1_ref[...])
    y_ref[...] = (mid_ref[...] + (total + vec_ref[7:8, :])).astype(BF16)


def last_call(a0, a1, middle, vec, w0, w1):
    return pl.pallas_call(
        last_kernel,
        grid=(TILES,),
        in_specs=[rows_of(a0.shape[1]), rows_of(a1.shape[1]), rows_of(D), kept((8, D)), kept(w0.shape), kept(w1.shape)],
        out_specs=rows_of(D),
        out_shape=jax.ShapeDtypeStruct((L, D), BF16),
        compiler_params=params(),
        cost_estimate=pl.CostEstimate(flops=2 * L * D * FF, bytes_accessed=17_000_000, transcendentals=0),
        name="feed_down",
    )(a0, a1, middle, vec, w0, w1)


def close_kernel(sizes, ids_ref, len_ref, lead_ref, vec_ref, sums_ref, qsums0_ref, qsums1_ref, bup0_ref, bup1_ref,
                 x_hbm, gmid_hbm, n1_hbm, g0_hbm, g1_hbm, w_hbm, gx_hbm, mine_ref, theirs_ref,
                 x, gmid, n1, g, w, plain, left, full, table, grads, sems):
    dps, fss = sizes
    tall, cols, thin, wide = D // dps, 3 * D // fss, D // fss, FF // fss
    ins = [
        pltpu.make_async_copy(src, dst, sems.at[k])
        for k, (src, dst) in enumerate(((n1_hbm, n1), (w_hbm, w), (x_hbm, x), (gmid_hbm, gmid)))
    ]
    joins = []
    for third in range(3):
        at = third * D
        for src in (g0_hbm, g1_hbm):
            part = src.shape[1] // 3
            joins.append(
                pltpu.make_async_copy(src.at[:, third * part:(third + 1) * part], g.at[:, at:at + part], sems.at[4])
            )
            at += part
    start(ins[:1] + joins + ins[1:])
    ins[0].wait()
    turn(n1, plain, left, ids_ref[0], dps)
    wait(joins)
    rest = cols - 256
    fold = 128 // rest
    some = tall // fold
    for third in range(3):
        at = slice(third * D, (third + 1) * D)
        full[:, at] = dot_nn(left[...], g[:, at]).astype(BF16)
    for f in range(fss):
        flip = ids_ref[1] ^ f
        y, z = flip & 1, flip >> 1
        for d in range(dps):
            own = slice(d * tall, (d + 1) * tall)
            c, away = d & 1, d >> 1
            grads[c, away, y, z, 0:tall, :] = full[own, f * cols:f * cols + 128]
            grads[c, away, y, z, tall:2 * tall, :] = full[own, f * cols + 128:f * cols + 256]
            for k in range(fold):
                grads[c, away, y, z, 2 * tall:2 * tall + some, k * rest:(k + 1) * rest] = (
                    full[d * tall + k * some:d * tall + (k + 1) * some, f * cols + 256:(f + 1) * cols]
                )
    big, little = pl.ds(0, 2 * tall + some), pl.ds(2 * tall + some, 16)
    sends = [
        [
            pltpu.make_async_copy(grads.at[c, :, :, :, rows, :], ref.at[:, :, :, rows, :], sems.at[at])
            for c, ref in ((0, mine_ref), (1, theirs_ref))
        ]
        for at, rows in ((5, big), (6, little))
    ]
    start(sends[0])
    wait(ins[1:])
    gain, shift = jnp.zeros((1, D), F32), jnp.zeros((1, D), F32)
    table[...] = jnp.zeros_like(table)
    bounds = bounds_of(len_ref)
    outs = []
    for r in range(TILES):
        rows = slice(r * ROWS, (r + 1) * ROWS)
        grad = dot_nt(g[rows, :], w[...])
        hat, inv = norm_parts(x[rows, :].astype(F32))
        gain = gain + jnp.sum(grad * hat, axis=0, keepdims=True)
        shift = shift + jnp.sum(grad, axis=0, keepdims=True)
        shape = (table.shape[0], ROWS)
        places = r * ROWS + lax.broadcasted_iota(jnp.int32, shape, 1)
        hot = lead_of(places, bounds, lead_ref) == lax.broadcasted_iota(jnp.int32, shape, 0)
        hot = hot.astype(BF16)
        high = grad.astype(BF16)
        low = (grad - high.astype(F32)).astype(BF16)
        table[...] += dot_nn(hot, high) + dot_nn(hot, low)
        gmid[rows, :] += norm_back(grad, hat, inv, vec_ref[0:1, :])
    out = pltpu.make_async_copy(gmid, gx_hbm, sems.at[7])
    out.start()
    bup = []
    for f in range(fss):
        for chunk, ref in ((1, bup1_ref), (0, bup0_ref)):
            many = chunk_cols(chunk, wide)[1]
            bup.append(ref[:, f * many:(f + 1) * many])
    bup = jnp.concatenate(bup, axis=1)
    qsums = jnp.concatenate([qsums0_ref[0:2, :], qsums1_ref[0:2, :]], axis=1)
    gvec = [gain, shift, sums_ref[0:1, :], sums_ref[1:2, :], qsums[0:1, :], qsums[1:2, :], sums_ref[2:3, :], sums_ref[3:4, :]]
    for d in range(dps):
        small = jnp.concatenate(
            gvec[2 * d:2 * d + 2] + [table[5 * d:5 * d + 5, :], bup[:, d * D:(d + 1) * D], jnp.zeros((8, D), F32)], axis=0
        )
        away = ids_ref[0] ^ d
        for f in range(fss):
            flip = ids_ref[1] ^ f
            part = jnp.concatenate([small[:, f * thin:(f + 1) * thin], jnp.zeros((16, 128 - thin), F32)], axis=1)
            grads[away & 1, away >> 1, flip & 1, flip >> 1, 2 * tall + some:, :] = part.astype(BF16)
    start(sends[1])
    wait(sends[0] + sends[1] + [out])


def close_call(ids, lengths, leads, x, gmid, n1, back0, back1, vec, w, sums, bup0, bup1, sizes):
    dps, fss = sizes
    tall = D // dps
    rows = 2 * tall + tall // (128 // (3 * D // fss - 256)) + 16
    shape = (dps // 2, 2, fss // 2, rows, 128)
    return pl.pallas_call(
        functools.partial(close_kernel, sizes),
        in_specs=[smem()] * 3 + [in_vmem()] * 6 + [any_space()] * 6,
        out_specs=[any_space()] * 3,
        out_shape=[jax.ShapeDtypeStruct((L, D), F32), jax.ShapeDtypeStruct(shape, BF16), jax.ShapeDtypeStruct(shape, BF16)],
        scratch_shapes=[
            pltpu.VMEM((L, D), BF16),
            pltpu.VMEM((L, D), F32),
            pltpu.VMEM((L, D), BF16),
            pltpu.VMEM((L, 3 * D), BF16),
            pltpu.VMEM((D, 3 * D), BF16),
            pltpu.VMEM((D, L), BF16),
            pltpu.VMEM((D, L), BF16),
            pltpu.VMEM((D, 3 * D), BF16),
            pltpu.VMEM((32, D), F32),
            pltpu.VMEM((2,) + shape, BF16),
            pltpu.SemaphoreType.DMA((8,)),
        ],
        compiler_params=params(),
        cost_estimate=pl.CostEstimate(flops=4 * L * D * 3 * D, bytes_accessed=25_000_000, transcendentals=0),
        name="close",
    )(ids, lengths, leads, vec, sums, back0[1], back1[1], bup0, bup1, x, gmid, n1, back0[0], back1[0], w)


def hop_dp(value, flip, ranks):
    return lax.ppermute(value, "dp", [(i, i ^ flip) for i in range(ranks)])


def hop_fsdp(value, flip, ranks):
    return lax.ppermute(value, "fsdp", [(i, i ^ flip) for i in range(ranks)])


def tie(values, *others):
    flat, tree = jax.tree.flatten(values)
    more = jax.tree.leaves(others)
    done = lax.optimization_barrier(tuple(flat) + tuple(more))
    return jax.tree.unflatten(tree, done[:len(flat)])


def gather_depth(piece, sizes):
    return [piece] + [hop_fsdp(piece, 2 * z, sizes[1]) for z in range(1, sizes[1] // 2)]


def gather_far(piece, sizes):
    return jnp.stack([piece, hop_fsdp(piece, sizes[1] // 2, sizes[1])])


def gather_near(pair, sizes):
    other = hop_fsdp(pair, sizes[1] // 4, sizes[1])
    return jnp.stack([pair[0], other[0], pair[1], other[1]])


def gather_sides(column, sizes):
    return hop_dp(column, 2, sizes[0]), hop_fsdp(column, 1, sizes[1])


def gather_corner(sides, sizes):
    by_x, by_y = sides
    half = by_x.shape[0] // 2
    return hop_fsdp(by_x[:half], 1, sizes[1]), hop_dp(by_y[half:], 2, sizes[0])


def cross(parts, sizes):
    return [hop_dp(part, 1, sizes[0]) for part in parts]


def name_parts(parts, others):
    half = parts[0].shape[0] // 2
    flips = ((0, 0), (2, 0), (0, 1), (2, 1), (2, 1 + 2 * half))
    own = [(dp, fs, part) for (dp, fs), part in zip(flips, parts)]
    return own + [(dp | 1, fs, part) for (dp, fs), part in zip(flips, others)]


def plus(*terms):
    return sum(term.astype(F32) for term in terms)


def reduce_core(mine, theirs, sizes):
    return mine, hop_dp(theirs, 1, sizes[0])


def reduce_sides(cored, sizes):
    both = plus(*cored).astype(BF16)
    half = both.shape[2] // 2
    first, second = both[:, :, :half], both[:, :, half:]
    got = hop_dp(first[1], 2, sizes[0]), hop_fsdp(second[:, 1], 1, sizes[1])
    return first[0], second[:, 0], got


def reduce_corner(sided, sizes):
    first, second, got = sided
    first, second = plus(first, got[0]).astype(BF16), plus(second, got[1]).astype(BF16)
    got = hop_fsdp(first[1], 1, sizes[1]), hop_dp(second[1], 2, sizes[0])
    return first[0], second[0], got


def reduce_near(cornered, sizes):
    first, second, got = cornered
    first, second = plus(first, got[0]).astype(BF16), plus(second, got[1]).astype(BF16)
    gone = hop_fsdp(jnp.stack([first[1], second[1]]), sizes[1] // 4, sizes[1])
    return first[0], second[0], gone


def reduce_far(neared, sizes):
    first, second, got = neared
    return first, got[0], hop_fsdp(plus(second, got[1]).astype(BF16), sizes[1] // 2, sizes[1])


def reduce_depth(cornered, sizes):
    first, second, got = cornered
    first, second = plus(first, got[0]).astype(BF16), plus(second, got[1]).astype(BF16)
    apart = [first[k] for k in range(first.shape[0])] + [second[k] for k in range(second.shape[0])]
    return [apart[0]] + [hop_fsdp(apart[z], 2 * z, sizes[1]) for z in range(1, len(apart))]


def per_device(sizes, tokens, lengths, lead_index, cotangent, w_qkv, w_out, w_up, w_down, vectors, lead_table, up_bias):
    dps, fss = sizes
    ids = jnp.stack([lax.axis_index("dp"), lax.axis_index("fsdp")]).astype(jnp.int32)
    thin, wide, tall = D // fss, FF // fss, D // dps
    x, gy = tokens.reshape(L, D), cotangent.reshape(L, D)

    piece0 = pack_first(w_qkv, jnp.concatenate([vectors, lead_table, up_bias], axis=0))
    w_down_t = w_down.T
    piece1 = jnp.concatenate([pack_chunk(0, w_up, w_down_t), fold_out(w_out)], axis=0)
    piece2 = pack_chunk(1, w_up, w_down_t)

    depth0 = gather_depth(piece0, sizes)
    depth0, piece1 = tie((depth0, piece1))
    column0 = jnp.stack(depth0)
    sides0, far1, other0 = gather_sides(column0, sizes), gather_far(piece1, sizes), cross((column0,), sizes)
    column0, sides0, other0, far1, piece2 = tie((column0, sides0, other0, far1, piece2))
    corner0, across0, column1 = gather_corner(sides0, sizes), cross(sides0, sizes), gather_near(far1, sizes)
    column0, sides0, corner0, other0, across0, column1, piece2 = tie(
        (column0, sides0, corner0, other0, across0, column1, piece2)
    )
    last0 = cross(corner0, sizes)
    last0, column1, piece2 = tie((last0, column1, piece2))

    sides1, depth2 = gather_sides(column1, sizes), gather_depth(piece2, sizes)
    found = name_parts((column0,) + sides0 + corner0, other0 + across0 + last0)
    opened = open_call(found, ids, lengths, lead_index, x, sizes)
    column1, sides1, depth2, opened = tie((column1, sides1, depth2, opened))
    n1, qkv, w_qkv, vec, table, bias0, bias1 = opened

    column2 = jnp.stack(depth2)
    corner1, other1, sides2 = gather_corner(sides1, sizes), cross((column1,), sizes), gather_sides(column2, sizes)
    attended = attend_call(lengths, qkv)
    column1, sides1, corner1, other1, column2, sides2, attended = tie(
        (column1, sides1, corner1, other1, column2, sides2, attended)
    )
    o, lse = attended

    last1 = cross(sides1 + corner1, sizes)
    last1, column2, sides2 = tie((last1, column2, sides2))

    corner2, other2 = gather_corner(sides2, sizes), cross((column2,) + sides2, sizes)
    found = name_parts((column1,) + sides1 + corner1, other1 + last1)
    first = feed_first(found, ids, o, x, gy, vec, bias0, sizes)
    column2, sides2, corner2, other2, first = tie((column2, sides2, corner2, other2, first))
    a0, bup0, middle, n2, gn2, wd0, w_out, mine0, theirs0 = first

    last2 = cross(corner2, sizes)
    last2, theirs0 = tie((last2, theirs0))

    grads0 = reduce_core(mine0, theirs0, sizes)
    found = name_parts((column2,) + sides2 + corner2, other2 + last2)
    second = feed_second(found, ids, o, n2, gy, middle, gn2, vec, bias1, w_out, sizes)
    grads0, second = tie((grads0, second))
    a1, bup1, sums, wd1, gmid, go, mine1, theirs1 = second

    grads0, grads1 = reduce_sides(grads0, sizes), reduce_core(mine1, theirs1, sizes)
    back0 = attend_back_call(lengths, qkv, o, go, lse, 0, 2)
    grads0, grads1, back0, go = tie((grads0, grads1, back0, go))

    grads0, grads1 = reduce_corner(grads0, sizes), reduce_sides(grads1, sizes)
    back1 = attend_back_call(lengths, qkv, o, go, lse, 2, PAIRS - 2)
    grads0, grads1, back0, back1 = tie((grads0, grads1, back0, back1))

    grads0, grads1 = reduce_near(grads0, sizes), reduce_corner(grads1, sizes)
    closed = close_call(
        ids, lengths, lead_index, x, gmid, n1, back0, back1, vec, w_qkv, sums, bup0, bup1, sizes
    )
    grads0, grads1, closed, a0 = tie((grads0, grads1, closed, a0))
    gx, mine2, theirs2 = closed

    grads2 = reduce_core(mine2, theirs2, sizes)
    grads2, a0 = tie((grads2, a0))
    grads0, grads1, grads2 = reduce_far(grads0, sizes), reduce_near(grads1, sizes), reduce_sides(grads2, sizes)
    y = last_call(a0, a1, middle, vec, wd0, wd1)
    grads0, grads1, grads2, y = tie((grads0, grads1, grads2, y))
    grads1, grads2 = reduce_far(grads1, sizes), reduce_corner(grads2, sizes)
    grads2 = reduce_depth(grads2, sizes)
    got0, got1, got2 = plus(*grads0), plus(*grads1), plus(*grads2)

    many = wide // 3
    up = jnp.concatenate([got1[:tall], got0[:tall]], axis=1)
    down = []
    for side in range(fss // dps):
        rows = slice(tall + side * thin, tall + (side + 1) * thin)
        down += [got1[rows], got0[rows]]
    down = jnp.concatenate(down, axis=1).T
    out = jnp.concatenate([got1[2 * tall:, :thin], got1[2 * tall:, thin:2 * thin]], axis=0)
    rest = 3 * thin - 256
    fold = 128 // rest
    some = tall // fold
    tail = got2[2 * tall:2 * tall + some]
    tail = jnp.concatenate([tail[:, k * rest:(k + 1) * rest] for k in range(fold)], axis=0)
    qkv_grad = jnp.concatenate([got2[:tall], got2[tall:2 * tall], tail], axis=1)
    small = got2[2 * tall + some:, :thin]
    return (
        y.reshape(1, L, D), gx.reshape(1, L, D), qkv_grad, out, up, down, small[0:2], small[2:7], small[7:8],
    )


def per_device_plain(sizes, tokens, lengths, lead_index, cotangent, w_qkv, w_out, w_up, w_down, vectors, table, bias):
    def full(shard):
        return lax.all_gather(lax.all_gather(shard, "fsdp", axis=1, tiled=True), "dp", axis=0, tiled=True)

    def share(grad):
        part = lax.psum_scatter(grad.astype(F32), "fsdp", scatter_dimension=1, tiled=True)
        return lax.psum_scatter(part, "dp", scatter_dimension=0, tiled=True)

    x, gy = tokens.reshape(L, D), cotangent.reshape(L, D)
    w_qkv, w_out, w_up, w_down_t = full(w_qkv), full(w_out), full(w_up), full(w_down).T
    vec, bias = full(vectors).astype(F32), full(bias).astype(F32).reshape(1, FF)
    table = jnp.pad(full(table), ((0, 32 - LEADS), (0, 0)))
    n1, qkv = qkv_call(lengths, lead_index, x, vec, table, w_qkv)
    o, lse = attend_call(lengths, qkv)
    middle, n2, a, slope = up_call(o, x, vec, w_out, w_up, bias)
    gh, gmid, gatt, go, sums, bup = feed_back_call(gy, slope, middle, vec, w_down_t, w_up, w_out)
    gqkv, qsums = attend_back_call(lengths, qkv, o, go, lse)
    gx, first_sums, gtable = first_back_call(lengths, lead_index, x, gmid, gqkv, vec, w_qkv)
    gvec = jnp.concatenate([first_sums[:2], sums[:2], qsums[:2], sums[2:4]], axis=0)
    y = down_call(a, middle, vec, w_down_t)
    return (
        y.reshape(1, L, D),
        gx.reshape(1, L, D),
        share(outer_call(n1, gqkv, "grad_qkv")),
        share(outer_call(o, gatt, "grad_out")),
        share(outer_call(n2, gh, "grad_up")),
        share(outer_call(gy, a, "grad_down").T),
        share(gvec),
        share(gtable[:LEADS]),
        share(bup[0].reshape(FF // D, D)),
    )


def solution(mesh):
    sizes = (mesh.shape["dp"], mesh.shape["fsdp"])
    whole_tiles = FF // sizes[1] == 384 and sizes[1] == 2 * sizes[0]
    plan = per_device if whole_tiles else per_device_plain
    rows, both = P(("dp", "fsdp"), None, None), P("dp", "fsdp")
    index = P(("dp", "fsdp"), None)
    return jax.shard_map(
        functools.partial(plan, sizes),
        mesh=mesh,
        in_specs=(rows, index, index, rows) + (both,) * 7,
        out_specs=(rows, rows) + (both,) * 7,
        check_vma=False,
    )
```

```python
import functools

import jax
import jax.numpy as jnp
from jax import lax
from jax.experimental import pallas as pl
from jax.experimental.pallas import tpu as pltpu
from jax.sharding import PartitionSpec as P

D = 768
HEADS = 12
HD = 64
FF = 3072
LEADS = 20
WIN = 8
L = 1024
EPSILON = 1e-05
MASKED = -1e30
ROWS = 256
TILES = L // ROWS
BLK = 128
PAIRS = HEADS // 2
SCALE = HD ** (-0.5)
VMEM_BYTES = 56 * 1024 * 1024

F32 = jnp.float32
BF16 = jnp.bfloat16


def params(limit=VMEM_BYTES):
    return pltpu.CompilerParams(vmem_limit_bytes=limit)


def dot_nn(a, b):
    return lax.dot_general(a, b, (((1,), (0,)), ((), ())), preferred_element_type=F32)


def dot_nt(a, b):
    return lax.dot_general(a, b, (((1,), (1,)), ((), ())), preferred_element_type=F32)


def whole(shape, space=pltpu.VMEM):
    return pl.BlockSpec(shape, lambda *_: (0,) * len(shape), memory_space=space)


def smem():
    return pl.BlockSpec(memory_space=pltpu.SMEM)


def rows_of(width):
    return pl.BlockSpec((ROWS, width), lambda i: (i, 0))


def norm_parts(values):
    center = values - jnp.mean(values, axis=-1, keepdims=True)
    spread = jnp.mean(center * center, axis=-1, keepdims=True)
    inv = lax.rsqrt(spread + EPSILON)
    return center * inv, inv


def bounds_of(lengths_ref):
    found, total = [], 0
    for w in range(WIN):
        total = total + lengths_ref[0, w]
        found.append(total)
    return found


def lead_of(places, bounds, lead_ref):
    lead = jnp.full(places.shape, -1, jnp.int32)
    for w in reversed(range(WIN)):
        lead = jnp.where(places < bounds[w], lead_ref[0, w], lead)
    return lead


def qkv_kernel(len_ref, lead_ref, x_ref, vec_ref, table_ref, w_ref, n1_ref, qkv_ref):
    step = pl.program_id(0)
    bounds = bounds_of(len_ref)
    hat, _ = norm_parts(x_ref[...].astype(F32))
    normed = hat * (1.0 + vec_ref[0:1, :]) + vec_ref[1:2, :]
    shape = (ROWS, table_ref.shape[0])
    places = step * ROWS + lax.broadcasted_iota(jnp.int32, shape, 0)
    hot = lead_of(places, bounds, lead_ref) == lax.broadcasted_iota(jnp.int32, shape, 1)
    n1 = (normed + dot_nn(hot.astype(BF16), table_ref[...])).astype(BF16)
    n1_ref[...] = n1
    for third in range(3):
        cols = slice(third * D, (third + 1) * D)
        part = dot_nn(n1, w_ref[:, cols])
        if third == 0:
            part = (part + vec_ref[4:5, :]).astype(BF16) * jnp.asarray(SCALE, BF16)
        elif third == 2:
            part = part + vec_ref[5:6, :]
        qkv_ref[:, cols] = part.astype(BF16)


def qkv_call(lengths, leads, x, vec, table, w):
    return pl.pallas_call(
        qkv_kernel,
        grid=(TILES,),
        in_specs=[smem(), smem(), rows_of(D), whole(vec.shape), whole(table.shape), whole(w.shape)],
        out_specs=[rows_of(D), rows_of(3 * D)],
        out_shape=[jax.ShapeDtypeStruct((L, D), BF16), jax.ShapeDtypeStruct((L, 3 * D), BF16)],
        compiler_params=params(),
        cost_estimate=pl.CostEstimate(flops=2 * L * D * 3 * D, bytes_accessed=12_000_000, transcendentals=0),
        name="norm_qkv",
    )(lengths, leads, x, vec, table, w)


SPANS = (1, 2, 3, 4, 6)


def dot_tn(a, b):
    return lax.dot_general(a, b, (((0,), (0,)), ((), ())), preferred_element_type=F32)


def key_span(bounds, block):
    first, last = block * BLK, block * BLK + BLK - 1
    start, end = jnp.int32(0), jnp.int32(L)
    for w in range(WIN):
        start = jnp.where(bounds[w] <= first, bounds[w], start)
    for w in reversed(range(WIN)):
        end = jnp.where(bounds[w] > last, bounds[w], end)
    return start // 16 * 16, end


def window_at(places, bounds):
    found = jnp.zeros(places.shape, jnp.int32)
    for w in range(WIN):
        found = found + (places >= bounds[w]).astype(jnp.int32)
    return found


def hide(bounds, start, rows, block):
    shape = (rows, 2 * BLK)
    keys = window_at(start + lax.broadcasted_iota(jnp.int32, (rows, 1), 0), bounds)
    lanes = lax.broadcasted_iota(jnp.int32, (1, 2 * BLK), 1)
    queries = window_at(block * BLK + jnp.where(lanes < BLK, lanes, lanes - BLK), bounds)
    return jnp.where(jnp.broadcast_to(keys, shape) == jnp.broadcast_to(queries, shape), 0.0, MASKED)


def split_pair(two):
    lanes = lax.broadcasted_iota(jnp.int32, two.shape, 1)
    zero = jnp.zeros_like(two)
    return jnp.concatenate([jnp.where(lanes < HD, two, zero), jnp.where(lanes < HD, zero, two)], axis=0)


def join_pair(both):
    lanes = lax.broadcasted_iota(jnp.int32, (BLK, BLK), 1)
    return jnp.where(lanes < HD, both[:BLK], both[BLK:])


def by_span(bounds, block, body):
    start, end = key_span(bounds, block)
    need = (end - start + BLK - 1) // BLK
    below = 0
    for span in SPANS:
        @pl.when((need > below) & (need <= span))
        def _(span=span):
            body(pl.multiple_of(jnp.minimum(start, L - span * BLK), 16), span * BLK)

        below = span


def attend_kernel(len_ref, qkv_ref, o_ref, lse_ref, hidden):
    bounds = bounds_of(len_ref)
    lse_ref[HEADS:, :] = jnp.zeros((lse_ref.shape[0] - HEADS, L), F32)

    def query_step(block, carry):
        at = pl.multiple_of(block * BLK, BLK)

        def body(start, rows):
            hidden[:rows] = hide(bounds, start, rows, block)
            def score(p):
                cols = slice(p * BLK, (p + 1) * BLK)
                keys = qkv_ref[pl.ds(start, rows), D + p * BLK:D + (p + 1) * BLK]
                return dot_nt(keys, split_pair(qkv_ref[pl.ds(at, BLK), cols])) + hidden[:rows]

            following = score(0)
            for p in range(PAIRS):
                scores = following
                if p + 1 < PAIRS:
                    following = score(p + 1)
                cols = slice(p * BLK, (p + 1) * BLK)
                vals = qkv_ref[pl.ds(start, rows), 2 * D + p * BLK:2 * D + (p + 1) * BLK]
                top = jnp.max(scores, axis=0, keepdims=True)
                expo = jnp.exp(scores - top)
                total = jnp.sum(expo, axis=0, keepdims=True)
                soft = (expo * (1.0 / total)).astype(BF16)
                o_ref[pl.ds(at, BLK), cols] = join_pair(dot_tn(soft, vals)).astype(BF16)
                log_total = top + jnp.log(total)
                lse_ref[2 * p:2 * p + 1, pl.ds(at, BLK)] = log_total[:, :BLK]
                lse_ref[2 * p + 1:2 * p + 2, pl.ds(at, BLK)] = log_total[:, BLK:]

        by_span(bounds, block, body)
        return carry

    lax.fori_loop(0, L // BLK, query_step, 0)


def attend_call(lengths, qkv):
    return pl.pallas_call(
        attend_kernel,
        in_specs=[smem(), pl.BlockSpec(memory_space=pltpu.VMEM)],
        out_specs=[pl.BlockSpec(memory_space=pltpu.VMEM)] * 2,
        out_shape=[jax.ShapeDtypeStruct((L, D), BF16), jax.ShapeDtypeStruct((16, L), F32)],
        scratch_shapes=[pltpu.VMEM((SPANS[-1] * BLK, 2 * BLK), F32)],
        compiler_params=params(),
        cost_estimate=pl.CostEstimate(flops=4 * L * L * D, bytes_accessed=8_000_000, transcendentals=0),
        name="attend",
    )(lengths, qkv)


def attend_back_kernel(first, len_ref, lse_ref, qkv_hbm, o_hbm, go_hbm, g_ref, sums_ref, q, k, v, o, go, hidden, dk, dv, sems):
    bounds = bounds_of(len_ref)
    wide = q.shape[1]
    at = first * BLK
    copies = [
        pltpu.make_async_copy(src.at[:, col:col + wide], dst, sems.at[n])
        for n, (src, dst, col) in enumerate(
            ((qkv_hbm, k, D + at), (qkv_hbm, q, at), (qkv_hbm, v, 2 * D + at), (go_hbm, go, at), (o_hbm, o, at))
        )
    ]
    for copy in copies:
        copy.start()
    dk[...] = jnp.zeros_like(dk)
    dv[...] = jnp.zeros_like(dv)
    sums_ref[...] = jnp.zeros_like(sums_ref)
    for copy in copies:
        copy.wait()

    def query_step(block, carry):
        at = pl.multiple_of(block * BLK, BLK)

        def body(start, rows):
            hidden[:rows] = hide(bounds, start, rows, block)
            for p in range(wide // BLK):
                head = 2 * (first + p)
                cols = slice(p * BLK, (p + 1) * BLK)
                keys, vals = k[pl.ds(start, rows), cols], v[pl.ds(start, rows), cols]
                grads = go[pl.ds(at, BLK), cols]
                prod = (grads.astype(F32) * o[pl.ds(at, BLK), cols].astype(F32)).T
                dots = jnp.concatenate(
                    [jnp.sum(prod[:HD], axis=0, keepdims=True), jnp.sum(prod[HD:], axis=0, keepdims=True)], axis=1
                )
                logs = jnp.concatenate(
                    [lse_ref[head:head + 1, pl.ds(at, BLK)], lse_ref[head + 1:head + 2, pl.ds(at, BLK)]], axis=1
                )
                queries, grads = split_pair(q[pl.ds(at, BLK), cols]), split_pair(grads)
                soft = jnp.exp(dot_nt(keys, queries) + hidden[:rows] - logs)
                grad_scores = (soft * (dot_nt(vals, grads) - dots)).astype(BF16)
                dv[pl.ds(start, rows), cols] += dot_nn(soft.astype(BF16), grads)
                dk[pl.ds(start, rows), cols] += dot_nn(grad_scores, queries)
                done = (join_pair(dot_tn(grad_scores, keys)) * SCALE).astype(BF16)
                g_ref[pl.ds(at, BLK), cols] = done
                sums_ref[0:1, cols] += jnp.sum(done.astype(F32), axis=0, keepdims=True)

        by_span(bounds, block, body)
        return carry

    lax.fori_loop(0, L // BLK, query_step, 0)
    g_ref[:, wide:2 * wide] = dk[...].astype(BF16)
    gv = dv[...].astype(BF16)
    g_ref[:, 2 * wide:] = gv
    sums_ref[1:2, :] = jnp.sum(gv.astype(F32), axis=0, keepdims=True)


def attend_back_call(lengths, qkv, o, go, lse, first=0, pairs=PAIRS):
    wide = pairs * BLK
    return pl.pallas_call(
        functools.partial(attend_back_kernel, first),
        in_specs=[smem(), pl.BlockSpec(memory_space=pltpu.VMEM)] + [pl.BlockSpec(memory_space=pl.ANY)] * 3,
        out_specs=[pl.BlockSpec(memory_space=pltpu.VMEM)] * 2,
        out_shape=[jax.ShapeDtypeStruct((L, 3 * wide), BF16), jax.ShapeDtypeStruct((8, wide), F32)],
        scratch_shapes=[pltpu.VMEM((L, wide), BF16)] * 5 + [
            pltpu.VMEM((SPANS[-1] * BLK, 2 * BLK), F32),
            pltpu.VMEM((L, wide), F32),
            pltpu.VMEM((L, wide), F32),
            pltpu.SemaphoreType.DMA((5,)),
        ],
        compiler_params=params(),
        cost_estimate=pl.CostEstimate(flops=10 * L * L * wide, bytes_accessed=15_000_000 * pairs // PAIRS, transcendentals=0),
        name="attend_back",
    )(lengths, lse, qkv, o, go)


def up_kernel(o_ref, x_ref, vec_ref, wo_ref, wu_ref, bu_ref, mid_ref, n2_ref, a_ref, slope_ref):
    middle = x_ref[...].astype(F32) + (dot_nn(o_ref[...], wo_ref[...]) + vec_ref[6:7, :])
    mid_ref[...] = middle
    hat, _ = norm_parts(middle)
    n2 = (hat * (1.0 + vec_ref[2:3, :]) + vec_ref[3:4, :]).astype(BF16)
    n2_ref[...] = n2
    width = 512
    for c in range(FF // width):
        cols = slice(c * width, (c + 1) * width)
        h = dot_nn(n2, wu_ref[:, cols]) + bu_ref[:, cols]
        act, slope = gate_pair(h)
        a_ref[:, cols] = act.astype(BF16)
        slope_ref[:, cols] = slope.astype(BF16)


def up_call(o, x, vec, wo, wu, bu):
    return pl.pallas_call(
        up_kernel,
        grid=(TILES,),
        in_specs=[rows_of(D), rows_of(D), whole(vec.shape), whole(wo.shape), whole(wu.shape), whole(bu.shape)],
        out_specs=[rows_of(D), rows_of(D), rows_of(FF), rows_of(FF)],
        out_shape=[
            jax.ShapeDtypeStruct((L, D), F32),
            jax.ShapeDtypeStruct((L, D), BF16),
            jax.ShapeDtypeStruct((L, FF), BF16),
            jax.ShapeDtypeStruct((L, FF), BF16),
        ],
        compiler_params=params(),
        cost_estimate=pl.CostEstimate(flops=2 * L * D * (FF + D), bytes_accessed=25_000_000, transcendentals=2 * L * FF),
        name="feed_up",
    )(o, x, vec, wo, wu, bu)


def down_kernel(a_ref, mid_ref, vec_ref, wdt_ref, y_ref):
    y_ref[...] = (mid_ref[...] + (dot_nt(a_ref[...], wdt_ref[...]) + vec_ref[7:8, :])).astype(BF16)


def down_call(a, middle, vec, wdt):
    return pl.pallas_call(
        down_kernel,
        grid=(TILES,),
        in_specs=[rows_of(FF), rows_of(D), whole(vec.shape), whole(wdt.shape)],
        out_specs=rows_of(D),
        out_shape=jax.ShapeDtypeStruct((L, D), BF16),
        compiler_params=params(),
        cost_estimate=pl.CostEstimate(flops=2 * L * D * FF, bytes_accessed=17_000_000, transcendentals=0),
        name="feed_down",
    )(a, middle, vec, wdt)


def feed_back_kernel(gy_ref, slope_ref, mid_ref, vec_ref, wdt_ref, wu_ref, wo_ref,
                     gh_ref, gmid_ref, gatt_ref, go_ref, sums_ref, bup_ref):
    @pl.when(pl.program_id(0) == 0)
    def _():
        sums_ref[...] = jnp.zeros_like(sums_ref)
        bup_ref[...] = jnp.zeros_like(bup_ref)

    gm = gy_ref[...]
    gy = gm.astype(F32)
    width = 768
    gn2 = None
    for c in range(FF // width):
        cols = slice(c * width, (c + 1) * width)
        ga = dot_nn(gm, wdt_ref[:, cols])
        gh = (ga * slope_ref[:, cols].astype(F32)).astype(BF16)
        gh_ref[:, cols] = gh
        bup_ref[0:1, cols] += jnp.sum(gh.astype(F32), axis=0, keepdims=True)
        part = dot_nt(gh, wu_ref[:, cols])
        gn2 = part if gn2 is None else gn2 + part
    hat, inv = norm_parts(mid_ref[...])
    sums_ref[0:1, :] += jnp.sum(gn2 * hat, axis=0, keepdims=True)
    sums_ref[1:2, :] += jnp.sum(gn2, axis=0, keepdims=True)
    gmid = gy + norm_back(gn2, hat, inv, vec_ref[2:3, :])
    gmid_ref[...] = gmid
    gatt = gmid.astype(BF16)
    gatt_ref[...] = gatt
    sums_ref[2:3, :] += jnp.sum(gatt.astype(F32), axis=0, keepdims=True)
    sums_ref[3:4, :] += jnp.sum(gy, axis=0, keepdims=True)
    go_ref[...] = dot_nt(gatt, wo_ref[...]).astype(BF16)


def feed_back_call(gy, slope, middle, vec, wdt, wu, wo):
    return pl.pallas_call(
        feed_back_kernel,
        grid=(TILES,),
        in_specs=[rows_of(D), rows_of(FF), rows_of(D), whole(vec.shape), whole(wdt.shape), whole(wu.shape), whole(wo.shape)],
        out_specs=[rows_of(FF), rows_of(D), rows_of(D), rows_of(D), whole((8, D)), whole((8, FF))],
        out_shape=[
            jax.ShapeDtypeStruct((L, FF), BF16),
            jax.ShapeDtypeStruct((L, D), F32),
            jax.ShapeDtypeStruct((L, D), BF16),
            jax.ShapeDtypeStruct((L, D), BF16),
            jax.ShapeDtypeStruct((8, D), F32),
            jax.ShapeDtypeStruct((8, FF), F32),
        ],
        compiler_params=params(),
        cost_estimate=pl.CostEstimate(flops=2 * L * D * (2 * FF + D), bytes_accessed=35_000_000, transcendentals=0),
        name="feed_back",
    )(gy, slope, middle, vec, wdt, wu, wo)


def outer_kernel(left_ref, right_ref, out_ref, turned):
    @pl.when(pl.program_id(0) == 0)
    def _():
        turned[...] = left_ref[...].T

    out_ref[...] = dot_nn(turned[...], right_ref[...]).astype(BF16)


def outer_call(left, right, name):
    wide = right.shape[1]
    width = 768
    return pl.pallas_call(
        outer_kernel,
        grid=(wide // width,),
        in_specs=[whole(left.shape), pl.BlockSpec((L, width), lambda i: (0, i))],
        out_specs=pl.BlockSpec((D, width), lambda i: (0, i)),
        out_shape=jax.ShapeDtypeStruct((D, wide), BF16),
        scratch_shapes=[pltpu.VMEM((D, L), BF16)],
        compiler_params=params(),
        cost_estimate=pl.CostEstimate(flops=2 * L * D * wide, bytes_accessed=4 * L * D + 4 * D * wide, transcendentals=0),
        name=name,
    )(left, right)


def first_back_kernel(len_ref, lead_ref, x_ref, gmid_ref, g_ref, vec_ref, w_ref, out_ref, sums_ref, table_ref):
    step = pl.program_id(0)

    @pl.when(step == 0)
    def _():
        sums_ref[...] = jnp.zeros_like(sums_ref)
        table_ref[...] = jnp.zeros_like(table_ref)

    gn1 = dot_nt(g_ref[...], w_ref[...])
    hat, inv = norm_parts(x_ref[...].astype(F32))
    sums_ref[0:1, :] += jnp.sum(gn1 * hat, axis=0, keepdims=True)
    sums_ref[1:2, :] += jnp.sum(gn1, axis=0, keepdims=True)
    shape = (table_ref.shape[0], ROWS)
    places = step * ROWS + lax.broadcasted_iota(jnp.int32, shape, 1)
    hot = lead_of(places, bounds_of(len_ref), lead_ref) == lax.broadcasted_iota(jnp.int32, shape, 0)
    hot = hot.astype(BF16)
    high = gn1.astype(BF16)
    low = (gn1 - high.astype(F32)).astype(BF16)
    table_ref[...] += dot_nn(hot, high) + dot_nn(hot, low)
    out_ref[...] = gmid_ref[...] + norm_back(gn1, hat, inv, vec_ref[0:1, :])


def first_back_call(lengths, leads, x, gmid, gqkv, vec, w):
    return pl.pallas_call(
        first_back_kernel,
        grid=(TILES,),
        in_specs=[smem(), smem(), rows_of(D), rows_of(D), rows_of(3 * D), whole(vec.shape), whole(w.shape)],
        out_specs=[rows_of(D), whole((8, D)), whole((32, D))],
        out_shape=[
            jax.ShapeDtypeStruct((L, D), F32),
            jax.ShapeDtypeStruct((8, D), F32),
            jax.ShapeDtypeStruct((32, D), F32),
        ],
        compiler_params=params(),
        cost_estimate=pl.CostEstimate(flops=2 * L * D * 3 * D, bytes_accessed=17_000_000, transcendentals=0),
        name="first_back",
    )(lengths, leads, x, gmid, gqkv, vec, w)


def slots(found):
    return [
        (at, k, dp, fs + 2 * k)
        for at, (dp, fs, part) in enumerate(found)
        for k in range(part.shape[0])
    ]

def chunk_cols(chunk, wide):
    third = wide // 3
    return (2 * third, third) if chunk == 0 else (0, 2 * third)


def any_space():
    return pl.BlockSpec(memory_space=pl.ANY)


def in_vmem():
    return pl.BlockSpec(memory_space=pltpu.VMEM)


def kept(shape):
    return pl.BlockSpec(shape, lambda *_: (0,) * len(shape), pipeline_mode=pl.Buffered(1))


def pack_first(w_qkv, small):
    tall, cols = w_qkv.shape
    left = cols - 256
    fold = 128 // left
    rows = tall // fold
    rest = jnp.concatenate([w_qkv[k * rows:(k + 1) * rows, 256:] for k in range(fold)], axis=1)
    small = jnp.pad(small, ((0, 16 - small.shape[0]), (0, 128 - small.shape[1])))
    return jnp.concatenate([w_qkv[:, :128], w_qkv[:, 128:256], rest, small], axis=0)


def pack_chunk(chunk, w_up, w_down_t):
    wide = w_up.shape[1]
    start, count = chunk_cols(chunk, wide)
    parts = [w_up[:, start:start + count]]
    for k in range(w_down_t.shape[1] // wide):
        parts.append(w_down_t[:, k * wide + start:k * wide + start + count])
    return jnp.concatenate(parts, axis=0)


def fold_out(w_out):
    tall, narrow = w_out.shape
    rows = tall // 4
    wide = jnp.concatenate([w_out[k * rows:(k + 1) * rows] for k in range(4)], axis=1)
    return jnp.concatenate([wide[:, k * 128:(k + 1) * 128] for k in range(4 * narrow // 128)], axis=0)


def start_all(copies):
    for copy in copies:
        copy.start()
    for copy in copies:
        copy.wait()


def open_kernel(plan, count, ids_ref, len_ref, lead_ref, x_ref, *refs):
    parts = refs[:count]
    n1_ref, qkv_ref, w_ref, vec_ref, table_ref, bias0_ref, bias1_ref, stage, table, bias, sem = refs[count:]
    step = pl.program_id(0)
    dps, fss = stage.shape[0], stage.shape[1]
    tall, cols, narrow, wide = D // dps, 3 * D // fss, D // fss, FF // fss

    @pl.when(step == 0)
    def _():
        start_all([
            pltpu.make_async_copy(parts[at].at[k], stage.at[ids_ref[0] ^ dp, ids_ref[1] ^ fs], sem)
            for at, k, dp, fs in plan
        ])
        table[...] = jnp.zeros_like(table)
        left = cols - 256
        fold = 128 // left
        rows = tall // fold
        for d in range(dps):
            for f in range(fss):
                at = slice(d * tall, (d + 1) * tall)
                w_ref[at, f * cols:f * cols + 128] = stage[d, f, :tall]
                w_ref[at, f * cols + 128:f * cols + 256] = stage[d, f, tall:2 * tall]
                for k in range(fold):
                    w_ref[d * tall + k * rows:d * tall + (k + 1) * rows, f * cols + 256:(f + 1) * cols] = (
                        stage[d, f, 2 * tall:2 * tall + rows, k * left:(k + 1) * left]
                    )
                small = stage[d, f, 2 * tall + rows:, :narrow].astype(F32)
                at = slice(f * narrow, (f + 1) * narrow)
                vec_ref[2 * d:2 * d + 2, at] = small[0:2]
                table[5 * d:5 * d + 5, at] = small[2:7]
                bias[0:1, d * D + f * narrow:d * D + (f + 1) * narrow] = small[7:8]
        table_ref[...] = table[...].astype(BF16)
        for chunk, ref in ((0, bias0_ref), (1, bias1_ref)):
            start, many = chunk_cols(chunk, wide)
            for f in range(fss):
                ref[:, f * many:(f + 1) * many] = bias[:, f * wide + start:f * wide + start + many]

    qkv_tile(step, len_ref, lead_ref, x_ref, vec_ref, table_ref, w_ref, n1_ref, qkv_ref)


def qkv_tile(step, len_ref, lead_ref, x_ref, vec_ref, table_ref, w_ref, n1_ref, qkv_ref):
    bounds = bounds_of(len_ref)
    hat, _ = norm_parts(x_ref[...].astype(F32))
    normed = hat * (1.0 + vec_ref[0:1, :]) + vec_ref[1:2, :]
    shape = (ROWS, table_ref.shape[0])
    places = step * ROWS + lax.broadcasted_iota(jnp.int32, shape, 0)
    hot = lead_of(places, bounds, lead_ref) == lax.broadcasted_iota(jnp.int32, shape, 1)
    n1 = (normed + dot_nn(hot.astype(BF16), table_ref[...])).astype(BF16)
    n1_ref[...] = n1
    for third in range(3):
        cols = slice(third * D, (third + 1) * D)
        part = dot_nn(n1, w_ref[:, cols])
        if third == 0:
            part = (part + vec_ref[4:5, :]).astype(BF16) * jnp.asarray(SCALE, BF16)
        elif third == 2:
            part = part + vec_ref[5:6, :]
        qkv_ref[:, cols] = part.astype(BF16)


def open_call(found, ids, lengths, leads, x, sizes):
    parts = [part for _, _, part in found]
    rows = parts[0].shape[1]
    dps, fss = sizes
    sides = [fss * chunk_cols(chunk, FF // fss)[1] for chunk in range(2)]
    shapes = [((L, D), BF16), ((L, 3 * D), BF16), ((D, 3 * D), BF16), ((8, D), F32), ((32, D), BF16)]
    shapes += [((1, side), F32) for side in sides]
    return pl.pallas_call(
        functools.partial(open_kernel, slots(found), len(parts)),
        grid=(TILES,),
        in_specs=[smem(), smem(), smem(), rows_of(D)] + [any_space()] * len(parts),
        out_specs=[rows_of(D), rows_of(3 * D)] + [kept(shape) for shape, _ in shapes[2:]],
        out_shape=[jax.ShapeDtypeStruct(shape, kind) for shape, kind in shapes],
        scratch_shapes=[
            pltpu.VMEM((dps, fss, rows, 128), BF16),
            pltpu.VMEM((32, D), F32),
            pltpu.VMEM((1, FF), F32),
            pltpu.SemaphoreType.DMA,
        ],
        compiler_params=params(),
        cost_estimate=pl.CostEstimate(flops=2 * L * D * 3 * D, bytes_accessed=18_000_000, transcendentals=0),
        name="open",
    )(ids, lengths, leads, x, *parts)


def chunk_copies(plan, ids_ref, parts, wu, wd, stage, sem, sizes):
    dps, fss = sizes
    tall, thin = D // dps, D // fss
    many = wu.shape[1] // fss
    copies = []
    for at, k, dp, fs in plan:
        d, f = ids_ref[0] ^ dp, ids_ref[1] ^ fs
        part = parts[at]

        def place(ref, row, rows, col):
            return ref.at[pl.ds(pl.multiple_of(row, 16), rows), pl.ds(pl.multiple_of(col, 128), many)]

        copies.append(pltpu.make_async_copy(part.at[k, pl.ds(0, tall), :], place(wu, d * tall, tall, f * many), sem))
        for side in range(fss // dps):
            rows = part.at[k, pl.ds(tall + side * thin, thin), :]
            copies.append(pltpu.make_async_copy(rows, place(wd, f * thin, thin, (d * (fss // dps) + side) * many), sem))
        if stage is not None:
            rows = part.at[k, pl.ds(tall + fss // dps * thin, stage.shape[2]), :]
            copies.append(pltpu.make_async_copy(rows, stage.at[d, f], sem))
    return copies


def unfold_out(stage, wo, sizes):
    dps, fss = sizes
    tall, thin = D // dps, D // fss
    rows = tall // 4
    for d in range(dps):
        for f in range(fss):
            flat = jnp.concatenate([stage[d, f, k * rows:(k + 1) * rows] for k in range(thin * 4 // 128)], axis=1)
            for k in range(4):
                wo[d * tall + k * rows:d * tall + (k + 1) * rows, f * thin:(f + 1) * thin] = flat[:, k * thin:(k + 1) * thin]


def start(copies):
    for copy in copies:
        copy.start()


def wait(copies):
    for copy in copies:
        copy.wait()


def turn(ref, plain, ordered, mine, count):
    plain[...] = ref[...].T
    tall = ordered.shape[0] // count
    for k in range(count):
        at = pl.multiple_of((mine ^ k) * tall, tall)
        ordered[k * tall:(k + 1) * tall, :] = plain[pl.ds(at, tall), :]


def gate_pair(h):
    cdf = 0.5 + 0.5 * lax.erf(h * 0.7071067811865476)
    return h * cdf, cdf + h * (0.3989422804014327 * jnp.exp(h * h * -0.5))


def norm_back(grad, hat, inv, gain):
    scaled = grad * (1.0 + gain)
    both = jnp.mean(scaled * hat, axis=-1, keepdims=True)
    return inv * (scaled - jnp.mean(scaled, axis=-1, keepdims=True) - hat * both)


def feed_step(step, gm_ref, n2, n2_t, gm_t, wu, wd, bias, a_ref, bup_ref, gh, gn2, grads, ids_ref, sizes):
    dps, fss = sizes
    pair = fss // dps
    width = a_ref.shape[1]
    many = width // pair
    tall, thin = D // dps, D // fss
    block = step ^ (ids_ref[1] // pair)
    cols = pl.ds(pl.multiple_of(block * width, width), width)
    own_u, own_d = wu[:, cols], wd[:, cols]
    shift = bias[:, cols]
    bup = jnp.zeros((1, width), F32)
    for r in range(TILES):
        rows = slice(r * ROWS, (r + 1) * ROWS)
        act, slope = gate_pair(dot_nn(n2[rows, :], own_u) + shift)
        a_ref[rows, :] = act.astype(BF16)
        part = (dot_nn(gm_ref[rows, :], own_d) * slope).astype(BF16)
        gh[rows, :] = part
        bup = bup + jnp.sum(part.astype(F32), axis=0, keepdims=True)
        gn2[rows, :] += dot_nt(part, own_u)
    bup_ref[:, cols] = bup
    grad = dot_nn(gm_t[...], a_ref[...]).astype(BF16)
    d = block ^ ids_ref[0]
    for f in range(fss):
        for side in range(pair):
            at = tall + side * thin
            grads[d & 1, d >> 1, f & 1, f >> 1, at:at + thin, :] = grad[f * thin:(f + 1) * thin, side * many:(side + 1) * many]
    grad = dot_nn(n2_t[...], gh[...]).astype(BF16)
    for side in range(pair):
        y = (ids_ref[1] & 1) ^ side
        for d in range(dps):
            grads[d & 1, d >> 1, y, step, :tall, :] = grad[d * tall:(d + 1) * tall, side * many:(side + 1) * many]


def up_copies(step, grads, mine_ref, theirs_ref, tall, sem):
    return [
        pltpu.make_async_copy(grads.at[c, :, :, step, pl.ds(0, tall), :], ref.at[:, :, step, pl.ds(0, tall), :], sem)
        for c, ref in ((0, mine_ref), (1, theirs_ref))
    ]


def down_copy(c, x, grads, ref, tall, sem):
    return pltpu.make_async_copy(
        grads.at[c, x, :, :, pl.ds(tall, tall), :], ref.at[x, :, :, pl.ds(tall, tall), :], sem
    )


def send_grads(step, ids_ref, grads, mine_ref, theirs_ref, up_sem, down_sem, sizes):
    tall = D // sizes[0]
    start(up_copies(step, grads, mine_ref, theirs_ref, tall, up_sem))
    away = step ^ (ids_ref[1] // (sizes[1] // sizes[0])) ^ ids_ref[0]
    for c, ref in ((0, mine_ref), (1, theirs_ref)):
        @pl.when((away & 1) == c)
        def _(c=c, ref=ref):
            down_copy(c, away >> 1, grads, ref, tall, down_sem).start()


def wait_grads(grads, mine_ref, theirs_ref, up_sem, down_sem, sizes):
    tall = D // sizes[0]
    for step in range(sizes[0]):
        wait(up_copies(step, grads, mine_ref, theirs_ref, tall, up_sem))
        down_copy(0, 0, grads, mine_ref, tall, down_sem).wait()


def feed_first_kernel(plan, count, sizes, ids_ref, vec_ref, bias_ref, o_hbm, x_hbm, gm_hbm, *refs):
    parts = refs[:count]
    (a_ref, bup_ref, mid_hbm, n2_hbm, gn2_hbm, wd_hbm, wo_hbm, mine_ref, theirs_ref,
     o, x, gm, mid, n2, gn2, wd, wo, wu, stage, plain, n2_t, gm_t, gh, grads, sems) = refs[count:]
    step = pl.program_id(0)
    outs = [
        pltpu.make_async_copy(src, dst, sems.at[4 + k])
        for k, (src, dst) in enumerate(((wd, wd_hbm), (wo, wo_hbm), (mid, mid_hbm), (n2, n2_hbm), (gn2, gn2_hbm)))
    ]

    @pl.when(step == 0)
    def _():
        ins = [pltpu.make_async_copy(src, dst, sems.at[1 + k]) for k, (src, dst) in enumerate(((gm_hbm, gm), (o_hbm, o), (x_hbm, x)))]
        lay = chunk_copies(plan, ids_ref, parts, wu, wd, stage, sems.at[0], sizes)
        start(ins[:1] + lay + ins[1:])
        ins[0].wait()
        turn(gm, plain, gm_t, ids_ref[1], sizes[1])
        gn2[...] = jnp.zeros_like(gn2)
        wait(lay)
        unfold_out(stage, wo, sizes)
        start(outs[:2])
        wait(ins[1:])
        for r in range(TILES):
            rows = slice(r * ROWS, (r + 1) * ROWS)
            middle = x[rows, :].astype(F32) + (dot_nn(o[rows, :], wo[...]) + vec_ref[6:7, :])
            mid[rows, :] = middle
            hat, _ = norm_parts(middle)
            n2[rows, :] = (hat * (1.0 + vec_ref[2:3, :]) + vec_ref[3:4, :]).astype(BF16)
        start(outs[2:4])
        turn(n2, plain, n2_t, ids_ref[0], sizes[0])

    feed_step(step, gm, n2, n2_t, gm_t, wu, wd, bias_ref, a_ref, bup_ref, gh, gn2, grads, ids_ref, sizes)
    send_grads(step, ids_ref, grads, mine_ref, theirs_ref, sems.at[9], sems.at[10], sizes)

    @pl.when(step == pl.num_programs(0) - 1)
    def _():
        outs[4].start()
        wait_grads(grads, mine_ref, theirs_ref, sems.at[9], sems.at[10], sizes)
        wait(outs)


def feed_first(found, ids, o, x, gm, vec, bias, sizes):
    parts = [part for _, _, part in found]
    dps, fss = sizes
    units = bias.shape[1]
    width, many = units // dps, units // fss
    rows = 2 * (D // dps)
    shape = (dps // 2, 2, fss // 2, rows, many)
    outs = [
        ((L, units), BF16), ((1, units), F32), ((L, D), F32), ((L, D), BF16), ((L, D), F32), ((D, units), BF16), ((D, D), BF16),
        (shape, BF16), (shape, BF16),
    ]
    return pl.pallas_call(
        functools.partial(feed_first_kernel, slots(found), len(parts), sizes),
        grid_spec=pltpu.PrefetchScalarGridSpec(
            num_scalar_prefetch=1,
            grid=(dps,),
            in_specs=[kept((8, D)), kept((1, units))] + [any_space()] * (3 + len(parts)),
            out_specs=[pl.BlockSpec((L, width), lambda i, ids: (0, i ^ (ids[1] // (fss // dps)))), kept((1, units))]
            + [any_space()] * 7,
            scratch_shapes=[
                pltpu.VMEM((L, D), BF16),
                pltpu.VMEM((L, D), BF16),
                pltpu.VMEM((L, D), BF16),
                pltpu.VMEM((L, D), F32),
                pltpu.VMEM((L, D), BF16),
                pltpu.VMEM((L, D), F32),
                pltpu.VMEM((D, units), BF16),
                pltpu.VMEM((D, D), BF16),
                pltpu.VMEM((D, units), BF16),
                pltpu.VMEM((dps, fss, parts[0].shape[1] - rows, 128), BF16),
                pltpu.VMEM((D, L), BF16),
                pltpu.VMEM((D, L), BF16),
                pltpu.VMEM((D, L), BF16),
                pltpu.VMEM((L, width), BF16),
                pltpu.VMEM((2,) + shape, BF16),
                pltpu.SemaphoreType.DMA((11,)),
            ],
        ),
        out_shape=[jax.ShapeDtypeStruct(s, kind) for s, kind in outs],
        compiler_params=params(),
        cost_estimate=pl.CostEstimate(flops=2 * L * D * (5 * units + D), bytes_accessed=30_000_000, transcendentals=2 * L * units),
        name="feed_first",
    )(ids, vec, bias, o, x, gm, *parts)


def feed_second_kernel(plan, count, sizes, ids_ref, vec_ref, bias_ref, o_hbm, n2_hbm, gm_hbm, mid_hbm, gn2_hbm, wo_hbm, *refs):
    parts = refs[:count]
    (a_ref, bup_ref, sums_ref, wd_hbm, gmid_hbm, go_hbm, mine_ref, theirs_ref,
     o, n2, gm, mid, gn2, wo, wd, wu, plain, n2_t, gm_t, gh, gatt, full, grads, sems) = refs[count:]
    step = pl.program_id(0)
    dps, fss = sizes
    tall, thin = D // dps, D // fss
    ins = [
        pltpu.make_async_copy(src, dst, sems.at[k])
        for k, (src, dst) in enumerate(((gm_hbm, gm), (n2_hbm, n2), (gn2_hbm, gn2), (o_hbm, o), (mid_hbm, mid), (wo_hbm, wo)))
    ]
    wd_out = pltpu.make_async_copy(wd, wd_hbm, sems.at[7])

    @pl.when(step == 0)
    def _():
        lay = chunk_copies(plan, ids_ref, parts, wu, wd, None, sems.at[6], sizes)
        start(ins[:2] + lay + ins[2:])
        ins[0].wait()
        turn(gm, plain, gm_t, ids_ref[1], fss)
        ins[1].wait()
        turn(n2, plain, n2_t, ids_ref[0], dps)
        wait(lay)
        wd_out.start()
        ins[2].wait()

    feed_step(step, gm, n2, n2_t, gm_t, wu, wd, bias_ref, a_ref, bup_ref, gh, gn2, grads, ids_ref, sizes)
    send_grads(step, ids_ref, grads, mine_ref, theirs_ref, sems.at[8], sems.at[9], sizes)

    @pl.when(step == pl.num_programs(0) - 1)
    def _():
        wait(ins[3:])
        turn(o, plain, n2_t, ids_ref[0], dps)
        sums = [jnp.zeros((1, D), F32)] * 4
        outs = []
        for r in range(TILES):
            rows = slice(r * ROWS, (r + 1) * ROWS)
            grad, gy = gn2[rows, :], gm[rows, :].astype(F32)
            hat, inv = norm_parts(mid[rows, :])
            gmid = gy + norm_back(grad, hat, inv, vec_ref[2:3, :])
            mid[rows, :] = gmid
            low = gmid.astype(BF16)
            gatt[rows, :] = low
            n2[rows, :] = dot_nt(low, wo[...]).astype(BF16)
            for k, term in enumerate((grad * hat, grad, low.astype(F32), gy)):
                sums[k] = sums[k] + jnp.sum(term, axis=0, keepdims=True)
        outs = [pltpu.make_async_copy(mid, gmid_hbm, sems.at[10]), pltpu.make_async_copy(n2, go_hbm, sems.at[11])]
        start(outs)
        sums_ref[...] = jnp.concatenate(sums + [jnp.zeros((4, D), F32)], axis=0)
        full[...] = dot_nn(n2_t[...], gatt[...]).astype(BF16)
        for f in range(fss):
            flip = ids_ref[1] ^ f
            for d in range(dps):
                for k in range(2):
                    at = 2 * tall
                    grads[d & 1, d >> 1, flip & 1, flip >> 1, at:at + tall // 2, k * thin:(k + 1) * thin] = (
                        full[d * tall + k * (tall // 2):d * tall + (k + 1) * (tall // 2), f * thin:(f + 1) * thin]
                    )
                grads[d & 1, d >> 1, flip & 1, flip >> 1, 2 * tall:, 2 * thin:] = jnp.zeros(
                    (tall // 2, grads.shape[5] - 2 * thin), BF16
                )
        rows = pl.ds(2 * tall, tall // 2)
        rest = [
            pltpu.make_async_copy(grads.at[c, :, :, :, rows, :], ref.at[:, :, :, rows, :], sems.at[12])
            for c, ref in ((0, mine_ref), (1, theirs_ref))
        ]
        start(rest)
        wait_grads(grads, mine_ref, theirs_ref, sems.at[8], sems.at[9], sizes)
        wait(rest + outs + [wd_out])


def feed_second(found, ids, o, n2, gm, mid, gn2, vec, bias, wo, sizes):
    parts = [part for _, _, part in found]
    dps, fss = sizes
    units = bias.shape[1]
    width, many = units // dps, units // fss
    tall = D // dps
    shape = (dps // 2, 2, fss // 2, 2 * tall + tall // 2, many)
    outs = [
        ((L, units), BF16), ((1, units), F32), ((8, D), F32), ((D, units), BF16), ((L, D), F32), ((L, D), BF16),
        (shape, BF16), (shape, BF16),
    ]
    return pl.pallas_call(
        functools.partial(feed_second_kernel, slots(found), len(parts), sizes),
        grid_spec=pltpu.PrefetchScalarGridSpec(
            num_scalar_prefetch=1,
            grid=(dps,),
            in_specs=[kept((8, D)), kept((1, units))] + [any_space()] * (6 + len(parts)),
            out_specs=[
                pl.BlockSpec((L, width), lambda i, ids: (0, i ^ (ids[1] // (fss // dps)))), kept((1, units)), kept((8, D)),
            ] + [any_space()] * 5,
            scratch_shapes=[
                pltpu.VMEM((L, D), BF16),
                pltpu.VMEM((L, D), BF16),
                pltpu.VMEM((L, D), BF16),
                pltpu.VMEM((L, D), F32),
                pltpu.VMEM((L, D), F32),
                pltpu.VMEM((D, D), BF16),
                pltpu.VMEM((D, units), BF16),
                pltpu.VMEM((D, units), BF16),
                pltpu.VMEM((D, L), BF16),
                pltpu.VMEM((D, L), BF16),
                pltpu.VMEM((D, L), BF16),
                pltpu.VMEM((L, width), BF16),
                pltpu.VMEM((L, D), BF16),
                pltpu.VMEM((D, D), BF16),
                pltpu.VMEM((2,) + shape, BF16),
                pltpu.SemaphoreType.DMA((13,)),
            ],
        ),
        out_shape=[jax.ShapeDtypeStruct(s, kind) for s, kind in outs],
        compiler_params=params(),
        cost_estimate=pl.CostEstimate(flops=2 * L * D * (5 * units + 2 * D), bytes_accessed=35_000_000, transcendentals=2 * L * units),
        name="feed_second",
    )(ids, vec, bias, o, n2, gm, mid, gn2, wo, *parts)


def last_kernel(a0_ref, a1_ref, mid_ref, vec_ref, w0_ref, w1_ref, y_ref):
    total = dot_nt(a0_ref[...], w0_ref[...]) + dot_nt(a1_ref[...], w1_ref[...])
    y_ref[...] = (mid_ref[...] + (total + vec_ref[7:8, :])).astype(BF16)


def last_call(a0, a1, middle, vec, w0, w1):
    return pl.pallas_call(
        last_kernel,
        grid=(TILES,),
        in_specs=[rows_of(a0.shape[1]), rows_of(a1.shape[1]), rows_of(D), kept((8, D)), kept(w0.shape), kept(w1.shape)],
        out_specs=rows_of(D),
        out_shape=jax.ShapeDtypeStruct((L, D), BF16),
        compiler_params=params(),
        cost_estimate=pl.CostEstimate(flops=2 * L * D * FF, bytes_accessed=17_000_000, transcendentals=0),
        name="feed_down",
    )(a0, a1, middle, vec, w0, w1)


def close_kernel(sizes, ids_ref, len_ref, lead_ref, vec_ref, sums_ref, qsums0_ref, qsums1_ref, bup0_ref, bup1_ref,
                 x_hbm, gmid_hbm, n1_hbm, g0_hbm, g1_hbm, w_hbm, gx_hbm, mine_ref, theirs_ref,
                 x, gmid, n1, g, w, plain, left, full, table, grads, sems):
    dps, fss = sizes
    tall, cols, thin, wide = D // dps, 3 * D // fss, D // fss, FF // fss
    ins = [
        pltpu.make_async_copy(src, dst, sems.at[k])
        for k, (src, dst) in enumerate(((n1_hbm, n1), (w_hbm, w), (x_hbm, x), (gmid_hbm, gmid)))
    ]
    joins = []
    for third in range(3):
        at = third * D
        for src in (g0_hbm, g1_hbm):
            part = src.shape[1] // 3
            joins.append(
                pltpu.make_async_copy(src.at[:, third * part:(third + 1) * part], g.at[:, at:at + part], sems.at[4])
            )
            at += part
    start(ins[:1] + joins + ins[1:])
    ins[0].wait()
    turn(n1, plain, left, ids_ref[0], dps)
    wait(joins)
    rest = cols - 256
    fold = 128 // rest
    some = tall // fold
    for third in range(3):
        at = slice(third * D, (third + 1) * D)
        full[:, at] = dot_nn(left[...], g[:, at]).astype(BF16)
    for f in range(fss):
        flip = ids_ref[1] ^ f
        y, z = flip & 1, flip >> 1
        for d in range(dps):
            own = slice(d * tall, (d + 1) * tall)
            c, away = d & 1, d >> 1
            grads[c, away, y, z, 0:tall, :] = full[own, f * cols:f * cols + 128]
            grads[c, away, y, z, tall:2 * tall, :] = full[own, f * cols + 128:f * cols + 256]
            for k in range(fold):
                grads[c, away, y, z, 2 * tall:2 * tall + some, k * rest:(k + 1) * rest] = (
                    full[d * tall + k * some:d * tall + (k + 1) * some, f * cols + 256:(f + 1) * cols]
                )
    big, little = pl.ds(0, 2 * tall + some), pl.ds(2 * tall + some, 16)
    sends = [
        [
            pltpu.make_async_copy(grads.at[c, :, :, :, rows, :], ref.at[:, :, :, rows, :], sems.at[at])
            for c, ref in ((0, mine_ref), (1, theirs_ref))
        ]
        for at, rows in ((5, big), (6, little))
    ]
    start(sends[0])
    wait(ins[1:])
    gain, shift = jnp.zeros((1, D), F32), jnp.zeros((1, D), F32)
    table[...] = jnp.zeros_like(table)
    bounds = bounds_of(len_ref)
    outs = []
    for r in range(TILES):
        rows = slice(r * ROWS, (r + 1) * ROWS)
        grad = dot_nt(g[rows, :], w[...])
        hat, inv = norm_parts(x[rows, :].astype(F32))
        gain = gain + jnp.sum(grad * hat, axis=0, keepdims=True)
        shift = shift + jnp.sum(grad, axis=0, keepdims=True)
        shape = (table.shape[0], ROWS)
        places = r * ROWS + lax.broadcasted_iota(jnp.int32, shape, 1)
        hot = lead_of(places, bounds, lead_ref) == lax.broadcasted_iota(jnp.int32, shape, 0)
        hot = hot.astype(BF16)
        high = grad.astype(BF16)
        low = (grad - high.astype(F32)).astype(BF16)
        table[...] += dot_nn(hot, high) + dot_nn(hot, low)
        gmid[rows, :] += norm_back(grad, hat, inv, vec_ref[0:1, :])
    out = pltpu.make_async_copy(gmid, gx_hbm, sems.at[7])
    out.start()
    bup = []
    for f in range(fss):
        for chunk, ref in ((1, bup1_ref), (0, bup0_ref)):
            many = chunk_cols(chunk, wide)[1]
            bup.append(ref[:, f * many:(f + 1) * many])
    bup = jnp.concatenate(bup, axis=1)
    qsums = jnp.concatenate([qsums0_ref[0:2, :], qsums1_ref[0:2, :]], axis=1)
    gvec = [gain, shift, sums_ref[0:1, :], sums_ref[1:2, :], qsums[0:1, :], qsums[1:2, :], sums_ref[2:3, :], sums_ref[3:4, :]]
    for d in range(dps):
        small = jnp.concatenate(
            gvec[2 * d:2 * d + 2] + [table[5 * d:5 * d + 5, :], bup[:, d * D:(d + 1) * D], jnp.zeros((8, D), F32)], axis=0
        )
        away = ids_ref[0] ^ d
        for f in range(fss):
            flip = ids_ref[1] ^ f
            part = jnp.concatenate([small[:, f * thin:(f + 1) * thin], jnp.zeros((16, 128 - thin), F32)], axis=1)
            grads[away & 1, away >> 1, flip & 1, flip >> 1, 2 * tall + some:, :] = part.astype(BF16)
    start(sends[1])
    wait(sends[0] + sends[1] + [out])


def close_call(ids, lengths, leads, x, gmid, n1, back0, back1, vec, w, sums, bup0, bup1, sizes):
    dps, fss = sizes
    tall = D // dps
    rows = 2 * tall + tall // (128 // (3 * D // fss - 256)) + 16
    shape = (dps // 2, 2, fss // 2, rows, 128)
    return pl.pallas_call(
        functools.partial(close_kernel, sizes),
        in_specs=[smem()] * 3 + [in_vmem()] * 6 + [any_space()] * 6,
        out_specs=[any_space()] * 3,
        out_shape=[jax.ShapeDtypeStruct((L, D), F32), jax.ShapeDtypeStruct(shape, BF16), jax.ShapeDtypeStruct(shape, BF16)],
        scratch_shapes=[
            pltpu.VMEM((L, D), BF16),
            pltpu.VMEM((L, D), F32),
            pltpu.VMEM((L, D), BF16),
            pltpu.VMEM((L, 3 * D), BF16),
            pltpu.VMEM((D, 3 * D), BF16),
            pltpu.VMEM((D, L), BF16),
            pltpu.VMEM((D, L), BF16),
            pltpu.VMEM((D, 3 * D), BF16),
            pltpu.VMEM((32, D), F32),
            pltpu.VMEM((2,) + shape, BF16),
            pltpu.SemaphoreType.DMA((8,)),
        ],
        compiler_params=params(),
        cost_estimate=pl.CostEstimate(flops=4 * L * D * 3 * D, bytes_accessed=25_000_000, transcendentals=0),
        name="close",
    )(ids, lengths, leads, vec, sums, back0[1], back1[1], bup0, bup1, x, gmid, n1, back0[0], back1[0], w)


def finish_kernel(count, tall, cols, thin, *refs):
    parts, (qkv_ref, vec_ref, table_ref, bias_ref) = refs[:count], refs[count:]
    total = sum(part[...].astype(F32) for part in parts)
    qkv_ref[:, 0:128] = total[:tall]
    qkv_ref[:, 128:256] = total[tall:2 * tall]
    rest = cols - 256
    some = tall * rest // 128
    for k in range(128 // rest):
        qkv_ref[k * some:(k + 1) * some, 256:cols] = total[2 * tall:2 * tall + some, k * rest:(k + 1) * rest]
    small = total[2 * tall + some:, :thin]
    vec_ref[...] = small[0:2]
    table_ref[...] = small[2:7]
    bias_ref[...] = small[7:8]


def finish_call(parts, tall, cols, thin):
    return pl.pallas_call(
        functools.partial(finish_kernel, len(parts), tall, cols, thin),
        in_specs=[in_vmem()] * len(parts),
        out_specs=[in_vmem()] * 4,
        out_shape=[jax.ShapeDtypeStruct((rows, wide), F32) for rows, wide in ((tall, cols), (2, thin), (5, thin), (1, thin))],
        compiler_params=params(16 * 1024 * 1024),
        cost_estimate=pl.CostEstimate(flops=1_000_000, bytes_accessed=1_000_000, transcendentals=0),
        name="finish",
    )(*parts)


def hop_dp(value, flip, ranks):
    return lax.ppermute(value, "dp", [(i, i ^ flip) for i in range(ranks)])


def hop_fsdp(value, flip, ranks):
    return lax.ppermute(value, "fsdp", [(i, i ^ flip) for i in range(ranks)])


def tie(values, *others):
    flat, tree = jax.tree.flatten(values)
    more = jax.tree.leaves(others)
    done = lax.optimization_barrier(tuple(flat) + tuple(more))
    return jax.tree.unflatten(tree, done[:len(flat)])


def gather_depth(piece, sizes):
    return [piece] + [hop_fsdp(piece, 2 * z, sizes[1]) for z in range(1, sizes[1] // 2)]


def gather_far(piece, sizes):
    return jnp.stack([piece, hop_fsdp(piece, sizes[1] // 2, sizes[1])])


def gather_near(pair, sizes):
    other = hop_fsdp(pair, sizes[1] // 4, sizes[1])
    return jnp.stack([pair[0], other[0], pair[1], other[1]])


def gather_sides(column, sizes):
    return hop_dp(column, 2, sizes[0]), hop_fsdp(column, 1, sizes[1])


def gather_corner(sides, sizes):
    by_x, by_y = sides
    half = by_x.shape[0] // 2
    return hop_fsdp(by_x[:half], 1, sizes[1]), hop_dp(by_y[half:], 2, sizes[0])


def cross(parts, sizes):
    return [hop_dp(part, 1, sizes[0]) for part in parts]


def name_parts(parts, others):
    half = parts[0].shape[0] // 2
    flips = ((0, 0), (2, 0), (0, 1), (2, 1), (2, 1 + 2 * half))
    own = [(dp, fs, part) for (dp, fs), part in zip(flips, parts)]
    return own + [(dp | 1, fs, part) for (dp, fs), part in zip(flips, others)]


def plus(*terms):
    return sum(term.astype(F32) for term in terms)


def reduce_core(mine, theirs, sizes):
    flat = theirs.reshape(-1, theirs.shape[-1])
    return mine.reshape(flat.shape), hop_dp(flat, 1, sizes[0])


def reduce_sides(cored, sizes):
    both = plus(*cored).astype(BF16)
    both = both.reshape(sizes[0] // 2, 2, sizes[1] // 2, -1, both.shape[-1])
    half = both.shape[2] // 2
    first, second = both[:, :, :half], both[:, :, half:]
    got = hop_dp(first[1], 2, sizes[0]), hop_fsdp(second[:, 1], 1, sizes[1])
    return first[0], second[:, 0], got


def reduce_corner(sided, sizes):
    first, second, got = sided
    first, second = plus(first, got[0]).astype(BF16), plus(second, got[1]).astype(BF16)
    got = hop_fsdp(first[1], 1, sizes[1]), hop_dp(second[1], 2, sizes[0])
    return first[0], second[0], got


def reduce_near(cornered, sizes):
    first, second, got = cornered
    first, second = plus(first, got[0]).astype(BF16), plus(second, got[1]).astype(BF16)
    gone = hop_fsdp(jnp.stack([first[1], second[1]]), sizes[1] // 4, sizes[1])
    return first[0], second[0], gone


def reduce_far(neared, sizes):
    first, second, got = neared
    return first, got[0], hop_fsdp(plus(second, got[1]).astype(BF16), sizes[1] // 2, sizes[1])


def reduce_depth(cornered, sizes):
    first, second, got = cornered
    first, second = plus(first, got[0]).astype(BF16), plus(second, got[1]).astype(BF16)
    apart = [first[k] for k in range(first.shape[0])] + [second[k] for k in range(second.shape[0])]
    return [apart[0]] + [hop_fsdp(apart[z], 2 * z, sizes[1]) for z in range(1, len(apart))]


def per_device(sizes, tokens, lengths, lead_index, cotangent, w_qkv, w_out, w_up, w_down, vectors, lead_table, up_bias):
    dps, fss = sizes
    ids = jnp.stack([lax.axis_index("dp"), lax.axis_index("fsdp")]).astype(jnp.int32)
    thin, wide, tall = D // fss, FF // fss, D // dps
    x, gy = tokens.reshape(L, D), cotangent.reshape(L, D)

    piece0 = pack_first(w_qkv, jnp.concatenate([vectors, lead_table, up_bias], axis=0))
    w_down_t = w_down.T
    piece1 = jnp.concatenate([pack_chunk(0, w_up, w_down_t), fold_out(w_out)], axis=0)
    piece2 = pack_chunk(1, w_up, w_down_t)

    depth0 = gather_depth(piece0, sizes)
    depth0, piece1 = tie((depth0, piece1))
    column0 = jnp.stack(depth0)
    sides0, far1, other0 = gather_sides(column0, sizes), gather_far(piece1, sizes), cross((column0,), sizes)
    column0, sides0, other0, far1, piece2 = tie((column0, sides0, other0, far1, piece2))
    corner0, across0, column1 = gather_corner(sides0, sizes), cross(sides0, sizes), gather_near(far1, sizes)
    column0, sides0, corner0, other0, across0, column1, piece2 = tie(
        (column0, sides0, corner0, other0, across0, column1, piece2)
    )
    last0 = cross(corner0, sizes)
    last0, column1, piece2 = tie((last0, column1, piece2))

    sides1, depth2 = gather_sides(column1, sizes), gather_depth(piece2, sizes)
    found = name_parts((column0,) + sides0 + corner0, other0 + across0 + last0)
    opened = open_call(found, ids, lengths, lead_index, x, sizes)
    column1, sides1, depth2, opened = tie((column1, sides1, depth2, opened))
    n1, qkv, w_qkv, vec, table, bias0, bias1 = opened

    column2 = jnp.stack(depth2)
    corner1, other1, sides2 = gather_corner(sides1, sizes), cross((column1,), sizes), gather_sides(column2, sizes)
    attended = attend_call(lengths, qkv)
    column1, sides1, corner1, other1, column2, sides2, attended = tie(
        (column1, sides1, corner1, other1, column2, sides2, attended)
    )
    o, lse = attended

    last1 = cross(sides1 + corner1, sizes)
    last1, column2, sides2 = tie((last1, column2, sides2))

    corner2, other2 = gather_corner(sides2, sizes), cross((column2,) + sides2, sizes)
    found = name_parts((column1,) + sides1 + corner1, other1 + last1)
    first = feed_first(found, ids, o, x, gy, vec, bias0, sizes)
    column2, sides2, corner2, other2, first = tie((column2, sides2, corner2, other2, first))
    a0, bup0, middle, n2, gn2, wd0, w_out, mine0, theirs0 = first

    last2 = cross(corner2, sizes)
    last2, theirs0 = tie((last2, theirs0))

    grads0 = reduce_core(mine0, theirs0, sizes)
    found = name_parts((column2,) + sides2 + corner2, other2 + last2)
    second = feed_second(found, ids, o, n2, gy, middle, gn2, vec, bias1, w_out, sizes)
    grads0, second = tie((grads0, second))
    a1, bup1, sums, wd1, gmid, go, mine1, theirs1 = second

    grads0, grads1 = reduce_sides(grads0, sizes), reduce_core(mine1, theirs1, sizes)
    back0 = attend_back_call(lengths, qkv, o, go, lse, 0, 1)
    grads0, grads1, back0, go = tie((grads0, grads1, back0, go))

    grads0, grads1 = reduce_corner(grads0, sizes), reduce_sides(grads1, sizes)
    back1 = attend_back_call(lengths, qkv, o, go, lse, 1, PAIRS - 1)
    grads0, grads1, back0, back1 = tie((grads0, grads1, back0, back1))

    grads0, grads1 = reduce_near(grads0, sizes), reduce_corner(grads1, sizes)
    closed = close_call(
        ids, lengths, lead_index, x, gmid, n1, back0, back1, vec, w_qkv, sums, bup0, bup1, sizes
    )
    grads0, grads1, closed, a0 = tie((grads0, grads1, closed, a0))
    gx, mine2, theirs2 = closed

    grads2 = reduce_core(mine2, theirs2, sizes)
    grads2, a0 = tie((grads2, a0))
    grads0, grads1, grads2 = reduce_far(grads0, sizes), reduce_near(grads1, sizes), reduce_sides(grads2, sizes)
    y = last_call(a0, a1, middle, vec, wd0, wd1)
    grads0, grads1, grads2, y = tie((grads0, grads1, grads2, y))
    grads1, grads2 = reduce_far(grads1, sizes), reduce_corner(grads2, sizes)
    grads2 = reduce_depth(grads2, sizes)
    got0, got1 = plus(*grads0), plus(*grads1)

    many = wide // 3
    up = jnp.concatenate([got1[:tall], got0[:tall]], axis=1)
    down = []
    for side in range(fss // dps):
        rows = slice(tall + side * thin, tall + (side + 1) * thin)
        down += [got1[rows], got0[rows]]
    down = jnp.concatenate(down, axis=1).T
    out = jnp.concatenate([got1[2 * tall:, :thin], got1[2 * tall:, thin:2 * thin]], axis=0)
    up, down, out, grads2 = tie((up, down, out, grads2))
    qkv_grad, gvec, gtable, gbias = finish_call(grads2, tall, 3 * thin, thin)
    return y.reshape(1, L, D), gx.reshape(1, L, D), qkv_grad, out, up, down, gvec, gtable, gbias


def per_device_plain(sizes, tokens, lengths, lead_index, cotangent, w_qkv, w_out, w_up, w_down, vectors, table, bias):
    def full(shard):
        return lax.all_gather(lax.all_gather(shard, "fsdp", axis=1, tiled=True), "dp", axis=0, tiled=True)

    def share(grad):
        part = lax.psum_scatter(grad.astype(F32), "fsdp", scatter_dimension=1, tiled=True)
        return lax.psum_scatter(part, "dp", scatter_dimension=0, tiled=True)

    x, gy = tokens.reshape(L, D), cotangent.reshape(L, D)
    w_qkv, w_out, w_up, w_down_t = full(w_qkv), full(w_out), full(w_up), full(w_down).T
    vec, bias = full(vectors).astype(F32), full(bias).astype(F32).reshape(1, FF)
    table = jnp.pad(full(table), ((0, 32 - LEADS), (0, 0)))
    n1, qkv = qkv_call(lengths, lead_index, x, vec, table, w_qkv)
    o, lse = attend_call(lengths, qkv)
    middle, n2, a, slope = up_call(o, x, vec, w_out, w_up, bias)
    gh, gmid, gatt, go, sums, bup = feed_back_call(gy, slope, middle, vec, w_down_t, w_up, w_out)
    gqkv, qsums = attend_back_call(lengths, qkv, o, go, lse)
    gx, first_sums, gtable = first_back_call(lengths, lead_index, x, gmid, gqkv, vec, w_qkv)
    gvec = jnp.concatenate([first_sums[:2], sums[:2], qsums[:2], sums[2:4]], axis=0)
    y = down_call(a, middle, vec, w_down_t)
    return (
        y.reshape(1, L, D),
        gx.reshape(1, L, D),
        share(outer_call(n1, gqkv, "grad_qkv")),
        share(outer_call(o, gatt, "grad_out")),
        share(outer_call(n2, gh, "grad_up")),
        share(outer_call(gy, a, "grad_down").T),
        share(gvec),
        share(gtable[:LEADS]),
        share(bup[0].reshape(FF // D, D)),
    )


def solution(mesh):
    sizes = (mesh.shape["dp"], mesh.shape["fsdp"])
    whole_tiles = FF // sizes[1] == 384 and sizes[1] == 2 * sizes[0]
    plan = per_device if whole_tiles else per_device_plain
    rows, both = P(("dp", "fsdp"), None, None), P("dp", "fsdp")
    index = P(("dp", "fsdp"), None)
    return jax.shard_map(
        functools.partial(plan, sizes),
        mesh=mesh,
        in_specs=(rows, index, index, rows) + (both,) * 7,
        out_specs=(rows, rows) + (both,) * 7,
        check_vma=False,
    )
```

```python
import functools

import jax
import jax.numpy as jnp
from jax import lax
from jax.experimental import pallas as pl
from jax.experimental.pallas import tpu as pltpu
from jax.sharding import PartitionSpec as P

D = 768
HEADS = 12
HD = 64
FF = 3072
LEADS = 20
WIN = 8
L = 1024
EPSILON = 1e-05
MASKED = -1e30
ROWS = 256
TILES = L // ROWS
BLK = 128
PAIRS = HEADS // 2
SCALE = HD ** (-0.5)
VMEM_BYTES = 56 * 1024 * 1024

F32 = jnp.float32
BF16 = jnp.bfloat16


def params(limit=VMEM_BYTES):
    return pltpu.CompilerParams(vmem_limit_bytes=limit)


def dot_nn(a, b):
    return lax.dot_general(a, b, (((1,), (0,)), ((), ())), preferred_element_type=F32)


def dot_nt(a, b):
    return lax.dot_general(a, b, (((1,), (1,)), ((), ())), preferred_element_type=F32)


def whole(shape, space=pltpu.VMEM):
    return pl.BlockSpec(shape, lambda *_: (0,) * len(shape), memory_space=space)


def smem():
    return pl.BlockSpec(memory_space=pltpu.SMEM)


def rows_of(width):
    return pl.BlockSpec((ROWS, width), lambda i: (i, 0))


def norm_parts(values):
    center = values - jnp.mean(values, axis=-1, keepdims=True)
    spread = jnp.mean(center * center, axis=-1, keepdims=True)
    inv = lax.rsqrt(spread + EPSILON)
    return center * inv, inv


def bounds_of(lengths_ref):
    found, total = [], 0
    for w in range(WIN):
        total = total + lengths_ref[0, w]
        found.append(total)
    return found


def lead_of(places, bounds, lead_ref):
    lead = jnp.full(places.shape, -1, jnp.int32)
    for w in reversed(range(WIN)):
        lead = jnp.where(places < bounds[w], lead_ref[0, w], lead)
    return lead


def qkv_kernel(len_ref, lead_ref, x_ref, vec_ref, table_ref, w_ref, n1_ref, qkv_ref):
    step = pl.program_id(0)
    bounds = bounds_of(len_ref)
    hat, _ = norm_parts(x_ref[...].astype(F32))
    normed = hat * (1.0 + vec_ref[0:1, :]) + vec_ref[1:2, :]
    shape = (ROWS, table_ref.shape[0])
    places = step * ROWS + lax.broadcasted_iota(jnp.int32, shape, 0)
    hot = lead_of(places, bounds, lead_ref) == lax.broadcasted_iota(jnp.int32, shape, 1)
    n1 = (normed + dot_nn(hot.astype(BF16), table_ref[...])).astype(BF16)
    n1_ref[...] = n1
    for third in range(3):
        cols = slice(third * D, (third + 1) * D)
        part = dot_nn(n1, w_ref[:, cols])
        if third == 0:
            part = (part + vec_ref[4:5, :]).astype(BF16) * jnp.asarray(SCALE, BF16)
        elif third == 2:
            part = part + vec_ref[5:6, :]
        qkv_ref[:, cols] = part.astype(BF16)


def qkv_call(lengths, leads, x, vec, table, w):
    return pl.pallas_call(
        qkv_kernel,
        grid=(TILES,),
        in_specs=[smem(), smem(), rows_of(D), whole(vec.shape), whole(table.shape), whole(w.shape)],
        out_specs=[rows_of(D), rows_of(3 * D)],
        out_shape=[jax.ShapeDtypeStruct((L, D), BF16), jax.ShapeDtypeStruct((L, 3 * D), BF16)],
        compiler_params=params(),
        cost_estimate=pl.CostEstimate(flops=2 * L * D * 3 * D, bytes_accessed=12_000_000, transcendentals=0),
        name="norm_qkv",
    )(lengths, leads, x, vec, table, w)


SPANS = (1, 2, 3, 4, 6)


def dot_tn(a, b):
    return lax.dot_general(a, b, (((0,), (0,)), ((), ())), preferred_element_type=F32)


def key_span(bounds, block):
    first, last = block * BLK, block * BLK + BLK - 1
    start, end = jnp.int32(0), jnp.int32(L)
    for w in range(WIN):
        start = jnp.where(bounds[w] <= first, bounds[w], start)
    for w in reversed(range(WIN)):
        end = jnp.where(bounds[w] > last, bounds[w], end)
    return start // 16 * 16, end


def window_at(places, bounds):
    found = jnp.zeros(places.shape, jnp.int32)
    for w in range(WIN):
        found = found + (places >= bounds[w]).astype(jnp.int32)
    return found


def hide(bounds, start, rows, block):
    shape = (rows, 2 * BLK)
    keys = window_at(start + lax.broadcasted_iota(jnp.int32, (rows, 1), 0), bounds)
    lanes = lax.broadcasted_iota(jnp.int32, (1, 2 * BLK), 1)
    queries = window_at(block * BLK + jnp.where(lanes < BLK, lanes, lanes - BLK), bounds)
    return jnp.where(jnp.broadcast_to(keys, shape) == jnp.broadcast_to(queries, shape), 0.0, MASKED)


def split_pair(two):
    lanes = lax.broadcasted_iota(jnp.int32, two.shape, 1)
    zero = jnp.zeros_like(two)
    return jnp.concatenate([jnp.where(lanes < HD, two, zero), jnp.where(lanes < HD, zero, two)], axis=0)


def join_pair(both):
    lanes = lax.broadcasted_iota(jnp.int32, (BLK, BLK), 1)
    return jnp.where(lanes < HD, both[:BLK], both[BLK:])


def by_span(bounds, block, body):
    start, end = key_span(bounds, block)
    need = (end - start + BLK - 1) // BLK
    below = 0
    for span in SPANS:
        @pl.when((need > below) & (need <= span))
        def _(span=span):
            body(pl.multiple_of(jnp.minimum(start, L - span * BLK), 16), span * BLK)

        below = span


def attend_kernel(len_ref, qkv_ref, o_ref, lse_ref, hidden):
    bounds = bounds_of(len_ref)
    lse_ref[HEADS:, :] = jnp.zeros((lse_ref.shape[0] - HEADS, L), F32)

    def query_step(block, carry):
        at = pl.multiple_of(block * BLK, BLK)

        def body(start, rows):
            hidden[:rows] = hide(bounds, start, rows, block)
            def score(p):
                cols = slice(p * BLK, (p + 1) * BLK)
                keys = qkv_ref[pl.ds(start, rows), D + p * BLK:D + (p + 1) * BLK]
                return dot_nt(keys, split_pair(qkv_ref[pl.ds(at, BLK), cols])) + hidden[:rows]

            following = score(0)
            for p in range(PAIRS):
                scores = following
                if p + 1 < PAIRS:
                    following = score(p + 1)
                cols = slice(p * BLK, (p + 1) * BLK)
                vals = qkv_ref[pl.ds(start, rows), 2 * D + p * BLK:2 * D + (p + 1) * BLK]
                top = jnp.max(scores, axis=0, keepdims=True)
                expo = jnp.exp(scores - top)
                total = jnp.sum(expo, axis=0, keepdims=True)
                soft = (expo * (1.0 / total)).astype(BF16)
                o_ref[pl.ds(at, BLK), cols] = join_pair(dot_tn(soft, vals)).astype(BF16)
                log_total = top + jnp.log(total)
                lse_ref[2 * p:2 * p + 1, pl.ds(at, BLK)] = log_total[:, :BLK]
                lse_ref[2 * p + 1:2 * p + 2, pl.ds(at, BLK)] = log_total[:, BLK:]

        by_span(bounds, block, body)
        return carry

    lax.fori_loop(0, L // BLK, query_step, 0)


def attend_call(lengths, qkv):
    return pl.pallas_call(
        attend_kernel,
        in_specs=[smem(), pl.BlockSpec(memory_space=pltpu.VMEM)],
        out_specs=[pl.BlockSpec(memory_space=pltpu.VMEM)] * 2,
        out_shape=[jax.ShapeDtypeStruct((L, D), BF16), jax.ShapeDtypeStruct((16, L), F32)],
        scratch_shapes=[pltpu.VMEM((SPANS[-1] * BLK, 2 * BLK), F32)],
        compiler_params=params(),
        cost_estimate=pl.CostEstimate(flops=4 * L * L * D, bytes_accessed=8_000_000, transcendentals=0),
        name="attend",
    )(lengths, qkv)


def attend_back_kernel(first, len_ref, lse_ref, qkv_hbm, o_hbm, go_hbm, g_ref, sums_ref, q, k, v, o, go, hidden, dk, dv, sems):
    bounds = bounds_of(len_ref)
    wide = q.shape[1]
    at = first * BLK
    copies = [
        pltpu.make_async_copy(src.at[:, col:col + wide], dst, sems.at[n])
        for n, (src, dst, col) in enumerate(
            ((qkv_hbm, k, D + at), (qkv_hbm, q, at), (qkv_hbm, v, 2 * D + at), (go_hbm, go, at), (o_hbm, o, at))
        )
    ]
    for copy in copies:
        copy.start()
    dk[...] = jnp.zeros_like(dk)
    dv[...] = jnp.zeros_like(dv)
    sums_ref[...] = jnp.zeros_like(sums_ref)
    for copy in copies:
        copy.wait()

    def query_step(block, carry):
        at = pl.multiple_of(block * BLK, BLK)

        def body(start, rows):
            hidden[:rows] = hide(bounds, start, rows, block)
            for p in range(wide // BLK):
                head = 2 * (first + p)
                cols = slice(p * BLK, (p + 1) * BLK)
                keys, vals = k[pl.ds(start, rows), cols], v[pl.ds(start, rows), cols]
                grads = go[pl.ds(at, BLK), cols]
                prod = (grads.astype(F32) * o[pl.ds(at, BLK), cols].astype(F32)).T
                dots = jnp.concatenate(
                    [jnp.sum(prod[:HD], axis=0, keepdims=True), jnp.sum(prod[HD:], axis=0, keepdims=True)], axis=1
                )
                logs = jnp.concatenate(
                    [lse_ref[head:head + 1, pl.ds(at, BLK)], lse_ref[head + 1:head + 2, pl.ds(at, BLK)]], axis=1
                )
                queries, grads = split_pair(q[pl.ds(at, BLK), cols]), split_pair(grads)
                soft = jnp.exp(dot_nt(keys, queries) + hidden[:rows] - logs)
                grad_scores = (soft * (dot_nt(vals, grads) - dots)).astype(BF16)
                dv[pl.ds(start, rows), cols] += dot_nn(soft.astype(BF16), grads)
                dk[pl.ds(start, rows), cols] += dot_nn(grad_scores, queries)
                done = (join_pair(dot_tn(grad_scores, keys)) * SCALE).astype(BF16)
                g_ref[pl.ds(at, BLK), cols] = done
                sums_ref[0:1, cols] += jnp.sum(done.astype(F32), axis=0, keepdims=True)

        by_span(bounds, block, body)
        return carry

    lax.fori_loop(0, L // BLK, query_step, 0)
    g_ref[:, wide:2 * wide] = dk[...].astype(BF16)
    gv = dv[...].astype(BF16)
    g_ref[:, 2 * wide:] = gv
    sums_ref[1:2, :] = jnp.sum(gv.astype(F32), axis=0, keepdims=True)


def attend_back_call(lengths, qkv, o, go, lse, first=0, pairs=PAIRS):
    wide = pairs * BLK
    return pl.pallas_call(
        functools.partial(attend_back_kernel, first),
        in_specs=[smem(), pl.BlockSpec(memory_space=pltpu.VMEM)] + [pl.BlockSpec(memory_space=pl.ANY)] * 3,
        out_specs=[pl.BlockSpec(memory_space=pltpu.VMEM)] * 2,
        out_shape=[jax.ShapeDtypeStruct((L, 3 * wide), BF16), jax.ShapeDtypeStruct((8, wide), F32)],
        scratch_shapes=[pltpu.VMEM((L, wide), BF16)] * 5 + [
            pltpu.VMEM((SPANS[-1] * BLK, 2 * BLK), F32),
            pltpu.VMEM((L, wide), F32),
            pltpu.VMEM((L, wide), F32),
            pltpu.SemaphoreType.DMA((5,)),
        ],
        compiler_params=params(),
        cost_estimate=pl.CostEstimate(flops=10 * L * L * wide, bytes_accessed=15_000_000 * pairs // PAIRS, transcendentals=0),
        name="attend_back",
    )(lengths, lse, qkv, o, go)


def up_kernel(o_ref, x_ref, vec_ref, wo_ref, wu_ref, bu_ref, mid_ref, n2_ref, a_ref, slope_ref):
    middle = x_ref[...].astype(F32) + (dot_nn(o_ref[...], wo_ref[...]) + vec_ref[6:7, :])
    mid_ref[...] = middle
    hat, _ = norm_parts(middle)
    n2 = (hat * (1.0 + vec_ref[2:3, :]) + vec_ref[3:4, :]).astype(BF16)
    n2_ref[...] = n2
    width = 512
    for c in range(FF // width):
        cols = slice(c * width, (c + 1) * width)
        h = dot_nn(n2, wu_ref[:, cols]) + bu_ref[:, cols]
        act, slope = gate_pair(h)
        a_ref[:, cols] = act.astype(BF16)
        slope_ref[:, cols] = slope.astype(BF16)


def up_call(o, x, vec, wo, wu, bu):
    return pl.pallas_call(
        up_kernel,
        grid=(TILES,),
        in_specs=[rows_of(D), rows_of(D), whole(vec.shape), whole(wo.shape), whole(wu.shape), whole(bu.shape)],
        out_specs=[rows_of(D), rows_of(D), rows_of(FF), rows_of(FF)],
        out_shape=[
            jax.ShapeDtypeStruct((L, D), F32),
            jax.ShapeDtypeStruct((L, D), BF16),
            jax.ShapeDtypeStruct((L, FF), BF16),
            jax.ShapeDtypeStruct((L, FF), BF16),
        ],
        compiler_params=params(),
        cost_estimate=pl.CostEstimate(flops=2 * L * D * (FF + D), bytes_accessed=25_000_000, transcendentals=2 * L * FF),
        name="feed_up",
    )(o, x, vec, wo, wu, bu)


def down_kernel(a_ref, mid_ref, vec_ref, wdt_ref, y_ref):
    y_ref[...] = (mid_ref[...] + (dot_nt(a_ref[...], wdt_ref[...]) + vec_ref[7:8, :])).astype(BF16)


def down_call(a, middle, vec, wdt):
    return pl.pallas_call(
        down_kernel,
        grid=(TILES,),
        in_specs=[rows_of(FF), rows_of(D), whole(vec.shape), whole(wdt.shape)],
        out_specs=rows_of(D),
        out_shape=jax.ShapeDtypeStruct((L, D), BF16),
        compiler_params=params(),
        cost_estimate=pl.CostEstimate(flops=2 * L * D * FF, bytes_accessed=17_000_000, transcendentals=0),
        name="feed_down",
    )(a, middle, vec, wdt)


def feed_back_kernel(gy_ref, slope_ref, mid_ref, vec_ref, wdt_ref, wu_ref, wo_ref,
                     gh_ref, gmid_ref, gatt_ref, go_ref, sums_ref, bup_ref):
    @pl.when(pl.program_id(0) == 0)
    def _():
        sums_ref[...] = jnp.zeros_like(sums_ref)
        bup_ref[...] = jnp.zeros_like(bup_ref)

    gm = gy_ref[...]
    gy = gm.astype(F32)
    width = 768
    gn2 = None
    for c in range(FF // width):
        cols = slice(c * width, (c + 1) * width)
        ga = dot_nn(gm, wdt_ref[:, cols])
        gh = (ga * slope_ref[:, cols].astype(F32)).astype(BF16)
        gh_ref[:, cols] = gh
        bup_ref[0:1, cols] += jnp.sum(gh.astype(F32), axis=0, keepdims=True)
        part = dot_nt(gh, wu_ref[:, cols])
        gn2 = part if gn2 is None else gn2 + part
    hat, inv = norm_parts(mid_ref[...])
    sums_ref[0:1, :] += jnp.sum(gn2 * hat, axis=0, keepdims=True)
    sums_ref[1:2, :] += jnp.sum(gn2, axis=0, keepdims=True)
    gmid = gy + norm_back(gn2, hat, inv, vec_ref[2:3, :])
    gmid_ref[...] = gmid
    gatt = gmid.astype(BF16)
    gatt_ref[...] = gatt
    sums_ref[2:3, :] += jnp.sum(gatt.astype(F32), axis=0, keepdims=True)
    sums_ref[3:4, :] += jnp.sum(gy, axis=0, keepdims=True)
    go_ref[...] = dot_nt(gatt, wo_ref[...]).astype(BF16)


def feed_back_call(gy, slope, middle, vec, wdt, wu, wo):
    return pl.pallas_call(
        feed_back_kernel,
        grid=(TILES,),
        in_specs=[rows_of(D), rows_of(FF), rows_of(D), whole(vec.shape), whole(wdt.shape), whole(wu.shape), whole(wo.shape)],
        out_specs=[rows_of(FF), rows_of(D), rows_of(D), rows_of(D), whole((8, D)), whole((8, FF))],
        out_shape=[
            jax.ShapeDtypeStruct((L, FF), BF16),
            jax.ShapeDtypeStruct((L, D), F32),
            jax.ShapeDtypeStruct((L, D), BF16),
            jax.ShapeDtypeStruct((L, D), BF16),
            jax.ShapeDtypeStruct((8, D), F32),
            jax.ShapeDtypeStruct((8, FF), F32),
        ],
        compiler_params=params(),
        cost_estimate=pl.CostEstimate(flops=2 * L * D * (2 * FF + D), bytes_accessed=35_000_000, transcendentals=0),
        name="feed_back",
    )(gy, slope, middle, vec, wdt, wu, wo)


def outer_kernel(left_ref, right_ref, out_ref, turned):
    @pl.when(pl.program_id(0) == 0)
    def _():
        turned[...] = left_ref[...].T

    out_ref[...] = dot_nn(turned[...], right_ref[...]).astype(BF16)


def outer_call(left, right, name):
    wide = right.shape[1]
    width = 768
    return pl.pallas_call(
        outer_kernel,
        grid=(wide // width,),
        in_specs=[whole(left.shape), pl.BlockSpec((L, width), lambda i: (0, i))],
        out_specs=pl.BlockSpec((D, width), lambda i: (0, i)),
        out_shape=jax.ShapeDtypeStruct((D, wide), BF16),
        scratch_shapes=[pltpu.VMEM((D, L), BF16)],
        compiler_params=params(),
        cost_estimate=pl.CostEstimate(flops=2 * L * D * wide, bytes_accessed=4 * L * D + 4 * D * wide, transcendentals=0),
        name=name,
    )(left, right)


def first_back_kernel(len_ref, lead_ref, x_ref, gmid_ref, g_ref, vec_ref, w_ref, out_ref, sums_ref, table_ref):
    step = pl.program_id(0)

    @pl.when(step == 0)
    def _():
        sums_ref[...] = jnp.zeros_like(sums_ref)
        table_ref[...] = jnp.zeros_like(table_ref)

    gn1 = dot_nt(g_ref[...], w_ref[...])
    hat, inv = norm_parts(x_ref[...].astype(F32))
    sums_ref[0:1, :] += jnp.sum(gn1 * hat, axis=0, keepdims=True)
    sums_ref[1:2, :] += jnp.sum(gn1, axis=0, keepdims=True)
    shape = (table_ref.shape[0], ROWS)
    places = step * ROWS + lax.broadcasted_iota(jnp.int32, shape, 1)
    hot = lead_of(places, bounds_of(len_ref), lead_ref) == lax.broadcasted_iota(jnp.int32, shape, 0)
    hot = hot.astype(BF16)
    high = gn1.astype(BF16)
    low = (gn1 - high.astype(F32)).astype(BF16)
    table_ref[...] += dot_nn(hot, high) + dot_nn(hot, low)
    out_ref[...] = gmid_ref[...] + norm_back(gn1, hat, inv, vec_ref[0:1, :])


def first_back_call(lengths, leads, x, gmid, gqkv, vec, w):
    return pl.pallas_call(
        first_back_kernel,
        grid=(TILES,),
        in_specs=[smem(), smem(), rows_of(D), rows_of(D), rows_of(3 * D), whole(vec.shape), whole(w.shape)],
        out_specs=[rows_of(D), whole((8, D)), whole((32, D))],
        out_shape=[
            jax.ShapeDtypeStruct((L, D), F32),
            jax.ShapeDtypeStruct((8, D), F32),
            jax.ShapeDtypeStruct((32, D), F32),
        ],
        compiler_params=params(),
        cost_estimate=pl.CostEstimate(flops=2 * L * D * 3 * D, bytes_accessed=17_000_000, transcendentals=0),
        name="first_back",
    )(lengths, leads, x, gmid, gqkv, vec, w)


def slots(found):
    return [
        (at, k, dp, fs + 2 * k)
        for at, (dp, fs, part) in enumerate(found)
        for k in range(part.shape[0])
    ]

def chunk_cols(chunk, wide):
    third = wide // 3
    return (2 * third, third) if chunk == 0 else (0, 2 * third)


def any_space():
    return pl.BlockSpec(memory_space=pl.ANY)


def in_vmem():
    return pl.BlockSpec(memory_space=pltpu.VMEM)


def kept(shape):
    return pl.BlockSpec(shape, lambda *_: (0,) * len(shape), pipeline_mode=pl.Buffered(1))


def pack_first(w_qkv, small):
    tall, cols = w_qkv.shape
    left = cols - 256
    fold = 128 // left
    rows = tall // fold
    rest = jnp.concatenate([w_qkv[k * rows:(k + 1) * rows, 256:] for k in range(fold)], axis=1)
    small = jnp.pad(small, ((0, 16 - small.shape[0]), (0, 128 - small.shape[1])))
    return jnp.concatenate([w_qkv[:, :128], w_qkv[:, 128:256], rest, small], axis=0)


def pack_chunk(chunk, w_up, w_down_t):
    wide = w_up.shape[1]
    start, count = chunk_cols(chunk, wide)
    parts = [w_up[:, start:start + count]]
    for k in range(w_down_t.shape[1] // wide):
        parts.append(w_down_t[:, k * wide + start:k * wide + start + count])
    return jnp.concatenate(parts, axis=0)


def fold_out(w_out):
    tall, narrow = w_out.shape
    rows = tall // 4
    wide = jnp.concatenate([w_out[k * rows:(k + 1) * rows] for k in range(4)], axis=1)
    return jnp.concatenate([wide[:, k * 128:(k + 1) * 128] for k in range(4 * narrow // 128)], axis=0)


def start_all(copies):
    for copy in copies:
        copy.start()
    for copy in copies:
        copy.wait()


def open_kernel(plan, count, ids_ref, len_ref, lead_ref, x_ref, *refs):
    parts = refs[:count]
    n1_ref, qkv_ref, w_ref, vec_ref, table_ref, bias0_ref, bias1_ref, stage, table, bias, sem = refs[count:]
    step = pl.program_id(0)
    dps, fss = stage.shape[0], stage.shape[1]
    tall, cols, narrow, wide = D // dps, 3 * D // fss, D // fss, FF // fss

    @pl.when(step == 0)
    def _():
        start_all([
            pltpu.make_async_copy(parts[at].at[k], stage.at[ids_ref[0] ^ dp, ids_ref[1] ^ fs], sem)
            for at, k, dp, fs in plan
        ])
        table[...] = jnp.zeros_like(table)
        left = cols - 256
        fold = 128 // left
        rows = tall // fold
        for d in range(dps):
            for f in range(fss):
                at = slice(d * tall, (d + 1) * tall)
                w_ref[at, f * cols:f * cols + 128] = stage[d, f, :tall]
                w_ref[at, f * cols + 128:f * cols + 256] = stage[d, f, tall:2 * tall]
                for k in range(fold):
                    w_ref[d * tall + k * rows:d * tall + (k + 1) * rows, f * cols + 256:(f + 1) * cols] = (
                        stage[d, f, 2 * tall:2 * tall + rows, k * left:(k + 1) * left]
                    )
                small = stage[d, f, 2 * tall + rows:, :narrow].astype(F32)
                at = slice(f * narrow, (f + 1) * narrow)
                vec_ref[2 * d:2 * d + 2, at] = small[0:2]
                table[5 * d:5 * d + 5, at] = small[2:7]
                bias[0:1, d * D + f * narrow:d * D + (f + 1) * narrow] = small[7:8]
        table_ref[...] = table[...].astype(BF16)
        for chunk, ref in ((0, bias0_ref), (1, bias1_ref)):
            start, many = chunk_cols(chunk, wide)
            for f in range(fss):
                ref[:, f * many:(f + 1) * many] = bias[:, f * wide + start:f * wide + start + many]

    qkv_tile(step, len_ref, lead_ref, x_ref, vec_ref, table_ref, w_ref, n1_ref, qkv_ref)


def qkv_tile(step, len_ref, lead_ref, x_ref, vec_ref, table_ref, w_ref, n1_ref, qkv_ref):
    bounds = bounds_of(len_ref)
    hat, _ = norm_parts(x_ref[...].astype(F32))
    normed = hat * (1.0 + vec_ref[0:1, :]) + vec_ref[1:2, :]
    shape = (ROWS, table_ref.shape[0])
    places = step * ROWS + lax.broadcasted_iota(jnp.int32, shape, 0)
    hot = lead_of(places, bounds, lead_ref) == lax.broadcasted_iota(jnp.int32, shape, 1)
    n1 = (normed + dot_nn(hot.astype(BF16), table_ref[...])).astype(BF16)
    n1_ref[...] = n1
    for third in range(3):
        cols = slice(third * D, (third + 1) * D)
        part = dot_nn(n1, w_ref[:, cols])
        if third == 0:
            part = (part + vec_ref[4:5, :]).astype(BF16) * jnp.asarray(SCALE, BF16)
        elif third == 2:
            part = part + vec_ref[5:6, :]
        qkv_ref[:, cols] = part.astype(BF16)


def open_call(found, ids, lengths, leads, x, sizes):
    parts = [part for _, _, part in found]
    rows = parts[0].shape[1]
    dps, fss = sizes
    sides = [fss * chunk_cols(chunk, FF // fss)[1] for chunk in range(2)]
    shapes = [((L, D), BF16), ((L, 3 * D), BF16), ((D, 3 * D), BF16), ((8, D), F32), ((32, D), BF16)]
    shapes += [((1, side), F32) for side in sides]
    return pl.pallas_call(
        functools.partial(open_kernel, slots(found), len(parts)),
        grid=(TILES,),
        in_specs=[smem(), smem(), smem(), rows_of(D)] + [any_space()] * len(parts),
        out_specs=[rows_of(D), rows_of(3 * D)] + [kept(shape) for shape, _ in shapes[2:]],
        out_shape=[jax.ShapeDtypeStruct(shape, kind) for shape, kind in shapes],
        scratch_shapes=[
            pltpu.VMEM((dps, fss, rows, 128), BF16),
            pltpu.VMEM((32, D), F32),
            pltpu.VMEM((1, FF), F32),
            pltpu.SemaphoreType.DMA,
        ],
        compiler_params=params(),
        cost_estimate=pl.CostEstimate(flops=2 * L * D * 3 * D, bytes_accessed=18_000_000, transcendentals=0),
        name="open",
    )(ids, lengths, leads, x, *parts)


def chunk_copies(plan, ids_ref, parts, wu, wd, stage, sem, sizes):
    dps, fss = sizes
    tall, thin = D // dps, D // fss
    many = wu.shape[1] // fss
    copies = []
    for at, k, dp, fs in plan:
        d, f = ids_ref[0] ^ dp, ids_ref[1] ^ fs
        part = parts[at]

        def place(ref, row, rows, col):
            return ref.at[pl.ds(pl.multiple_of(row, 16), rows), pl.ds(pl.multiple_of(col, 128), many)]

        copies.append(pltpu.make_async_copy(part.at[k, pl.ds(0, tall), :], place(wu, d * tall, tall, f * many), sem))
        for side in range(fss // dps):
            rows = part.at[k, pl.ds(tall + side * thin, thin), :]
            copies.append(pltpu.make_async_copy(rows, place(wd, f * thin, thin, (d * (fss // dps) + side) * many), sem))
        if stage is not None:
            rows = part.at[k, pl.ds(tall + fss // dps * thin, stage.shape[2]), :]
            copies.append(pltpu.make_async_copy(rows, stage.at[d, f], sem))
    return copies


def unfold_out(stage, wo, sizes):
    dps, fss = sizes
    tall, thin = D // dps, D // fss
    rows = tall // 4
    for d in range(dps):
        for f in range(fss):
            flat = jnp.concatenate([stage[d, f, k * rows:(k + 1) * rows] for k in range(thin * 4 // 128)], axis=1)
            for k in range(4):
                wo[d * tall + k * rows:d * tall + (k + 1) * rows, f * thin:(f + 1) * thin] = flat[:, k * thin:(k + 1) * thin]


def start(copies):
    for copy in copies:
        copy.start()


def wait(copies):
    for copy in copies:
        copy.wait()


def turn(ref, plain, ordered, mine, count):
    plain[...] = ref[...].T
    tall = ordered.shape[0] // count
    for k in range(count):
        at = pl.multiple_of((mine ^ k) * tall, tall)
        ordered[k * tall:(k + 1) * tall, :] = plain[pl.ds(at, tall), :]


def gate_pair(h):
    cdf = 0.5 + 0.5 * lax.erf(h * 0.7071067811865476)
    return h * cdf, cdf + h * (0.3989422804014327 * jnp.exp(h * h * -0.5))


def norm_back(grad, hat, inv, gain):
    scaled = grad * (1.0 + gain)
    both = jnp.mean(scaled * hat, axis=-1, keepdims=True)
    return inv * (scaled - jnp.mean(scaled, axis=-1, keepdims=True) - hat * both)


def feed_step(step, gm_ref, n2, n2_t, gm_t, wu, wd, bias, a_ref, bup_ref, gh, gn2, grads, ids_ref, sizes):
    dps, fss = sizes
    pair = fss // dps
    width = a_ref.shape[1]
    many = width // pair
    tall, thin = D // dps, D // fss
    block = step ^ (ids_ref[1] // pair)
    cols = pl.ds(pl.multiple_of(block * width, width), width)
    own_u, own_d = wu[:, cols], wd[:, cols]
    shift = bias[:, cols]
    bup = jnp.zeros((1, width), F32)
    for r in range(TILES):
        rows = slice(r * ROWS, (r + 1) * ROWS)
        act, slope = gate_pair(dot_nn(n2[rows, :], own_u) + shift)
        a_ref[rows, :] = act.astype(BF16)
        part = (dot_nn(gm_ref[rows, :], own_d) * slope).astype(BF16)
        gh[rows, :] = part
        bup = bup + jnp.sum(part.astype(F32), axis=0, keepdims=True)
        gn2[rows, :] += dot_nt(part, own_u)
    bup_ref[:, cols] = bup
    grad = dot_nn(gm_t[...], a_ref[...]).astype(BF16)
    d = block ^ ids_ref[0]
    for f in range(fss):
        for side in range(pair):
            at = tall + side * thin
            grads[d & 1, d >> 1, f & 1, f >> 1, at:at + thin, :] = grad[f * thin:(f + 1) * thin, side * many:(side + 1) * many]
    grad = dot_nn(n2_t[...], gh[...]).astype(BF16)
    for side in range(pair):
        y = (ids_ref[1] & 1) ^ side
        for d in range(dps):
            grads[d & 1, d >> 1, y, step, :tall, :] = grad[d * tall:(d + 1) * tall, side * many:(side + 1) * many]


def up_copies(step, grads, mine_ref, theirs_ref, tall, sem):
    return [
        pltpu.make_async_copy(grads.at[c, :, :, step, pl.ds(0, tall), :], ref.at[:, :, step, pl.ds(0, tall), :], sem)
        for c, ref in ((0, mine_ref), (1, theirs_ref))
    ]


def down_copy(c, x, grads, ref, tall, sem):
    return pltpu.make_async_copy(
        grads.at[c, x, :, :, pl.ds(tall, tall), :], ref.at[x, :, :, pl.ds(tall, tall), :], sem
    )


def send_grads(step, ids_ref, grads, mine_ref, theirs_ref, up_sem, down_sem, sizes):
    tall = D // sizes[0]
    start(up_copies(step, grads, mine_ref, theirs_ref, tall, up_sem))
    away = step ^ (ids_ref[1] // (sizes[1] // sizes[0])) ^ ids_ref[0]
    for c, ref in ((0, mine_ref), (1, theirs_ref)):
        @pl.when((away & 1) == c)
        def _(c=c, ref=ref):
            down_copy(c, away >> 1, grads, ref, tall, down_sem).start()


def wait_grads(grads, mine_ref, theirs_ref, up_sem, down_sem, sizes):
    tall = D // sizes[0]
    for step in range(sizes[0]):
        wait(up_copies(step, grads, mine_ref, theirs_ref, tall, up_sem))
        down_copy(0, 0, grads, mine_ref, tall, down_sem).wait()


def feed_first_kernel(plan, count, sizes, ids_ref, vec_ref, bias_ref, o_hbm, x_hbm, gm_hbm, *refs):
    parts = refs[:count]
    (a_ref, bup_ref, mid_hbm, n2_hbm, gn2_hbm, wd_hbm, wo_hbm, mine_ref, theirs_ref,
     o, x, gm, mid, n2, gn2, wd, wo, wu, stage, plain, n2_t, gm_t, gh, grads, sems) = refs[count:]
    step = pl.program_id(0)
    outs = [
        pltpu.make_async_copy(src, dst, sems.at[4 + k])
        for k, (src, dst) in enumerate(((wd, wd_hbm), (wo, wo_hbm), (mid, mid_hbm), (n2, n2_hbm), (gn2, gn2_hbm)))
    ]

    @pl.when(step == 0)
    def _():
        ins = [pltpu.make_async_copy(src, dst, sems.at[1 + k]) for k, (src, dst) in enumerate(((gm_hbm, gm), (o_hbm, o), (x_hbm, x)))]
        lay = chunk_copies(plan, ids_ref, parts, wu, wd, stage, sems.at[0], sizes)
        start(ins[:1] + lay + ins[1:])
        ins[0].wait()
        turn(gm, plain, gm_t, ids_ref[1], sizes[1])
        gn2[...] = jnp.zeros_like(gn2)
        wait(lay)
        unfold_out(stage, wo, sizes)
        start(outs[:2])
        wait(ins[1:])
        for r in range(TILES):
            rows = slice(r * ROWS, (r + 1) * ROWS)
            middle = x[rows, :].astype(F32) + (dot_nn(o[rows, :], wo[...]) + vec_ref[6:7, :])
            mid[rows, :] = middle
            hat, _ = norm_parts(middle)
            n2[rows, :] = (hat * (1.0 + vec_ref[2:3, :]) + vec_ref[3:4, :]).astype(BF16)
        start(outs[2:4])
        turn(n2, plain, n2_t, ids_ref[0], sizes[0])

    feed_step(step, gm, n2, n2_t, gm_t, wu, wd, bias_ref, a_ref, bup_ref, gh, gn2, grads, ids_ref, sizes)
    send_grads(step, ids_ref, grads, mine_ref, theirs_ref, sems.at[9], sems.at[10], sizes)

    @pl.when(step == pl.num_programs(0) - 1)
    def _():
        outs[4].start()
        wait_grads(grads, mine_ref, theirs_ref, sems.at[9], sems.at[10], sizes)
        wait(outs)


def feed_first(found, ids, o, x, gm, vec, bias, sizes):
    parts = [part for _, _, part in found]
    dps, fss = sizes
    units = bias.shape[1]
    width, many = units // dps, units // fss
    rows = 2 * (D // dps)
    shape = (dps // 2, 2, fss // 2, rows, many)
    outs = [
        ((L, units), BF16), ((1, units), F32), ((L, D), F32), ((L, D), BF16), ((L, D), F32), ((D, units), BF16), ((D, D), BF16),
        (shape, BF16), (shape, BF16),
    ]
    return pl.pallas_call(
        functools.partial(feed_first_kernel, slots(found), len(parts), sizes),
        grid_spec=pltpu.PrefetchScalarGridSpec(
            num_scalar_prefetch=1,
            grid=(dps,),
            in_specs=[kept((8, D)), kept((1, units))] + [any_space()] * (3 + len(parts)),
            out_specs=[pl.BlockSpec((L, width), lambda i, ids: (0, i ^ (ids[1] // (fss // dps)))), kept((1, units))]
            + [any_space()] * 7,
            scratch_shapes=[
                pltpu.VMEM((L, D), BF16),
                pltpu.VMEM((L, D), BF16),
                pltpu.VMEM((L, D), BF16),
                pltpu.VMEM((L, D), F32),
                pltpu.VMEM((L, D), BF16),
                pltpu.VMEM((L, D), F32),
                pltpu.VMEM((D, units), BF16),
                pltpu.VMEM((D, D), BF16),
                pltpu.VMEM((D, units), BF16),
                pltpu.VMEM((dps, fss, parts[0].shape[1] - rows, 128), BF16),
                pltpu.VMEM((D, L), BF16),
                pltpu.VMEM((D, L), BF16),
                pltpu.VMEM((D, L), BF16),
                pltpu.VMEM((L, width), BF16),
                pltpu.VMEM((2,) + shape, BF16),
                pltpu.SemaphoreType.DMA((11,)),
            ],
        ),
        out_shape=[jax.ShapeDtypeStruct(s, kind) for s, kind in outs],
        compiler_params=params(),
        cost_estimate=pl.CostEstimate(flops=2 * L * D * (5 * units + D), bytes_accessed=30_000_000, transcendentals=2 * L * units),
        name="feed_first",
    )(ids, vec, bias, o, x, gm, *parts)


def feed_second_kernel(plan, count, sizes, ids_ref, vec_ref, bias_ref, o_hbm, n2_hbm, gm_hbm, mid_hbm, gn2_hbm, wo_hbm, *refs):
    parts = refs[:count]
    (a_ref, bup_ref, sums_ref, wd_hbm, gmid_hbm, go_hbm, mine_ref, theirs_ref,
     o, n2, gm, mid, gn2, wo, wd, wu, plain, n2_t, gm_t, gh, gatt, full, grads, sems) = refs[count:]
    step = pl.program_id(0)
    dps, fss = sizes
    tall, thin = D // dps, D // fss
    ins = [
        pltpu.make_async_copy(src, dst, sems.at[k])
        for k, (src, dst) in enumerate(((gm_hbm, gm), (n2_hbm, n2), (gn2_hbm, gn2), (o_hbm, o), (mid_hbm, mid), (wo_hbm, wo)))
    ]
    wd_out = pltpu.make_async_copy(wd, wd_hbm, sems.at[7])

    @pl.when(step == 0)
    def _():
        lay = chunk_copies(plan, ids_ref, parts, wu, wd, None, sems.at[6], sizes)
        start(ins[:2] + lay + ins[2:3])
        ins[0].wait()
        turn(gm, plain, gm_t, ids_ref[1], fss)
        ins[1].wait()
        turn(n2, plain, n2_t, ids_ref[0], dps)
        wait(lay)
        start(ins[3:])
        wd_out.start()
        ins[2].wait()

    feed_step(step, gm, n2, n2_t, gm_t, wu, wd, bias_ref, a_ref, bup_ref, gh, gn2, grads, ids_ref, sizes)
    send_grads(step, ids_ref, grads, mine_ref, theirs_ref, sems.at[8], sems.at[9], sizes)

    @pl.when(step == pl.num_programs(0) - 1)
    def _():
        wait(ins[3:])
        turn(o, plain, n2_t, ids_ref[0], dps)
        sums = [jnp.zeros((1, D), F32)] * 4
        outs = []
        for r in range(TILES):
            rows = slice(r * ROWS, (r + 1) * ROWS)
            grad, gy = gn2[rows, :], gm[rows, :].astype(F32)
            hat, inv = norm_parts(mid[rows, :])
            gmid = gy + norm_back(grad, hat, inv, vec_ref[2:3, :])
            mid[rows, :] = gmid
            low = gmid.astype(BF16)
            gatt[rows, :] = low
            n2[rows, :] = dot_nt(low, wo[...]).astype(BF16)
            for k, term in enumerate((grad * hat, grad, low.astype(F32), gy)):
                sums[k] = sums[k] + jnp.sum(term, axis=0, keepdims=True)
        outs = [pltpu.make_async_copy(mid, gmid_hbm, sems.at[10]), pltpu.make_async_copy(n2, go_hbm, sems.at[11])]
        start(outs)
        sums_ref[...] = jnp.concatenate(sums + [jnp.zeros((4, D), F32)], axis=0)
        full[...] = dot_nn(n2_t[...], gatt[...]).astype(BF16)
        for f in range(fss):
            flip = ids_ref[1] ^ f
            for d in range(dps):
                for k in range(2):
                    at = 2 * tall
                    grads[d & 1, d >> 1, flip & 1, flip >> 1, at:at + tall // 2, k * thin:(k + 1) * thin] = (
                        full[d * tall + k * (tall // 2):d * tall + (k + 1) * (tall // 2), f * thin:(f + 1) * thin]
                    )
                grads[d & 1, d >> 1, flip & 1, flip >> 1, 2 * tall:, 2 * thin:] = jnp.zeros(
                    (tall // 2, grads.shape[5] - 2 * thin), BF16
                )
        rows = pl.ds(2 * tall, tall // 2)
        rest = [
            pltpu.make_async_copy(grads.at[c, :, :, :, rows, :], ref.at[:, :, :, rows, :], sems.at[12])
            for c, ref in ((0, mine_ref), (1, theirs_ref))
        ]
        start(rest)
        wait_grads(grads, mine_ref, theirs_ref, sems.at[8], sems.at[9], sizes)
        wait(rest + outs + [wd_out])


def feed_second(found, ids, o, n2, gm, mid, gn2, vec, bias, wo, sizes):
    parts = [part for _, _, part in found]
    dps, fss = sizes
    units = bias.shape[1]
    width, many = units // dps, units // fss
    tall = D // dps
    shape = (dps // 2, 2, fss // 2, 2 * tall + tall // 2, many)
    outs = [
        ((L, units), BF16), ((1, units), F32), ((8, D), F32), ((D, units), BF16), ((L, D), F32), ((L, D), BF16),
        (shape, BF16), (shape, BF16),
    ]
    return pl.pallas_call(
        functools.partial(feed_second_kernel, slots(found), len(parts), sizes),
        grid_spec=pltpu.PrefetchScalarGridSpec(
            num_scalar_prefetch=1,
            grid=(dps,),
            in_specs=[kept((8, D)), kept((1, units))] + [any_space()] * (6 + len(parts)),
            out_specs=[
                pl.BlockSpec((L, width), lambda i, ids: (0, i ^ (ids[1] // (fss // dps)))), kept((1, units)), kept((8, D)),
            ] + [any_space()] * 5,
            scratch_shapes=[
                pltpu.VMEM((L, D), BF16),
                pltpu.VMEM((L, D), BF16),
                pltpu.VMEM((L, D), BF16),
                pltpu.VMEM((L, D), F32),
                pltpu.VMEM((L, D), F32),
                pltpu.VMEM((D, D), BF16),
                pltpu.VMEM((D, units), BF16),
                pltpu.VMEM((D, units), BF16),
                pltpu.VMEM((D, L), BF16),
                pltpu.VMEM((D, L), BF16),
                pltpu.VMEM((D, L), BF16),
                pltpu.VMEM((L, width), BF16),
                pltpu.VMEM((L, D), BF16),
                pltpu.VMEM((D, D), BF16),
                pltpu.VMEM((2,) + shape, BF16),
                pltpu.SemaphoreType.DMA((13,)),
            ],
        ),
        out_shape=[jax.ShapeDtypeStruct(s, kind) for s, kind in outs],
        compiler_params=params(),
        cost_estimate=pl.CostEstimate(flops=2 * L * D * (5 * units + 2 * D), bytes_accessed=35_000_000, transcendentals=2 * L * units),
        name="feed_second",
    )(ids, vec, bias, o, n2, gm, mid, gn2, wo, *parts)


def last_kernel(a0_ref, a1_ref, mid_ref, vec_ref, w0_ref, w1_ref, y_ref):
    total = dot_nt(a0_ref[...], w0_ref[...]) + dot_nt(a1_ref[...], w1_ref[...])
    y_ref[...] = (mid_ref[...] + (total + vec_ref[7:8, :])).astype(BF16)


def last_call(a0, a1, middle, vec, w0, w1):
    return pl.pallas_call(
        last_kernel,
        grid=(TILES,),
        in_specs=[rows_of(a0.shape[1]), rows_of(a1.shape[1]), rows_of(D), kept((8, D)), kept(w0.shape), kept(w1.shape)],
        out_specs=rows_of(D),
        out_shape=jax.ShapeDtypeStruct((L, D), BF16),
        compiler_params=params(),
        cost_estimate=pl.CostEstimate(flops=2 * L * D * FF, bytes_accessed=17_000_000, transcendentals=0),
        name="feed_down",
    )(a0, a1, middle, vec, w0, w1)


def close_kernel(sizes, ids_ref, len_ref, lead_ref, vec_ref, sums_ref, qsums0_ref, qsums1_ref, bup0_ref, bup1_ref,
                 x_hbm, gmid_hbm, n1_hbm, g0_hbm, g1_hbm, w_hbm, gx_hbm, mine_ref, theirs_ref,
                 x, gmid, n1, g, w, plain, left, full, table, grads, sems):
    dps, fss = sizes
    tall, cols, thin, wide = D // dps, 3 * D // fss, D // fss, FF // fss
    ins = [
        pltpu.make_async_copy(src, dst, sems.at[k])
        for k, (src, dst) in enumerate(((n1_hbm, n1), (w_hbm, w), (x_hbm, x), (gmid_hbm, gmid)))
    ]
    joins = []
    for third in range(3):
        at = third * D
        for src in (g0_hbm, g1_hbm):
            part = src.shape[1] // 3
            joins.append(
                pltpu.make_async_copy(src.at[:, third * part:(third + 1) * part], g.at[:, at:at + part], sems.at[4])
            )
            at += part
    start(ins[:1] + joins)
    ins[0].wait()
    turn(n1, plain, left, ids_ref[0], dps)
    wait(joins)
    start(ins[1:])
    rest = cols - 256
    fold = 128 // rest
    some = tall // fold
    for third in range(3):
        at = slice(third * D, (third + 1) * D)
        full[:, at] = dot_nn(left[...], g[:, at]).astype(BF16)
    for f in range(fss):
        flip = ids_ref[1] ^ f
        y, z = flip & 1, flip >> 1
        for d in range(dps):
            own = slice(d * tall, (d + 1) * tall)
            c, away = d & 1, d >> 1
            grads[c, away, y, z, 0:tall, :] = full[own, f * cols:f * cols + 128]
            grads[c, away, y, z, tall:2 * tall, :] = full[own, f * cols + 128:f * cols + 256]
            for k in range(fold):
                grads[c, away, y, z, 2 * tall:2 * tall + some, k * rest:(k + 1) * rest] = (
                    full[d * tall + k * some:d * tall + (k + 1) * some, f * cols + 256:(f + 1) * cols]
                )
    big, little = pl.ds(0, 2 * tall + some), pl.ds(2 * tall + some, 16)
    sends = [
        [
            pltpu.make_async_copy(grads.at[c, :, :, :, rows, :], ref.at[:, :, :, rows, :], sems.at[at])
            for c, ref in ((0, mine_ref), (1, theirs_ref))
        ]
        for at, rows in ((5, big), (6, little))
    ]
    start(sends[0])
    wait(ins[1:])
    gain, shift = jnp.zeros((1, D), F32), jnp.zeros((1, D), F32)
    table[...] = jnp.zeros_like(table)
    bounds = bounds_of(len_ref)
    outs = []
    for r in range(TILES):
        rows = slice(r * ROWS, (r + 1) * ROWS)
        grad = dot_nt(g[rows, :], w[...])
        hat, inv = norm_parts(x[rows, :].astype(F32))
        gain = gain + jnp.sum(grad * hat, axis=0, keepdims=True)
        shift = shift + jnp.sum(grad, axis=0, keepdims=True)
        shape = (table.shape[0], ROWS)
        places = r * ROWS + lax.broadcasted_iota(jnp.int32, shape, 1)
        hot = lead_of(places, bounds, lead_ref) == lax.broadcasted_iota(jnp.int32, shape, 0)
        hot = hot.astype(BF16)
        high = grad.astype(BF16)
        low = (grad - high.astype(F32)).astype(BF16)
        table[...] += dot_nn(hot, high) + dot_nn(hot, low)
        gmid[rows, :] += norm_back(grad, hat, inv, vec_ref[0:1, :])
    out = pltpu.make_async_copy(gmid, gx_hbm, sems.at[7])
    out.start()
    bup = []
    for f in range(fss):
        for chunk, ref in ((1, bup1_ref), (0, bup0_ref)):
            many = chunk_cols(chunk, wide)[1]
            bup.append(ref[:, f * many:(f + 1) * many])
    bup = jnp.concatenate(bup, axis=1)
    qsums = jnp.concatenate([qsums0_ref[0:2, :], qsums1_ref[0:2, :]], axis=1)
    gvec = [gain, shift, sums_ref[0:1, :], sums_ref[1:2, :], qsums[0:1, :], qsums[1:2, :], sums_ref[2:3, :], sums_ref[3:4, :]]
    for d in range(dps):
        small = jnp.concatenate(
            gvec[2 * d:2 * d + 2] + [table[5 * d:5 * d + 5, :], bup[:, d * D:(d + 1) * D], jnp.zeros((8, D), F32)], axis=0
        )
        away = ids_ref[0] ^ d
        for f in range(fss):
            flip = ids_ref[1] ^ f
            part = jnp.concatenate([small[:, f * thin:(f + 1) * thin], jnp.zeros((16, 128 - thin), F32)], axis=1)
            grads[away & 1, away >> 1, flip & 1, flip >> 1, 2 * tall + some:, :] = part.astype(BF16)
    start(sends[1])
    wait(sends[0] + sends[1] + [out])


def close_call(ids, lengths, leads, x, gmid, n1, back0, back1, vec, w, sums, bup0, bup1, sizes):
    dps, fss = sizes
    tall = D // dps
    rows = 2 * tall + tall // (128 // (3 * D // fss - 256)) + 16
    shape = (dps // 2, 2, fss // 2, rows, 128)
    return pl.pallas_call(
        functools.partial(close_kernel, sizes),
        in_specs=[smem()] * 3 + [in_vmem()] * 6 + [any_space()] * 6,
        out_specs=[any_space()] * 3,
        out_shape=[jax.ShapeDtypeStruct((L, D), F32), jax.ShapeDtypeStruct(shape, BF16), jax.ShapeDtypeStruct(shape, BF16)],
        scratch_shapes=[
            pltpu.VMEM((L, D), BF16),
            pltpu.VMEM((L, D), F32),
            pltpu.VMEM((L, D), BF16),
            pltpu.VMEM((L, 3 * D), BF16),
            pltpu.VMEM((D, 3 * D), BF16),
            pltpu.VMEM((D, L), BF16),
            pltpu.VMEM((D, L), BF16),
            pltpu.VMEM((D, 3 * D), BF16),
            pltpu.VMEM((32, D), F32),
            pltpu.VMEM((2,) + shape, BF16),
            pltpu.SemaphoreType.DMA((8,)),
        ],
        compiler_params=params(),
        cost_estimate=pl.CostEstimate(flops=4 * L * D * 3 * D, bytes_accessed=25_000_000, transcendentals=0),
        name="close",
    )(ids, lengths, leads, vec, sums, back0[1], back1[1], bup0, bup1, x, gmid, n1, back0[0], back1[0], w)


def finish_kernel(count, tall, cols, thin, *refs):
    parts, (qkv_ref, vec_ref, table_ref, bias_ref) = refs[:count], refs[count:]
    total = sum(part[...].astype(F32) for part in parts)
    qkv_ref[:, 0:128] = total[:tall]
    qkv_ref[:, 128:256] = total[tall:2 * tall]
    rest = cols - 256
    some = tall * rest // 128
    for k in range(128 // rest):
        qkv_ref[k * some:(k + 1) * some, 256:cols] = total[2 * tall:2 * tall + some, k * rest:(k + 1) * rest]
    small = total[2 * tall + some:, :thin]
    vec_ref[...] = small[0:2]
    table_ref[...] = small[2:7]
    bias_ref[...] = small[7:8]


def finish_call(parts, tall, cols, thin):
    return pl.pallas_call(
        functools.partial(finish_kernel, len(parts), tall, cols, thin),
        in_specs=[in_vmem()] * len(parts),
        out_specs=[in_vmem()] * 4,
        out_shape=[jax.ShapeDtypeStruct((rows, wide), F32) for rows, wide in ((tall, cols), (2, thin), (5, thin), (1, thin))],
        compiler_params=params(16 * 1024 * 1024),
        cost_estimate=pl.CostEstimate(flops=1_000_000, bytes_accessed=1_000_000, transcendentals=0),
        name="finish",
    )(*parts)


def hop_dp(value, flip, ranks):
    return lax.ppermute(value, "dp", [(i, i ^ flip) for i in range(ranks)])


def hop_fsdp(value, flip, ranks):
    return lax.ppermute(value, "fsdp", [(i, i ^ flip) for i in range(ranks)])


def tie(values, *others):
    flat, tree = jax.tree.flatten(values)
    more = jax.tree.leaves(others)
    done = lax.optimization_barrier(tuple(flat) + tuple(more))
    return jax.tree.unflatten(tree, done[:len(flat)])


def gather_depth(piece, sizes):
    return [piece] + [hop_fsdp(piece, 2 * z, sizes[1]) for z in range(1, sizes[1] // 2)]


def gather_far(piece, sizes):
    return jnp.stack([piece, hop_fsdp(piece, sizes[1] // 2, sizes[1])])


def gather_near(pair, sizes):
    other = hop_fsdp(pair, sizes[1] // 4, sizes[1])
    return jnp.stack([pair[0], other[0], pair[1], other[1]])


def gather_sides(column, sizes):
    return hop_dp(column, 2, sizes[0]), hop_fsdp(column, 1, sizes[1])


def gather_corner(sides, sizes):
    by_x, by_y = sides
    half = by_x.shape[0] // 2
    return hop_fsdp(by_x[:half], 1, sizes[1]), hop_dp(by_y[half:], 2, sizes[0])


def cross(parts, sizes):
    return [hop_dp(part, 1, sizes[0]) for part in parts]


def name_parts(parts, others):
    half = parts[0].shape[0] // 2
    flips = ((0, 0), (2, 0), (0, 1), (2, 1), (2, 1 + 2 * half))
    own = [(dp, fs, part) for (dp, fs), part in zip(flips, parts)]
    return own + [(dp | 1, fs, part) for (dp, fs), part in zip(flips, others)]


def plus(*terms):
    return sum(term.astype(F32) for term in terms)


def reduce_core(mine, theirs, sizes):
    flat = theirs.reshape(-1, theirs.shape[-1])
    return mine.reshape(flat.shape), hop_dp(flat, 1, sizes[0])


def reduce_sides(cored, sizes):
    both = plus(*cored).astype(BF16)
    both = both.reshape(sizes[0] // 2, 2, sizes[1] // 2, -1, both.shape[-1])
    half = both.shape[2] // 2
    first, second = both[:, :, :half], both[:, :, half:]
    got = hop_dp(first[1], 2, sizes[0]), hop_fsdp(second[:, 1], 1, sizes[1])
    return first[0], second[:, 0], got


def reduce_corner(sided, sizes):
    first, second, got = sided
    first, second = plus(first, got[0]).astype(BF16), plus(second, got[1]).astype(BF16)
    got = hop_fsdp(first[1], 1, sizes[1]), hop_dp(second[1], 2, sizes[0])
    return first[0], second[0], got


def reduce_near(cornered, sizes):
    first, second, got = cornered
    first, second = plus(first, got[0]).astype(BF16), plus(second, got[1]).astype(BF16)
    gone = hop_fsdp(jnp.stack([first[1], second[1]]), sizes[1] // 4, sizes[1])
    return first[0], second[0], gone


def reduce_far(neared, sizes):
    first, second, got = neared
    return first, got[0], hop_fsdp(plus(second, got[1]).astype(BF16), sizes[1] // 2, sizes[1])


def reduce_depth(cornered, sizes):
    first, second, got = cornered
    first, second = plus(first, got[0]).astype(BF16), plus(second, got[1]).astype(BF16)
    apart = [first[k] for k in range(first.shape[0])] + [second[k] for k in range(second.shape[0])]
    return [apart[0]] + [hop_fsdp(apart[z], 2 * z, sizes[1]) for z in range(1, len(apart))]


def per_device(sizes, tokens, lengths, lead_index, cotangent, w_qkv, w_out, w_up, w_down, vectors, lead_table, up_bias):
    dps, fss = sizes
    ids = jnp.stack([lax.axis_index("dp"), lax.axis_index("fsdp")]).astype(jnp.int32)
    thin, wide, tall = D // fss, FF // fss, D // dps
    x, gy = tokens.reshape(L, D), cotangent.reshape(L, D)

    piece0 = pack_first(w_qkv, jnp.concatenate([vectors, lead_table, up_bias], axis=0))
    w_down_t = w_down.T
    piece1 = jnp.concatenate([pack_chunk(0, w_up, w_down_t), fold_out(w_out)], axis=0)
    piece2 = pack_chunk(1, w_up, w_down_t)

    depth0 = gather_depth(piece0, sizes)
    depth0, piece1 = tie((depth0, piece1))
    column0 = jnp.stack(depth0)
    sides0, far1, other0 = gather_sides(column0, sizes), gather_far(piece1, sizes), cross((column0,), sizes)
    column0, sides0, other0, far1, piece2 = tie((column0, sides0, other0, far1, piece2))
    corner0, across0, column1 = gather_corner(sides0, sizes), cross(sides0, sizes), gather_near(far1, sizes)
    column0, sides0, corner0, other0, across0, column1, piece2 = tie(
        (column0, sides0, corner0, other0, across0, column1, piece2)
    )
    last0 = cross(corner0, sizes)
    last0, column1, piece2 = tie((last0, column1, piece2))

    sides1, depth2 = gather_sides(column1, sizes), gather_depth(piece2, sizes)
    found = name_parts((column0,) + sides0 + corner0, other0 + across0 + last0)
    opened = open_call(found, ids, lengths, lead_index, x, sizes)
    column1, sides1, depth2, opened = tie((column1, sides1, depth2, opened))
    n1, qkv, w_qkv, vec, table, bias0, bias1 = opened

    column2 = jnp.stack(depth2)
    corner1, other1, sides2 = gather_corner(sides1, sizes), cross((column1,), sizes), gather_sides(column2, sizes)
    attended = attend_call(lengths, qkv)
    column1, sides1, corner1, other1, column2, sides2, attended = tie(
        (column1, sides1, corner1, other1, column2, sides2, attended)
    )
    o, lse = attended

    last1 = cross(sides1 + corner1, sizes)
    last1, column2, sides2 = tie((last1, column2, sides2))

    corner2, other2 = gather_corner(sides2, sizes), cross((column2,) + sides2, sizes)
    found = name_parts((column1,) + sides1 + corner1, other1 + last1)
    first = feed_first(found, ids, o, x, gy, vec, bias0, sizes)
    column2, sides2, corner2, other2, first = tie((column2, sides2, corner2, other2, first))
    a0, bup0, middle, n2, gn2, wd0, w_out, mine0, theirs0 = first

    last2 = cross(corner2, sizes)
    last2, theirs0 = tie((last2, theirs0))

    grads0 = reduce_core(mine0, theirs0, sizes)
    found = name_parts((column2,) + sides2 + corner2, other2 + last2)
    second = feed_second(found, ids, o, n2, gy, middle, gn2, vec, bias1, w_out, sizes)
    grads0, second = tie((grads0, second))
    a1, bup1, sums, wd1, gmid, go, mine1, theirs1 = second

    grads0, grads1 = reduce_sides(grads0, sizes), reduce_core(mine1, theirs1, sizes)
    back0 = attend_back_call(lengths, qkv, o, go, lse, 0, 1)
    grads0, grads1, back0, go = tie((grads0, grads1, back0, go))

    grads0, grads1 = reduce_corner(grads0, sizes), reduce_sides(grads1, sizes)
    back1 = attend_back_call(lengths, qkv, o, go, lse, 1, PAIRS - 1)
    grads0, grads1, back0, back1 = tie((grads0, grads1, back0, back1))

    grads0, grads1 = reduce_near(grads0, sizes), reduce_corner(grads1, sizes)
    closed = close_call(
        ids, lengths, lead_index, x, gmid, n1, back0, back1, vec, w_qkv, sums, bup0, bup1, sizes
    )
    grads0, grads1, closed, a0 = tie((grads0, grads1, closed, a0))
    gx, mine2, theirs2 = closed

    grads2 = reduce_core(mine2, theirs2, sizes)
    grads2, a0 = tie((grads2, a0))
    grads0, grads1, grads2 = reduce_far(grads0, sizes), reduce_near(grads1, sizes), reduce_sides(grads2, sizes)
    y = last_call(a0, a1, middle, vec, wd0, wd1)
    grads0, grads1, grads2, y = tie((grads0, grads1, grads2, y))
    grads1, grads2 = reduce_far(grads1, sizes), reduce_corner(grads2, sizes)
    grads2 = reduce_depth(grads2, sizes)
    got0, got1 = plus(*grads0), plus(*grads1)

    many = wide // 3
    up = jnp.concatenate([got1[:tall], got0[:tall]], axis=1)
    down = []
    for side in range(fss // dps):
        rows = slice(tall + side * thin, tall + (side + 1) * thin)
        down += [got1[rows], got0[rows]]
    down = jnp.concatenate(down, axis=1).T
    out = jnp.concatenate([got1[2 * tall:, :thin], got1[2 * tall:, thin:2 * thin]], axis=0)
    up, down, out, grads2 = tie((up, down, out, grads2))
    qkv_grad, gvec, gtable, gbias = finish_call(grads2, tall, 3 * thin, thin)
    return y.reshape(1, L, D), gx.reshape(1, L, D), qkv_grad, out, up, down, gvec, gtable, gbias


def per_device_plain(sizes, tokens, lengths, lead_index, cotangent, w_qkv, w_out, w_up, w_down, vectors, table, bias):
    def full(shard):
        return lax.all_gather(lax.all_gather(shard, "fsdp", axis=1, tiled=True), "dp", axis=0, tiled=True)

    def share(grad):
        part = lax.psum_scatter(grad.astype(F32), "fsdp", scatter_dimension=1, tiled=True)
        return lax.psum_scatter(part, "dp", scatter_dimension=0, tiled=True)

    x, gy = tokens.reshape(L, D), cotangent.reshape(L, D)
    w_qkv, w_out, w_up, w_down_t = full(w_qkv), full(w_out), full(w_up), full(w_down).T
    vec, bias = full(vectors).astype(F32), full(bias).astype(F32).reshape(1, FF)
    table = jnp.pad(full(table), ((0, 32 - LEADS), (0, 0)))
    n1, qkv = qkv_call(lengths, lead_index, x, vec, table, w_qkv)
    o, lse = attend_call(lengths, qkv)
    middle, n2, a, slope = up_call(o, x, vec, w_out, w_up, bias)
    gh, gmid, gatt, go, sums, bup = feed_back_call(gy, slope, middle, vec, w_down_t, w_up, w_out)
    gqkv, qsums = attend_back_call(lengths, qkv, o, go, lse)
    gx, first_sums, gtable = first_back_call(lengths, lead_index, x, gmid, gqkv, vec, w_qkv)
    gvec = jnp.concatenate([first_sums[:2], sums[:2], qsums[:2], sums[2:4]], axis=0)
    y = down_call(a, middle, vec, w_down_t)
    return (
        y.reshape(1, L, D),
        gx.reshape(1, L, D),
        share(outer_call(n1, gqkv, "grad_qkv")),
        share(outer_call(o, gatt, "grad_out")),
        share(outer_call(n2, gh, "grad_up")),
        share(outer_call(gy, a, "grad_down").T),
        share(gvec),
        share(gtable[:LEADS]),
        share(bup[0].reshape(FF // D, D)),
    )


def solution(mesh):
    sizes = (mesh.shape["dp"], mesh.shape["fsdp"])
    whole_tiles = FF // sizes[1] == 384 and sizes[1] == 2 * sizes[0]
    plan = per_device if whole_tiles else per_device_plain
    rows, both = P(("dp", "fsdp"), None, None), P("dp", "fsdp")
    index = P(("dp", "fsdp"), None)
    return jax.shard_map(
        functools.partial(plan, sizes),
        mesh=mesh,
        in_specs=(rows, index, index, rows) + (both,) * 7,
        out_specs=(rows, rows) + (both,) * 7,
        check_vma=False,
    )
```
